32 devices in a mesh: lat: 8 (over z, core), lon: 4 (over y, x).
Axes of the slice: x: 2, y: 2, z: 4, core: 2. Of those that a mesh axis runs over, the one named last changes fastest.
Arguments:
- winds: float32 [2, 16, 720, 2880], P(None, None, 'lat', 'lon'), may hold values from -6 to 6
- theta: float32 [16, 720, 2880], P(None, 'lat', 'lon'), may hold values from -6 to 6
- thick: float32 [16, 720, 2880], P(None, 'lat', 'lon'), may hold values from 0.5 to 1.5
- polar_rows: int32 [240], replicated, may hold values from 0 to 719, as said below
- cutoffs: int32 [240], replicated, may hold values from 1 to 719, as said below
Outputs:
- new_winds: float32 [2, 16, 720, 2880], P(None, None, 'lat', 'lon')
- new_theta: float32 [16, 720, 2880], P(None, 'lat', 'lon')
- new_thick: float32 [16, 720, 2880], P(None, 'lat', 'lon')
The draws below stay inside these ranges and needn't reach their ends.
Inputs may be any that keep to these rules, and one draw needn't show every extreme that they name: `polar_rows`: each row is listed once, in an order drawn from the seed. The listed rows are a run of rows from row 0 up together with a run of rows ending at row 719; each run has between 90 and 150 rows, so no row of the middle half of the latitudes is listed. `cutoffs`: rows 0 and 719 have cutoff 1, and the listed row of each run that lies farthest from its pole has cutoff 720 - 1. Any other listed row that lies d rows from its nearest pole (d = 0 at the pole) has a cutoff between min(d + 1, 719) and min(2 (d + 1), 719).
All inputs are finite; a program needn't handle non-finite values.
Results may differ from the reference program's by a relative error of at most 0.000071.
Values sent between devices are 32-bit elements; how exact they have to be, the bound alone decides.
No kernel may reach another device: no remote copies, remote signals or barrier semaphores. Data moves between devices by JAX's collectives and lax.ppermute only.
A program may use at most 192 MiB of HBM per device.

```python
import jax
import jax.numpy as jnp
from jax import lax

NLON = 2880
LEV = 16
NLAT = 720
KW = 720
NPOLE = 120
NF = 240


def polar_layout(key):
    north = jax.random.randint(key, (), NPOLE - NPOLE // 4, NPOLE + NPOLE // 4 + 1).astype(jnp.int32)
    place = jnp.arange(NF, dtype=jnp.int32)
    rows = jnp.where(place < north, place, NLAT - NF + place).astype(jnp.int32)
    order = jax.random.permutation(jax.random.fold_in(key, 5), NF)
    return (rows[order].astype(jnp.int32), north)


def draw_polar_rows(key, part):
    rows, north = polar_layout(key)
    return rows


def draw_cutoffs(key, part):
    rows, north = polar_layout(key)
    key = jax.random.fold_in(key, 23)
    depth = jnp.minimum(rows, NLAT - 1 - rows)
    lower = jnp.minimum(depth + 1, KW - 1)
    upper = jnp.minimum(2 * (depth + 1), KW - 1)
    drawn = jax.random.randint(key, (NF,), lower, upper + 1).astype(jnp.int32)
    deepest = (rows == north - 1) | (rows == NLAT - NF + north)
    drawn = jnp.where(deepest, KW - 1, drawn)
    drawn = jnp.where(depth == 0, 1, drawn)
    return drawn.astype(jnp.int32)


def steps_of(stream_key, shape, split, low, top_value):
    level, own = 1.0, jax.random.fold_in(stream_key, 6)
    for axis_at, blocks in split:
        steps = jnp.exp(jax.random.uniform(jax.random.fold_in(own, axis_at), (blocks,), jnp.float32, low / len(split), top_value / len(split)))
        level = level * jnp.repeat(steps, shape[axis_at] // blocks).reshape([-1 if axis == axis_at else 1 for axis in range(len(shape))])
    return level


def gaussian(rng, shape, width, reach, split=(), held_as=jnp.bfloat16):
    entries = jax.random.normal(rng, shape, jnp.float32) * width
    if len(split) > 0:
        entries = steps_of(rng, shape, split, -0.22, 0.18) * entries
    return jnp.clip(entries, min=-reach, max=reach).astype(held_as)


def setup_inputs(seed: int = 0) -> dict:
    key_of = jax.random.split(jax.random.key(seed), 6)
    return {
        "winds": gaussian(key_of[0], (2, LEV, NLAT, NLON), 1.0, 6.0, ((2, 8), (3, 4)), jnp.float32),
        "theta": gaussian(key_of[1], (LEV, NLAT, NLON), 1.0, 6.0, ((1, 8), (2, 4)), jnp.float32),
        "thick": jnp.clip(0.5 + 1.0 * jax.random.uniform(key_of[2], (LEV, NLAT, NLON), jnp.float32) ** steps_of(key_of[2], (LEV, NLAT, NLON), ((1, 8), (2, 4)), -0.2, 0.2), 0.5, 1.5),
        "polar_rows": draw_polar_rows(jax.random.fold_in(key_of[5], 71), 0),
        "cutoffs": draw_cutoffs(jax.random.fold_in(key_of[5], 71), 0),
    }


def truncate_row(field, keep, listed):
    spec = jnp.fft.rfft(field, axis=1)
    spec = jnp.where(keep, spec, jnp.zeros_like(spec))
    back = jnp.fft.irfft(spec, n=NLON, axis=1).astype(field.dtype)
    return jnp.where(listed[:, None], back, field)


def diff_lon(field):
    return (jnp.roll(field, -1, axis=1) - jnp.roll(field, 1, axis=1)) * 0.5


def diff_lat(field):
    padded = jnp.pad(field, ((1, 1), (0, 0)))
    return (padded[2:] - padded[:-2]) * 0.5


def reference(winds, theta, thick, polar_rows, cutoffs):
    cut_full = jnp.full((NLAT,), -1, jnp.int32).at[polar_rows].set(cutoffs)
    listed = cut_full >= 0
    wave = jnp.arange(NLON // 2 + 1, dtype=jnp.int32)
    keep = wave[None, :] <= cut_full[:, None]
    centre = (jnp.arange(NLAT, dtype=jnp.int32).astype(winds.dtype) + 0.5) * (jnp.pi / NLAT)
    coslat = jnp.sin(centre)[:, None]
    sinlat = (-jnp.cos(centre))[:, None]

    def level(fields):
        uu, vv, tt, hh = [truncate_row(f, keep, listed) for f in fields]
        new_h = hh - 0.05 * diff_lon(uu * hh) / coslat - 0.2 * diff_lat(vv * hh * coslat) / coslat
        new_t = tt - 0.05 * uu * diff_lon(tt) / coslat - 0.2 * vv * diff_lat(tt)
        new_u = uu - 0.05 * uu * diff_lon(uu) / coslat - 0.2 * vv * diff_lat(uu) - 0.1 * diff_lon(hh) / coslat + 0.3 * sinlat * vv
        new_v = vv - 0.05 * uu * diff_lon(vv) / coslat - 0.2 * vv * diff_lat(vv) - 0.3 * diff_lat(hh) - 0.3 * sinlat * uu
        return new_u, new_v, new_t, new_h

    outs = lax.map(level, (winds[0], winds[1], theta, thick))
    return jnp.stack([outs[0], outs[1]]), outs[2], outs[3]
```

```python
import functools

import jax
import jax.numpy as jnp
import ml_dtypes
import numpy as np
from jax import lax
from jax.experimental import pallas as pl
from jax.experimental.pallas import tpu as pltpu
from jax.sharding import PartitionSpec as P

TILE = 16
SUB = 8
FIELDS = 4
VMEM = 58 * 1024 * 1024


def round_up(value, step):
    return -(-value // step) * step


class Plan:
    def __init__(self, lat, lon, levels, rows, width, listed):
        self.lat, self.lon, self.levels, self.rows, self.width = lat, lon, levels, rows, width
        self.total_rows, self.length = lat * rows, lon * width
        self.chunks = levels // SUB
        self.lanes = TILE * SUB
        self.parts = lon // FIELDS
        self.wide = round_up(width + 2, 128)
        pole = listed // 2
        self.low, self.high = pole - pole // 4, pole + pole // 4
        top = self.length // 4 - 1

        def bound(depth):
            return min(2 * (depth + 1), top)

        self.roles = []
        last = self.high - 2
        for role in range(lat // 2):
            start = role * rows
            if start - 1 > last:
                break
            active = max(0, min(rows, last + 1 - start))
            count = -(-(active + 2) // TILE)
            waves = [bound(start + TILE * j + TILE - 1) for j in range(count)]
            deepest = start + active - 1
            if start + rows <= last:
                deepest = start + rows
            waves[-1] = bound(deepest)
            sizes = [round_up(2 * wave + 1, 16) for wave in waves]
            north = [TILE * j for j in range(count - 1)] + [
                max(0, min(TILE * (count - 1) - 2, rows - TILE))
            ]
            south = [rows - TILE * (j + 1) for j in range(count - 1)] + [
                max(0, rows - TILE * count + 2)
            ]
            self.roles.append(
                dict(
                    count=count,
                    sizes=sizes,
                    offsets=[sum(sizes[:j]) for j in range(count)],
                    total=sum(sizes),
                    starts=(north, south),
                )
            )
        self.tiles = max(role["count"] for role in self.roles)
        self.table = max(max(role["sizes"]) for role in self.roles)
        self.far_roles = [
            role
            for role in range(lat // 2)
            if role * rows - 1 <= self.high - 1 and (role + 1) * rows >= self.low - 1
        ]

    def blocks(self, role):
        return (role, self.lat - 1 - role)

    def slot_rows(self):
        table = np.full((len(self.roles), 2, self.tiles, TILE), -2, np.int32)
        for at, role in enumerate(self.roles):
            for hemi in range(2):
                for j in range(role["count"]):
                    own = role["starts"][hemi][j] + np.arange(TILE)
                    if j == role["count"] - 1:
                        place = 0 if hemi == 0 else TILE - 2
                        own[place], own[place + 1] = -1, self.rows
                    table[at, hemi, j] = own
        return table

    def start_rows(self):
        table = np.zeros((len(self.roles) + 1, 2, self.tiles), np.int32)
        for at, role in enumerate(self.roles):
            for hemi in range(2):
                table[at, hemi, : role["count"]] = role["starts"][hemi]
        return table


def split_table(table):
    high = table.astype(ml_dtypes.bfloat16)
    low = (table - high.astype(np.float64)).astype(ml_dtypes.bfloat16)
    return high, low


def waves_of(count):
    index = np.arange(count)
    return (index + 1) // 2, (index % 2 == 0) & (index > 0)


def trig(plan, count, points):
    wave, odd = waves_of(count)
    angle = (wave[:, None] * points[None, :]) % plan.length * (2.0 * np.pi / plan.length)
    return np.where(odd[:, None], np.sin(angle), np.cos(angle))


def out_points(plan):
    points = np.zeros(plan.wide, np.int64)
    points[: plan.width + 1] = np.arange(plan.width + 1)
    points[-1] = -1
    used = np.zeros(plan.wide, bool)
    used[: plan.width + 1] = True
    used[-1] = True
    return points, used


@functools.lru_cache(maxsize=None)
def tables(sizes):
    plan = Plan(*sizes)
    wave, odd = waves_of(plan.table)
    points, used = out_points(plan)
    forward, inverse, far = [], [], []
    weight = np.where(wave == 0, 1.0, 2.0) / plan.length
    for place in range(plan.lon):
        forward.append(trig(plan, plan.table, place * plan.width + np.arange(plan.width)))
        inverse.append(trig(plan, plan.table, place * plan.width + points) * weight[:, None] * used[None, :])
    keep = np.arange(1, plan.length // 4)
    ring = np.arange(plan.length)
    kernel = 1.0 / plan.length + (2.0 / plan.length) * np.cos(
        (keep[:, None] * ring[None, :]) % plan.length * (2.0 * np.pi / plan.length)
    ).sum(axis=0)
    for shift in range(plan.lon):
        source = shift * plan.width + np.arange(plan.width)
        far.append(kernel[(points[None, :] - source[:, None]) % plan.length] * used[None, :])
    return tuple(split_table(np.stack(table)) for table in (forward, inverse, far))


def split(value):
    high = value.astype(jnp.bfloat16)
    low = (value - high.astype(jnp.float32)).astype(jnp.bfloat16)
    return high, low


def three_pass(left, right, dims):
    def dot(a, b):
        return lax.dot_general(a, b, (dims, ((), ())), preferred_element_type=jnp.float32)

    return dot(left[0], right[0]) + (dot(left[0], right[1]) + dot(left[1], right[0]))


def forward_kernel(plan, scal, wind, theta, thick, top, bottom, t_high, t_low, *refs):
    outs, held = refs[:-1], refs[-1]
    step = pl.program_id(0)
    for at, role in enumerate(plan.roles):
        for j in range(role["count"]):

            @pl.when((scal[2] == at) & (step == j))
            def _(at=at, role=role, j=j):
                held[0] = wind[0]
                held[1] = wind[1]
                held[2] = theta[...]
                held[3] = thick[...]
                if j == role["count"] - 1:
                    place = scal[3] * (TILE - 2)
                    for field in range(FIELDS):
                        held[field, place] = top[field]
                        held[field, place + 1] = bottom[field]
                points = [held[u ^ scal[0]].reshape(plan.lanes, plan.width) for u in range(FIELDS)]
                size, offset = role["sizes"][j], role["offsets"][j]
                spec = three_pass(
                    (t_high[0, :size], t_low[0, :size]),
                    split(jnp.concatenate(points, axis=0)),
                    ((1,), (1,)),
                )
                for u in range(FIELDS):
                    outs[at * FIELDS + u][offset : offset + size, :] = spec[
                        :, u * plan.lanes : (u + 1) * plan.lanes
                    ]


def forward(plan, chunk, scal, winds, theta, thick, top, bottom, tabs):
    def tile_spec(lead):
        block = (pl.Element(TILE), pl.Element(SUB), pl.Element(plan.width))
        if lead:
            return pl.BlockSpec(
                (pl.Element(2),) + block, lambda j, s: (0, s[5 + j], chunk * SUB, 0)
            )
        return pl.BlockSpec(block, lambda j, s: (s[5 + j], chunk * SUB, 0))

    halo = pl.BlockSpec((FIELDS, SUB, plan.width), lambda j, s: (0, chunk, 0))
    table = pl.BlockSpec(
        (1, plan.table, plan.width), lambda j, s: (s[1], 0, 0), pipeline_mode=pl.Buffered(1)
    )
    totals = [role["total"] for role in plan.roles for _ in range(FIELDS)]
    flops = 2 * 3 * max(role["total"] for role in plan.roles) * FIELDS * plan.lanes * plan.width
    return pl.pallas_call(
        functools.partial(forward_kernel, plan),
        grid_spec=pltpu.PrefetchScalarGridSpec(
            num_scalar_prefetch=1,
            grid=(plan.tiles,),
            in_specs=[tile_spec(True), tile_spec(False), tile_spec(False), halo, halo, table, table],
            out_specs=[pl.BlockSpec((total, plan.lanes), lambda j, s: (0, 0)) for total in totals],
            scratch_shapes=[pltpu.VMEM((FIELDS, TILE, SUB, plan.width), jnp.float32)],
        ),
        out_shape=[jax.ShapeDtypeStruct((total, plan.lanes), jnp.float32) for total in totals],
        compiler_params=pltpu.CompilerParams(vmem_limit_bytes=VMEM),
        cost_estimate=pl.CostEstimate(flops=flops, bytes_accessed=20_000_000, transcendentals=0),
        name="partial_spectra",
    )(scal, winds, theta, thick, top, bottom, *tabs)


def far_kernel(plan, rows, d_high, d_low, out):
    part = three_pass(split(rows[0]), (d_high[0], d_low[0]), ((1,), (0,)))

    @pl.when(pl.program_id(0) == 0)
    def _():
        out[...] = part

    @pl.when(pl.program_id(0) > 0)
    def _():
        out[...] += part


def far_rows(plan, rows, tabs):
    count = rows.shape[1]
    table = pl.BlockSpec((1, plan.width, plan.wide), lambda j: (j, 0, 0))
    return pl.pallas_call(
        functools.partial(far_kernel, plan),
        grid=(plan.lon,),
        in_specs=[pl.BlockSpec((1, count, plan.width), lambda j: (j, 0, 0)), table, table],
        out_specs=pl.BlockSpec((count, plan.wide), lambda j: (0, 0)),
        out_shape=jax.ShapeDtypeStruct((count, plan.wide), jnp.float32),
        compiler_params=pltpu.CompilerParams(vmem_limit_bytes=VMEM),
        cost_estimate=pl.CostEstimate(
            flops=6 * count * plan.length * plan.wide, bytes_accessed=10_000_000, transcendentals=0
        ),
        name="farthest_rows",
    )(rows, *tabs)


def step_kernel(plan, step_rows, first, scal, slots, coef, wind, theta, thick, sides, top, bottom, far, cuts, i_high, i_low, *refs):
    spectra = refs[: FIELDS * len(plan.roles)]
    refs = refs[FIELDS * len(plan.roles) :]
    if not first:
        refs = refs[3:]
    new_wind, new_theta, new_thick, held, tile = refs
    block = pl.program_id(0)
    rows, width, wide = plan.rows, plan.width, plan.wide

    @pl.when(block == 0)
    def _():
        lane = lax.broadcasted_iota(jnp.int32, (SUB, wide - width), 1)

        def load(row, _):
            for field in range(FIELDS):
                side = sides[field, row]
                held[field, row + 1, :, :width] = (
                    wind[field, row] if field < 2 else (theta, thick)[field - 2][row]
                )
                held[field, row + 1, :, width:] = jnp.where(
                    lane == 0, side[:, 1:2], jnp.where(lane == wide - width - 1, side[:, 0:1], 0.0)
                )
            return 0

        lax.fori_loop(0, rows, load, 0)
        for field in range(FIELDS):
            held[field, 0, :, :width] = top[field]
            held[field, rows + 1, :, :width] = bottom[field]

        for at, role in enumerate(plan.roles):

            @pl.when(scal[2] == at)
            def _(at=at, role=role):
                for j in range(role["count"]):
                    size, offset = role["sizes"][j], role["offsets"][j]
                    index = lax.broadcasted_iota(jnp.int32, (size, plan.lanes), 0)
                    keep = lax.shift_right_logical(index + 1, 1) <= cuts[j : j + 1, :]
                    spec = jnp.concatenate(
                        [
                            jnp.where(keep, spectra[at * FIELDS + u][offset : offset + size, :], 0.0)
                            for u in range(FIELDS)
                        ],
                        axis=1,
                    )
                    back = three_pass(
                        split(spec), (i_high[0, :size], i_low[0, :size]), ((0,), (0,))
                    )
                    tile[...] = back.reshape(FIELDS, TILE, SUB, wide)

                    def store(row, _):
                        target = slots[j * TILE + row]

                        @pl.when(target >= 0)
                        def _():
                            for u in range(FIELDS):
                                held[u ^ scal[0], target] = tile[u, row]

                        return 0

                    lax.fori_loop(0, TILE, store, 0)

        @pl.when(scal[4] >= 0)
        def _():
            for field in range(FIELDS):
                held[field, scal[4]] = far[field]

    def stencil(row, _):
        at = block * step_rows + row

        def coefficient(which):
            return coef[which * rows + at]

        def diff_lon(value):
            return pltpu.roll(value, wide - 1, 1) - pltpu.roll(value, 1, 1)

        near = [held[field, at] for field in range(FIELDS)]
        here = [held[field, at + 1] for field in range(FIELDS)]
        next_ = [held[field, at + 2] for field in range(FIELDS)]
        u, v, t, h = here
        along, across, push, turn = [coefficient(k) for k in range(4)]
        advect = along * u
        carry = 0.1 * v
        turn_v, turn_u = turn * v, turn * u
        new_h = (
            h
            - along * diff_lon(u * h)
            - across * (next_[1] * next_[3] * coefficient(5) - near[1] * near[3] * coefficient(4))
        )
        new_t = t - advect * diff_lon(t) - carry * (next_[2] - near[2])
        new_u = u - advect * diff_lon(u) - carry * (next_[0] - near[0]) - push * diff_lon(h) + turn_v
        new_v = v - advect * diff_lon(v) - carry * (next_[1] - near[1]) - 0.15 * (next_[3] - near[3]) - turn_u
        new_wind[0, row] = new_u[:, :width]
        new_wind[1, row] = new_v[:, :width]
        new_theta[row] = new_t[:, :width]
        new_thick[row] = new_h[:, :width]
        return 0

    lax.fori_loop(0, step_rows, stencil, 0, unroll=3)


def substep(plan, chunk, scal, slots, coef, winds, theta, thick, sides, top, bottom, far, cuts, tabs, spectra, before):
    rows, width = plan.rows, plan.width
    step_rows = max(k for k in range(1, 16) if rows % k == 0)
    once = pl.Buffered(1)

    def whole(shape, index):
        return pl.BlockSpec(shape, index, pipeline_mode=once)

    table = whole((1, plan.table, plan.wide), lambda i, s, *_: (s[1], 0, 0))
    smem = pl.BlockSpec(memory_space=pltpu.SMEM)
    in_specs = [
        smem,
        smem,
        whole((2, rows, SUB, width), lambda i, s: (0, 0, chunk, 0)),
        whole((rows, SUB, width), lambda i, s: (0, chunk, 0)),
        whole((rows, SUB, width), lambda i, s: (0, chunk, 0)),
        whole((FIELDS, rows, SUB, 2), lambda i, s: (0, 0, chunk, 0)),
        whole((FIELDS, SUB, width), lambda i, s: (0, chunk, 0)),
        whole((FIELDS, SUB, width), lambda i, s: (0, chunk, 0)),
        whole((FIELDS, SUB, plan.wide), lambda i, s: (0, chunk, 0)),
        whole((plan.tiles, plan.lanes), lambda i, s: (0, 0)),
        table,
        table,
    ] + [whole(spec.shape, lambda i, s: (0, 0)) for spec in spectra]
    operands = [slots, coef, winds, theta, thick, sides, top, bottom, far, cuts, *tabs, *spectra]
    aliases = {}
    if before is not None:
        aliases = {1 + len(operands) + k: k for k in range(3)}
        in_specs += [pl.BlockSpec(memory_space=pl.ANY)] * 3
        operands += list(before)
    shapes = [(2, rows, plan.levels, width)] + [(rows, plan.levels, width)] * 2
    flops = 2 * 3 * max(role["total"] for role in plan.roles) * FIELDS * plan.lanes * plan.wide
    return pl.pallas_call(
        functools.partial(step_kernel, plan, step_rows, before is None),
        grid_spec=pltpu.PrefetchScalarGridSpec(
            num_scalar_prefetch=1,
            grid=(rows // step_rows,),
            in_specs=in_specs,
            out_specs=[
                pl.BlockSpec((2, step_rows, SUB, width), lambda i, s: (0, i, chunk, 0)),
                pl.BlockSpec((step_rows, SUB, width), lambda i, s: (i, chunk, 0)),
                pl.BlockSpec((step_rows, SUB, width), lambda i, s: (i, chunk, 0)),
            ],
            scratch_shapes=[
                pltpu.VMEM((FIELDS, rows + 2, SUB, plan.wide), jnp.float32),
                pltpu.VMEM((FIELDS, TILE, SUB, plan.wide), jnp.float32),
            ],
        ),
        out_shape=[jax.ShapeDtypeStruct(shape, jnp.float32) for shape in shapes],
        input_output_aliases=aliases,
        compiler_params=pltpu.CompilerParams(vmem_limit_bytes=VMEM),
        cost_estimate=pl.CostEstimate(flops=flops, bytes_accessed=25_000_000, transcendentals=0),
        name="inverse_and_substep",
    )(scal, *operands)


def lon_swap(plan, value, role, bit):
    pairs = [
        (block * plan.lon + place, block * plan.lon + (place ^ (1 << bit)))
        for block in plan.blocks(role)
        for place in range(plan.lon)
    ]
    return lax.ppermute(value, ("lat", "lon"), pairs)


def sum_over_lon(plan, role, slots, order):
    slots = dict(slots)
    for bit in order:
        sent = [s for s in slots if s >> bit & 1]
        for s in sorted(sent, key=lambda s: -bin(s).count("1")):
            slots[s ^ (1 << bit)] = slots[s ^ (1 << bit)] + lon_swap(plan, slots.pop(s), role, bit)
    for bit in reversed(order):
        for s in sorted(slots):
            slots[s | (1 << bit)] = lon_swap(plan, slots[s], role, bit)
    return slots


def all_sums(plan, place, arrays):
    result = []
    bits = plan.lon.bit_length() - 1
    for role in range(len(plan.roles)):
        order = list(range(bits)) if role % 2 == 0 else list(reversed(range(bits)))
        fields = arrays[role * FIELDS : (role + 1) * FIELDS]
        parts, own = plan.parts, place % plan.parts
        slots = {}
        for u, field in enumerate(fields):
            pieces = field.reshape(parts, -1, plan.lanes)
            for k in range(parts):
                slots[u * parts + k] = pieces[k ^ own] if parts > 1 else field
        slots = sum_over_lon(plan, role, slots, order)
        for u in range(FIELDS):
            if parts > 1:
                pieces = jnp.stack([slots[u * parts + k] for k in range(parts)])
                result.append(pieces[jnp.arange(parts) ^ own].reshape(-1, plan.lanes))
            else:
                result.append(slots[u])
    return result


def body(winds, theta, thick, polar_rows, cutoffs):
    lat, lon = lax.axis_size("lat"), lax.axis_size("lon")
    levels, rows, width = theta.shape
    sizes = (lat, lon, levels, rows, width, polar_rows.shape[0])
    plan = Plan(*sizes)
    t_tabs, i_tabs, d_tabs = [tuple(jnp.asarray(part) for part in pair) for pair in tables(sizes)]
    block, place = lax.axis_index("lat"), lax.axis_index("lon")
    winds = winds.transpose(0, 2, 1, 3)
    theta = theta.transpose(1, 0, 2)
    thick = thick.transpose(1, 0, 2)
    hemi = (block >= lat // 2).astype(jnp.int32)
    role = jnp.where(hemi == 1, lat - 1 - block, block)
    known = jnp.minimum(role, len(plan.roles))

    def line(row):
        return jnp.concatenate([winds[:, row], theta[row][None], thick[row][None]])

    south_pairs = [(b * lon + p, (b + 1) * lon + p) for b in range(lat - 1) for p in range(lon)]
    north_pairs = [(to, at) for at, to in south_pairs]
    top = lax.ppermute(line(rows - 1), ("lat", "lon"), south_pairs)
    bottom = lax.ppermute(line(0), ("lat", "lon"), north_pairs)

    north_run = jnp.sum((polar_rows < plan.total_rows // 2).astype(jnp.int32))
    far_row = jnp.where(hemi == 1, plan.total_rows - polar_rows.shape[0] + north_run, north_run - 1)
    far_at = far_row - block * rows + 1
    far_at = jnp.where((far_at >= 0) & (far_at <= rows + 1), far_at, -1)
    starts = jnp.asarray(plan.start_rows())[known, hemi]
    scal = jnp.concatenate(
        [jnp.stack([place // plan.parts, place, role, hemi, far_at]).astype(jnp.int32), starts]
    )

    arrays = [
        forward(plan, chunk, scal, winds, theta, thick, top, bottom, t_tabs)
        for chunk in range(plan.chunks)
    ]
    sums = [all_sums(plan, place, part) for part in arrays]

    at = jnp.clip(far_at - 1, 0, rows - 1)
    own = jnp.concatenate(
        [
            lax.dynamic_index_in_dim(winds, at, 1, keepdims=False),
            lax.dynamic_index_in_dim(theta, at, 0),
            lax.dynamic_index_in_dim(thick, at, 0),
        ]
    )
    own = jnp.where(far_at == 0, top, jnp.where(far_at == rows + 1, bottom, own))
    own = own.reshape(FIELDS * levels, width)
    moved = [own]
    for shift in range(1, lon):
        pairs = [
            (b * lon + (p + shift) % lon, b * lon + p)
            for r in plan.far_roles
            for b in plan.blocks(r)
            for p in range(lon)
        ]
        moved.append(lax.ppermute(own, ("lat", "lon"), pairs))
    far = far_rows(plan, jnp.stack(moved), d_tabs).reshape(FIELDS, levels, plan.wide)

    def edge(place_at):
        return jnp.concatenate(
            [winds[..., place_at], theta[None, ..., place_at], thick[None, ..., place_at]]
        )

    west = lax.ppermute(edge(width - 1), "lon", [(i, (i + 1) % lon) for i in range(lon)])
    east = lax.ppermute(edge(0), "lon", [((i + 1) % lon, i) for i in range(lon)])
    sides = jnp.stack([west, east], axis=-1)

    local = jnp.asarray(plan.slot_rows())[jnp.minimum(role, len(plan.roles) - 1), hemi].reshape(-1)
    hits = polar_rows[None, :] == (local + block * rows)[:, None]
    cut = jnp.sum(jnp.where(hits, cutoffs[None, :] + 1, 0), axis=1) - 1
    slots = jnp.where((cut >= 0) & (local >= -1), local + 1, -1).astype(jnp.int32)
    cuts = jnp.repeat(cut.reshape(plan.tiles, TILE), SUB, axis=1).astype(jnp.int32)

    ring = block * rows - 1 + jnp.arange(rows + 2, dtype=jnp.int32)
    centre = (ring.astype(jnp.float32) + 0.5) * (jnp.pi / plan.total_rows)
    cos, sin = jnp.sin(centre), -jnp.cos(centre)
    mid = cos[1:-1]
    coef = jnp.concatenate([0.025 / mid, 0.1 / mid, 0.05 / mid, 0.3 * sin[1:-1], cos[:-2], cos[2:]])

    out = None
    for chunk in range(plan.chunks):
        out = substep(
            plan, chunk, scal, slots, coef, winds, theta, thick, sides, top, bottom, far, cuts,
            i_tabs, sums[chunk], out,
        )
    return (out[0].transpose(0, 2, 1, 3), out[1].transpose(1, 0, 2), out[2].transpose(1, 0, 2))


def solution(mesh):
    in_specs = (P(None, None, "lat", "lon"), P(None, "lat", "lon"), P(None, "lat", "lon"), P(), P())
    out_specs = (P(None, None, "lat", "lon"), P(None, "lat", "lon"), P(None, "lat", "lon"))
    return jax.shard_map(body, mesh=mesh, in_specs=in_specs, out_specs=out_specs, check_vma=False)
```

```python
import functools

import jax
import jax.numpy as jnp
import ml_dtypes
import numpy as np
from jax import lax
from jax.experimental import pallas as pl
from jax.experimental.pallas import tpu as pltpu
from jax.sharding import PartitionSpec as P

TILE = 8
FIELDS = 4
VMEM = 58 * 1024 * 1024


def round_up(value, step):
    return -(-value // step) * step


class Plan:
    def __init__(self, lat, lon, levels, rows, width, listed):
        self.lat, self.lon, self.levels, self.rows, self.width = lat, lon, levels, rows, width
        self.total_rows, self.length = lat * rows, lon * width
        self.lanes = TILE * levels
        self.parts = lon // FIELDS
        self.wide = round_up(width + 2, 128)
        pole = listed // 2
        self.low, self.high = pole - pole // 4, pole + pole // 4
        top = self.length // 4 - 1

        def bound(depth):
            return min(2 * (depth + 1), top)

        self.roles = []
        last = self.high - 2
        for role in range(lat // 2):
            start = role * rows
            if start - 1 > last:
                break
            active = max(0, min(rows, last + 1 - start))
            count = -(-(active + 2) // TILE)
            waves = [bound(start + TILE * j + TILE - 1) for j in range(count)]
            deepest = start + active - 1
            if start + rows <= last:
                deepest = start + rows
            waves[-1] = bound(deepest)
            sizes = [round_up(2 * wave + 1, 16) for wave in waves]
            north = [TILE * j for j in range(count - 1)] + [
                max(0, min(TILE * (count - 1) - 2, rows - TILE))
            ]
            south = [rows - TILE * (j + 1) for j in range(count - 1)] + [
                max(0, rows - TILE * count + 2)
            ]
            self.roles.append(
                dict(
                    count=count,
                    sizes=sizes,
                    offsets=[sum(sizes[:j]) for j in range(count)],
                    total=sum(sizes),
                    starts=(north, south),
                )
            )
        self.tiles = max(role["count"] for role in self.roles)
        self.table = max(max(role["sizes"]) for role in self.roles)
        self.far_roles = [
            role
            for role in range(lat // 2)
            if role * rows - 1 <= self.high - 1 and (role + 1) * rows >= self.low - 1
        ]

    def blocks(self, role):
        return (role, self.lat - 1 - role)

    def slot_rows(self):
        table = np.full((len(self.roles), 2, self.tiles, TILE), -2, np.int32)
        for at, role in enumerate(self.roles):
            for hemi in range(2):
                for j in range(role["count"]):
                    own = role["starts"][hemi][j] + np.arange(TILE)
                    if j == role["count"] - 1:
                        place = 0 if hemi == 0 else TILE - 2
                        own[place], own[place + 1] = -1, self.rows
                    table[at, hemi, j] = own
        return table

    def start_rows(self):
        table = np.zeros((len(self.roles) + 1, 2, self.tiles), np.int32)
        for at, role in enumerate(self.roles):
            for hemi in range(2):
                table[at, hemi, : role["count"]] = role["starts"][hemi]
        return table


def split_table(table):
    high = table.astype(ml_dtypes.bfloat16)
    low = (table - high.astype(np.float64)).astype(ml_dtypes.bfloat16)
    return high, low


def waves_of(count):
    index = np.arange(count)
    return (index + 1) // 2, (index % 2 == 0) & (index > 0)


def trig(plan, count, points):
    wave, odd = waves_of(count)
    angle = (wave[:, None] * points[None, :]) % plan.length * (2.0 * np.pi / plan.length)
    return np.where(odd[:, None], np.sin(angle), np.cos(angle))


def out_points(plan):
    points = np.zeros(plan.wide, np.int64)
    points[: plan.width + 1] = np.arange(plan.width + 1)
    points[-1] = -1
    used = np.zeros(plan.wide, bool)
    used[: plan.width + 1] = True
    used[-1] = True
    return points, used


@functools.lru_cache(maxsize=None)
def tables(sizes):
    plan = Plan(*sizes)
    wave, odd = waves_of(plan.table)
    points, used = out_points(plan)
    forward, inverse, far = [], [], []
    weight = np.where(wave == 0, 1.0, 2.0) / plan.length
    for place in range(plan.lon):
        forward.append(trig(plan, plan.table, place * plan.width + np.arange(plan.width)))
        inverse.append(trig(plan, plan.table, place * plan.width + points) * weight[:, None] * used[None, :])
    keep = np.arange(1, plan.length // 4)
    ring = np.arange(plan.length)
    kernel = 1.0 / plan.length + (2.0 / plan.length) * np.cos(
        (keep[:, None] * ring[None, :]) % plan.length * (2.0 * np.pi / plan.length)
    ).sum(axis=0)
    for shift in range(plan.lon):
        source = shift * plan.width + np.arange(plan.width)
        far.append(kernel[(points[None, :] - source[:, None]) % plan.length] * used[None, :])
    return tuple(split_table(np.stack(table)) for table in (forward, inverse, far))


def split(value):
    high = value.astype(jnp.bfloat16)
    low = (value - high.astype(jnp.float32)).astype(jnp.bfloat16)
    return high, low


def three_pass(left, right, dims):
    def dot(a, b):
        return lax.dot_general(a, b, (dims, ((), ())), preferred_element_type=jnp.float32)

    return dot(left[0], right[0]) + (dot(left[0], right[1]) + dot(left[1], right[0]))


TABLE_AT = 11


def forward_kernel(plan, sets, scal, winds, theta, thick, top, bottom, t_high, t_low, *refs):
    count = len(plan.roles)
    outs, (points, spectra, in_sems, out_sems) = refs[:count], refs[count:]
    lanes, width = plan.lanes, plan.width
    for at, role in enumerate(plan.roles):

        @pl.when(scal[2] == at)
        def _(at=at, role=role):
            fields = [u ^ scal[0] for u in sets[at]]

            def fetch(j):
                rows = pl.ds(scal[TABLE_AT + j], TILE)
                for i, field in enumerate(fields):
                    to, sem = points.at[j % 2, i], in_sems.at[j % 2, i]

                    @pl.when(field < 2)
                    def _():
                        pltpu.make_async_copy(winds.at[jnp.minimum(field, 1), rows], to, sem).start()

                    @pl.when(field == 2)
                    def _():
                        pltpu.make_async_copy(theta.at[rows], to, sem).start()

                    @pl.when(field == 3)
                    def _():
                        pltpu.make_async_copy(thick.at[rows], to, sem).start()

            def arrive(j):
                rows = pl.ds(scal[TABLE_AT + j], TILE)
                for i in range(len(fields)):
                    pltpu.make_async_copy(theta.at[rows], points.at[j % 2, i], in_sems.at[j % 2, i]).wait()

            def leave(j):
                size, offset = role["sizes"][j], role["offsets"][j]
                return [
                    pltpu.make_async_copy(
                        spectra.at[j % 2, i, pl.ds(0, size)],
                        outs[at].at[i, pl.ds(offset, size)],
                        out_sems.at[j % 2, i],
                    )
                    for i in range(len(fields))
                ]

            fetch(0)
            for j in range(role["count"]):
                if j + 1 < role["count"]:
                    fetch(j + 1)
                arrive(j)
                if j == role["count"] - 1:
                    place = scal[3] * (TILE - 2)
                    for i, field in enumerate(fields):
                        points[j % 2, i, place] = top[field]
                        points[j % 2, i, place + 1] = bottom[field]
                size = role["sizes"][j]
                spec = three_pass(
                    (t_high[0, :size], t_low[0, :size]),
                    split(points[j % 2].reshape(len(fields) * lanes, width)),
                    ((1,), (1,)),
                )
                if j >= 2:
                    for copy in leave(j - 2):
                        copy.wait()
                for i in range(len(fields)):
                    spectra[j % 2, i, :size, :] = spec[:, i * lanes : (i + 1) * lanes]
                for copy in leave(j):
                    copy.start()
            for j in range(max(0, role["count"] - 2), role["count"]):
                for copy in leave(j):
                    copy.wait()


def forward(plan, sets, scal, winds, theta, thick, top, bottom, tabs):
    count = len(sets[0])
    anywhere = pl.BlockSpec(memory_space=pl.ANY)
    halo = pl.BlockSpec((FIELDS, plan.levels, plan.width), lambda i, s: (0, 0, 0))
    table = pl.BlockSpec((1, plan.table, plan.width), lambda i, s: (s[1], 0, 0))
    totals = [role["total"] for role in plan.roles]
    return pl.pallas_call(
        functools.partial(forward_kernel, plan, sets),
        grid_spec=pltpu.PrefetchScalarGridSpec(
            num_scalar_prefetch=1,
            grid=(1,),
            in_specs=[anywhere] * 3 + [halo, halo, table, table],
            out_specs=[anywhere] * len(totals),
            scratch_shapes=[
                pltpu.VMEM((2, count, TILE, plan.levels, plan.width), jnp.float32),
                pltpu.VMEM((2, count, plan.table, plan.lanes), jnp.float32),
                pltpu.SemaphoreType.DMA((2, count)),
                pltpu.SemaphoreType.DMA((2, count)),
            ],
        ),
        out_shape=[jax.ShapeDtypeStruct((count, total, plan.lanes), jnp.float32) for total in totals],
        compiler_params=pltpu.CompilerParams(vmem_limit_bytes=VMEM),
        cost_estimate=pl.CostEstimate(
            flops=6 * max(totals) * count * plan.lanes * plan.width,
            bytes_accessed=15_000_000,
            transcendentals=0,
        ),
        name="partial_spectra",
    )(scal, winds, theta, thick, top, bottom, *tabs)


def far_kernel(plan, rows, d_high, d_low, out):
    part = three_pass(split(rows[0]), (d_high[0], d_low[0]), ((1,), (0,)))

    @pl.when(pl.program_id(0) == 0)
    def _():
        out[...] = part

    @pl.when(pl.program_id(0) > 0)
    def _():
        out[...] += part


def far_rows(plan, rows, tabs):
    count = rows.shape[1]
    table = pl.BlockSpec((1, plan.width, plan.wide), lambda j: (j, 0, 0))
    return pl.pallas_call(
        functools.partial(far_kernel, plan),
        grid=(plan.lon,),
        in_specs=[pl.BlockSpec((1, count, plan.width), lambda j: (j, 0, 0)), table, table],
        out_specs=pl.BlockSpec((count, plan.wide), lambda j: (0, 0)),
        out_shape=jax.ShapeDtypeStruct((count, plan.wide), jnp.float32),
        compiler_params=pltpu.CompilerParams(vmem_limit_bytes=VMEM),
        cost_estimate=pl.CostEstimate(
            flops=6 * count * plan.length * plan.wide, bytes_accessed=10_000_000, transcendentals=0
        ),
        name="farthest_rows",
    )(rows, *tabs)


def step_kernel(plan, step_rows, scal, coef, wind, theta, thick, sides, top, bottom, far, cuts, i_high, i_low, *refs):
    spectra = refs[: FIELDS * len(plan.roles)]
    new_wind, new_theta, new_thick, held, sums, sems = refs[FIELDS * len(plan.roles) :]
    step = pl.program_id(0)
    rows, width, wide, levels = plan.rows, plan.width, plan.wide, plan.levels
    last_step = rows // step_rows

    @pl.when(step == 0)
    def _():
        for at, role in enumerate(plan.roles):

            @pl.when(scal[2] == at)
            def _(at=at, role=role):
                order = [role["count"] - 1] + list(range(role["count"] - 1))

                def copies(j):
                    part = pl.ds(role["offsets"][j], role["sizes"][j])
                    return [
                        pltpu.make_async_copy(
                            spectra[at * FIELDS + u].at[part], sums.at[u, part], sems.at[j, u]
                        )
                        for u in range(FIELDS)
                    ]

                for j in order:
                    for copy in copies(j):
                        copy.start()
                for j in order:
                    for copy in copies(j):
                        copy.wait()
                    size, offset = role["sizes"][j], role["offsets"][j]
                    index = lax.broadcasted_iota(jnp.int32, (size, plan.lanes), 0)
                    keep = lax.shift_right_logical(index + 1, 1) <= cuts[j : j + 1, :]
                    spec = jnp.concatenate(
                        [
                            jnp.where(keep, sums[u, offset : offset + size, :], 0.0)
                            for u in range(FIELDS)
                        ],
                        axis=1,
                    )
                    back = three_pass(
                        split(spec.T), (i_high[0, :size], i_low[0, :size]), ((1,), (0,))
                    ).reshape(FIELDS, TILE, levels, wide)
                    for u in range(FIELDS):
                        held[u ^ scal[0], pl.ds(scal[TABLE_AT + j] + 1, TILE)] = back[u]
                    if j == role["count"] - 1:
                        for hemi in range(2):
                            place = hemi * (TILE - 2)
                            for side in range(2):

                                @pl.when((scal[3] == hemi) & (scal[5 + side] == 1))
                                def _(place=place, side=side):
                                    for u in range(FIELDS):
                                        held[u ^ scal[0], side * (rows + 1)] = back[u, place + side]

        for side, line in enumerate((top, bottom)):

            @pl.when(scal[5 + side] == 0)
            def _(side=side, line=line):
                for field in range(FIELDS):
                    held[field, side * (rows + 1), :, :width] = line[field]

    base = step * step_rows

    @pl.when(step < last_step)
    def _():
        lane = lax.broadcasted_iota(jnp.int32, (levels, wide - width), 1)

        def load(row, _):
            at = row - base
            for field in range(FIELDS):
                side = sides[field, at]
                held[field, row + 1, :, :width] = (
                    wind[field, at] if field < 2 else (theta, thick)[field - 2][at]
                )
                held[field, row + 1, :, width:] = jnp.where(
                    lane == 0, side[:, 1:2], jnp.where(lane == wide - width - 1, side[:, 0:1], 0.0)
                )
            return 0

        lax.fori_loop(jnp.maximum(base, scal[7]), jnp.minimum(base + step_rows, scal[8]), load, 0)

    @pl.when(step == 0)
    def _():
        @pl.when(scal[4] >= 0)
        def _():
            for field in range(FIELDS):
                held[field, scal[4]] = far[field]

    def diff_lon(value):
        return pltpu.roll(value, wide - 1, 1) - pltpu.roll(value, 1, 1)

    def stencil(row, _):
        at = base - step_rows + row
        along, across, push, turn, cos_north, cos_south = [coef[k * rows + at] for k in range(6)]
        for part in range(levels // 8):
            some = pl.ds(part * 8, 8)

            def near(field):
                return held[field, at, some]

            def here(field):
                return held[field, at + 1, some]

            def after(field):
                return held[field, at + 2, some]

            u, v = here(0), here(1)
            advect, carry = along * u, 0.1 * v
            h = here(3)
            new_thick[row, some] = (
                h
                - along * diff_lon(u * h)
                - (across * cos_south * (after(1) * after(3)) - across * cos_north * (near(1) * near(3)))
            )[:, :width]
            new_wind[0, row, some] = (
                u - advect * diff_lon(u) - carry * (after(0) - near(0)) - push * diff_lon(h) + turn * v
            )[:, :width]
            new_wind[1, row, some] = (
                v
                - advect * diff_lon(v)
                - carry * (after(1) - near(1))
                - 0.15 * (after(3) - near(3))
                - turn * u
            )[:, :width]
            t = here(2)
            new_theta[row, some] = (t - advect * diff_lon(t) - carry * (after(2) - near(2)))[:, :width]
        return 0

    @pl.when(step > 0)
    def _():
        lax.fori_loop(0, step_rows, stencil, 0)


def substep(plan, step_rows, scal, coef, winds, theta, thick, sides, top, bottom, far, cuts, tabs, spectra):
    rows, width, levels = plan.rows, plan.width, plan.levels
    once = pl.Buffered(1)
    steps = rows // step_rows

    def block(i, s):
        return jnp.clip(i, s[9], s[10])

    def whole(shape, index):
        return pl.BlockSpec(shape, index, pipeline_mode=once)

    table = whole((1, plan.table, plan.wide), lambda i, s: (s[1], 0, 0))
    anywhere = pl.BlockSpec(memory_space=pl.ANY)
    in_specs = [
        pl.BlockSpec(memory_space=pltpu.SMEM),
        pl.BlockSpec((2, step_rows, levels, width), lambda i, s: (0, block(i, s), 0, 0)),
        pl.BlockSpec((step_rows, levels, width), lambda i, s: (block(i, s), 0, 0)),
        pl.BlockSpec((step_rows, levels, width), lambda i, s: (block(i, s), 0, 0)),
        pl.BlockSpec((FIELDS, step_rows, levels, 2), lambda i, s: (0, block(i, s), 0, 0)),
        whole((FIELDS, levels, width), lambda i, s: (0, 0, 0)),
        whole((FIELDS, levels, width), lambda i, s: (0, 0, 0)),
        whole((FIELDS, levels, plan.wide), lambda i, s: (0, 0, 0)),
        whole((plan.tiles, plan.lanes), lambda i, s: (0, 0)),
        table,
        table,
    ] + [anywhere] * len(spectra)
    shapes = [(2, rows, levels, width)] + [(rows, levels, width)] * 2
    most = max(role["total"] for role in plan.roles)
    return pl.pallas_call(
        functools.partial(step_kernel, plan, step_rows),
        grid_spec=pltpu.PrefetchScalarGridSpec(
            num_scalar_prefetch=1,
            grid=(steps + 1,),
            in_specs=in_specs,
            out_specs=[
                pl.BlockSpec((2, step_rows, levels, width), lambda i, s: (0, jnp.maximum(i - 1, 0), 0, 0)),
                pl.BlockSpec((step_rows, levels, width), lambda i, s: (jnp.maximum(i - 1, 0), 0, 0)),
                pl.BlockSpec((step_rows, levels, width), lambda i, s: (jnp.maximum(i - 1, 0), 0, 0)),
            ],
            scratch_shapes=[
                pltpu.VMEM((FIELDS, rows + 2, levels, plan.wide), jnp.float32),
                pltpu.VMEM((FIELDS, most, plan.lanes), jnp.float32),
                pltpu.SemaphoreType.DMA((plan.tiles, FIELDS)),
            ],
        ),
        out_shape=[jax.ShapeDtypeStruct(shape, jnp.float32) for shape in shapes],
        compiler_params=pltpu.CompilerParams(vmem_limit_bytes=VMEM),
        cost_estimate=pl.CostEstimate(
            flops=6 * most * FIELDS * plan.lanes * plan.wide, bytes_accessed=40_000_000, transcendentals=0
        ),
        name="inverse_and_substep",
    )(scal, coef, winds, theta, thick, sides, top, bottom, far, cuts, *tabs, *spectra)


def lon_swap(plan, value, role, bit):
    pairs = [
        (block * plan.lon + place, block * plan.lon + (place ^ (1 << bit)))
        for block in plan.blocks(role)
        for place in range(plan.lon)
    ]
    return lax.ppermute(value, ("lat", "lon"), pairs)


def spread(plan, role, slots, order):
    for bit in reversed(order):
        for s in sorted(slots):
            slots[s | (1 << bit)] = lon_swap(plan, slots[s], role, bit)
    return slots


def gather_sums(plan, role, slots, order):
    slots = dict(slots)
    for bit in order:
        sent = [s for s in slots if s >> bit & 1]
        for s in sorted(sent, key=lambda s: -bin(s).count("1")):
            slots[s ^ (1 << bit)] = slots[s ^ (1 << bit)] + lon_swap(plan, slots.pop(s), role, bit)
    return spread(plan, role, slots, order)


def field_sets(plan):
    sent, kept = [], []
    for at in range(len(plan.roles)):
        bit = at % 2
        sent.append([u for u in range(FIELDS) if u >> bit & 1])
        kept.append([u for u in range(FIELDS) if not u >> bit & 1])
    return sent, kept


def role_sums(plan, place, at, sent, kept):
    first, second = field_sets(plan)
    parts, own = plan.parts, place % plan.parts
    if parts == 1:
        near, far = at % 2, 1 - at % 2
        moved = lon_swap(plan, sent, at, near)
        send = kept[1] + moved[1]
        slots = {0: (kept[0] + moved[0]) + lon_swap(plan, send, at, far)}
        slots = spread(plan, at, slots, [near, far])
        return [slots[u] for u in range(FIELDS)]
    bits = plan.lon.bit_length() - 1
    slots = {}
    for us, array in ((first[at], sent), (second[at], kept)):
        for i, u in enumerate(us):
            pieces = array[i].reshape(parts, -1, plan.lanes)
            for k in range(parts):
                slots[u * parts + k] = pieces[k ^ own]
    order = list(range(bits)) if at % 2 == 0 else list(reversed(range(bits)))
    slots = gather_sums(plan, at, slots, order)
    result = []
    for u in range(FIELDS):
        pieces = jnp.stack([slots[u * parts + k] for k in range(parts)])
        result.append(pieces[jnp.arange(parts) ^ own].reshape(-1, plan.lanes))
    return result


def body(winds, theta, thick, polar_rows, cutoffs):
    lat, lon = lax.axis_size("lat"), lax.axis_size("lon")
    levels, rows, width = theta.shape
    sizes = (lat, lon, levels, rows, width, polar_rows.shape[0])
    plan = Plan(*sizes)
    t_tabs, i_tabs, d_tabs = [tuple(jnp.asarray(part) for part in pair) for pair in tables(sizes)]
    block, place = lax.axis_index("lat"), lax.axis_index("lon")
    winds = winds.transpose(0, 2, 1, 3)
    theta = theta.transpose(1, 0, 2)
    thick = thick.transpose(1, 0, 2)
    hemi = (block >= lat // 2).astype(jnp.int32)
    role = jnp.where(hemi == 1, lat - 1 - block, block)
    known = jnp.minimum(role, len(plan.roles))

    def line(row):
        return jnp.stack([winds[0, row], winds[1, row], theta[row], thick[row]])

    south_pairs = [(b * lon + p, (b + 1) * lon + p) for b in range(lat - 1) for p in range(lon)]
    north_pairs = [(to, at) for at, to in south_pairs]
    top = lax.ppermute(line(rows - 1), ("lat", "lon"), south_pairs)
    bottom = lax.ppermute(line(0), ("lat", "lon"), north_pairs)

    step_rows = max(k for k in range(1, 16) if rows % k == 0)
    listed = polar_rows.shape[0]
    north_run = jnp.sum((polar_rows < plan.total_rows // 2).astype(jnp.int32))
    south_first = plan.total_rows - listed + north_run
    far_row = jnp.where(hemi == 1, south_first, north_run - 1)
    far_at = far_row - block * rows + 1
    far_at = jnp.where((far_at >= 0) & (far_at <= rows + 1), far_at, -1)
    raw_from = jnp.clip(north_run - block * rows, 0, rows)
    raw_to = jnp.clip(south_first - block * rows, 0, rows)
    block_from = jnp.minimum(raw_from, rows - 1) // step_rows
    block_to = jnp.maximum(block_from, jnp.maximum(raw_to - 1, 0) // step_rows)
    above, below = block * rows - 1, (block + 1) * rows

    def is_listed(row):
        return (row >= 0) & (row < plan.total_rows) & ((row < north_run) | (row >= south_first))

    starts = jnp.asarray(plan.start_rows())[known, hemi]
    facts = [
        place // plan.parts, place, role, hemi, far_at, is_listed(above), is_listed(below),
        raw_from, raw_to, block_from, block_to,
    ]
    scal = jnp.concatenate([jnp.stack([jnp.asarray(fact).astype(jnp.int32) for fact in facts]), starts])

    first, second = field_sets(plan)
    sent = forward(plan, first, scal, winds, theta, thick, top, bottom, t_tabs)
    kept = forward(plan, second, scal, winds, theta, thick, top, bottom, t_tabs)
    sums = []
    for at in range(len(plan.roles)):
        sums += role_sums(plan, place, at, sent[at], kept[at])

    at = jnp.clip(far_at - 1, 0, rows - 1)
    own = jnp.stack(
        [
            lax.dynamic_index_in_dim(array, at, 0, keepdims=False)
            for array in (winds[0], winds[1], theta, thick)
        ]
    )
    own = jnp.where(far_at == 0, top, jnp.where(far_at == rows + 1, bottom, own))
    own = own.reshape(FIELDS * levels, width)
    moved = [own]
    for shift in range(1, lon):
        pairs = [
            (b * lon + (p + shift) % lon, b * lon + p)
            for r in plan.far_roles
            for b in plan.blocks(r)
            for p in range(lon)
        ]
        moved.append(lax.ppermute(own, ("lat", "lon"), pairs))
    far = far_rows(plan, jnp.stack(moved), d_tabs).reshape(FIELDS, levels, plan.wide)

    def edge(place_at):
        return jnp.stack([array[..., place_at] for array in (winds[0], winds[1], theta, thick)])

    west = lax.ppermute(edge(width - 1), "lon", [(i, (i + 1) % lon) for i in range(lon)])
    east = lax.ppermute(edge(0), "lon", [((i + 1) % lon, i) for i in range(lon)])
    sides = jnp.stack([west, east], axis=-1)

    local = jnp.asarray(plan.slot_rows())[jnp.minimum(role, len(plan.roles) - 1), hemi].reshape(-1)
    hits = polar_rows[None, :] == (local + block * rows)[:, None]
    cut = jnp.sum(jnp.where(hits, cutoffs[None, :] + 1, 0), axis=1) - 1
    cuts = jnp.repeat(cut.reshape(plan.tiles, TILE), levels, axis=1).astype(jnp.int32)

    ring = block * rows - 1 + jnp.arange(rows + 2, dtype=jnp.int32)
    centre = (ring.astype(jnp.float32) + 0.5) * (jnp.pi / plan.total_rows)
    cos, sin = jnp.sin(centre), -jnp.cos(centre)
    mid = cos[1:-1]
    coef = jnp.concatenate([0.025 / mid, 0.1 / mid, 0.05 / mid, 0.3 * sin[1:-1], cos[:-2], cos[2:]])

    out = substep(
        plan, step_rows, scal, coef, winds, theta, thick, sides, top, bottom, far, cuts, i_tabs, sums
    )
    return (out[0].transpose(0, 2, 1, 3), out[1].transpose(1, 0, 2), out[2].transpose(1, 0, 2))


def solution(mesh):
    in_specs = (P(None, None, "lat", "lon"), P(None, "lat", "lon"), P(None, "lat", "lon"), P(), P())
    out_specs = (P(None, None, "lat", "lon"), P(None, "lat", "lon"), P(None, "lat", "lon"))
    return jax.shard_map(body, mesh=mesh, in_specs=in_specs, out_specs=out_specs, check_vma=False)
```

```python
import functools

import jax
import jax.numpy as jnp
import ml_dtypes
import numpy as np
from jax import lax
from jax.experimental import pallas as pl
from jax.experimental.pallas import tpu as pltpu
from jax.sharding import PartitionSpec as P

FIELDS = 4
LANES = 128
VMEM = 60 * 1024 * 1024


def round_up(value, step):
    return -(-value // step) * step


class Group:
    def __init__(self, first, stop, extras, blocks, levels):
        self.first, self.stop, self.extras, self.blocks = first, stop, extras, blocks
        self.own = stop - first
        self.slots = self.own + len(extras)
        self.height = self.slots * levels
        self.total = self.height * blocks


class Plan:
    def __init__(self, lat, lon, levels, rows, width, listed):
        self.lat, self.lon, self.levels, self.rows, self.width = lat, lon, levels, rows, width
        self.total_rows, self.length = lat * rows, lon * width
        self.parts = lon // FIELDS
        self.wide = round_up(width + 2, LANES)
        pole = listed // 2
        self.high = pole + pole // 4
        top = self.length // 4 - 1

        def blocks_of(depth):
            return -(-(2 * min(2 * (depth + 1), top) + 1) // LANES)

        self.roles = []
        last = self.high - 2
        for role in range(lat // 2):
            start = role * rows
            if start - 1 > last:
                break
            need = {}
            for depth in range(start, min(start + rows - 1, last) + 1):
                need.setdefault(blocks_of(depth), []).append(depth - start)
            extras = {}
            if role > 0:
                extras.setdefault(blocks_of(start - 1), []).append("near")
            if start + rows <= last:
                extras.setdefault(blocks_of(start + rows), []).append("far")
            groups = []
            for blocks in sorted(set(need) | set(extras)):
                own = need.get(blocks, [0, -1])
                groups.append(
                    Group(own[0], own[-1] + 1 if blocks in need else 0, extras.get(blocks, []), blocks, levels)
                )
            groups.append(Group(0, 0, ["farthest"], -(-(2 * top + 1) // LANES), levels))
            self.roles.append(groups)
        self.slots = max(sum(group.slots for group in groups) for groups in self.roles)
        self.table = LANES * max(group.blocks for groups in self.roles for group in groups)
        count = len(self.roles)
        self.lent = {}
        if self.parts == 1 and 2 * count <= lat // 2:
            self.lent = {count - 1: len(self.roles[-1]) - 2}

    def blocks(self, role):
        return (role, self.lat - 1 - role)

    def parcels(self, at):
        indices = range(len(self.roles[at]))
        away = self.lent.get(at)
        home = [g for g in indices if g != away]
        return [home] if away is None else [home, [away]]

    def places(self):
        result, number = {}, 0
        for at in range(len(self.roles)):
            for parcel in self.parcels(at):
                offset = 0
                for g in parcel:
                    result[at, g] = (number, offset)
                    offset += self.roles[at][g].total
                number += 1
        return result

    def heights(self):
        return [
            sum(self.roles[at][g].total for g in parcel)
            for at in range(len(self.roles))
            for parcel in self.parcels(at)
        ]

    def slot_rows(self):
        table = np.full((len(self.roles), 2, self.slots), -1, np.int32)
        for at, groups in enumerate(self.roles):
            for hemi in range(2):
                rows = []
                for group in groups:
                    first = group.first if hemi == 0 else self.rows - group.stop
                    rows += [first + 1 + k for k in range(group.own)]
                    ends = (0, self.rows + 1) if hemi == 0 else (self.rows + 1, 0)
                    rows += [{"near": ends[0], "far": ends[1], "farthest": -2}[name] for name in group.extras]
                table[at, hemi, : len(rows)] = rows
        return table


def split_table(table):
    high = table.astype(ml_dtypes.bfloat16)
    low = (table - high.astype(np.float64)).astype(ml_dtypes.bfloat16)
    return high, low


@functools.lru_cache(maxsize=None)
def tables(sizes):
    plan = Plan(*sizes)
    index = np.arange(plan.table)
    wave, odd = (index + 1) // 2, (index % 2 == 0) & (index > 0)
    used = wave < plan.length // 4
    points = np.zeros(plan.wide, np.int64)
    points[: plan.width + 1] = np.arange(plan.width + 1)
    points[-1] = -1
    shown = np.zeros(plan.wide, bool)
    shown[: plan.width + 1] = True
    shown[-1] = True

    def trig(at):
        angle = (wave[:, None] * at[None, :]) % plan.length * (2.0 * np.pi / plan.length)
        return np.where(odd[:, None], np.sin(angle), np.cos(angle)) * used[:, None]

    weight = np.where(wave == 0, 1.0, 2.0) / plan.length
    forward, inverse = [], []
    for place in range(plan.lon):
        forward.append(trig(place * plan.width + np.arange(plan.width)).T)
        inverse.append(trig(place * plan.width + points) * weight[:, None] * shown[None, :])
    return tuple(split_table(np.stack(table)) for table in (forward, inverse))


def split(value):
    high = value.astype(jnp.bfloat16)
    low = (value - high.astype(jnp.float32)).astype(jnp.bfloat16)
    return high, low


def three_pass(left, right):
    total = jnp.dot(left[0], right[0], preferred_element_type=jnp.float32)
    total += jnp.dot(left[0], right[1], preferred_element_type=jnp.float32)
    total += jnp.dot(left[1], right[0], preferred_element_type=jnp.float32)
    return total


def forward_kernel(plan, sets, scal, winds, theta, thick, top, bottom, t_high, t_low, *refs):
    places, heights = plan.places(), plan.heights()
    outs, (points, spectra, in_sems, out_sems) = refs[: len(heights)], refs[len(heights) :]
    levels, width = plan.levels, plan.width
    for at, groups in enumerate(plan.roles):

        @pl.when(scal[2] == at)
        def _(at=at, groups=groups):
            order = sorted(range(len(groups)), key=lambda g: -groups[g].blocks)
            units = [(g, i, u) for g in order for i, u in enumerate(sets[at])]

            def first_row(group):
                if "farthest" in group.extras:
                    return jnp.clip(scal[4] - 1, 0, plan.rows - 1), 1
                return jnp.where(scal[3] == 1, plan.rows - group.stop, group.first), group.own

            def fetch(n):
                g, _, u = units[n]
                first, count = first_row(groups[g])
                rows, field = pl.ds(first, count), u ^ scal[0]
                to, sem = points.at[n % 2, pl.ds(0, count)], in_sems.at[n % 2]

                @pl.when(field < 2)
                def _():
                    pltpu.make_async_copy(winds.at[jnp.minimum(field, 1), rows], to, sem).start()

                @pl.when(field == 2)
                def _():
                    pltpu.make_async_copy(theta.at[rows], to, sem).start()

                @pl.when(field == 3)
                def _():
                    pltpu.make_async_copy(thick.at[rows], to, sem).start()

            def arrive(n):
                first, count = first_row(groups[units[n][0]])
                pltpu.make_async_copy(
                    theta.at[pl.ds(first, count)], points.at[n % 2, pl.ds(0, count)], in_sems.at[n % 2]
                ).wait()

            def leave(n):
                g, i, _ = units[n]
                number, offset = places[at, g]
                total = groups[g].total
                return pltpu.make_async_copy(
                    spectra.at[n % 2, pl.ds(0, total)],
                    outs[number].at[i, pl.ds(offset, total)],
                    out_sems.at[n % 2],
                )

            fetch(0)
            for n, (g, i, u) in enumerate(units):
                group = groups[g]
                if n + 1 < len(units):
                    fetch(n + 1)
                arrive(n)
                field = u ^ scal[0]
                for k, name in enumerate(group.extras):
                    slot = group.own + k
                    if name == "farthest":
                        from_top, from_bottom = scal[4] == 0, scal[4] == plan.rows + 1
                        slot = 0
                    else:
                        from_top = scal[3] == (0 if name == "near" else 1)
                        from_bottom = jnp.logical_not(from_top)

                    @pl.when(from_top)
                    def _(slot=slot, n=n):
                        points[n % 2, slot] = top[field]

                    @pl.when(from_bottom)
                    def _(slot=slot, n=n):
                        points[n % 2, slot] = bottom[field]

                lanes = group.blocks * LANES
                spec = three_pass(
                    split(points[n % 2, : group.slots].reshape(group.height, width)),
                    (t_high[0, :, :lanes], t_low[0, :, :lanes]),
                )
                if n >= 2:
                    leave(n - 2).wait()
                for b in range(group.blocks):
                    spectra[n % 2, b * group.height : (b + 1) * group.height, :] = spec[
                        :, b * LANES : (b + 1) * LANES
                    ]
                leave(n).start()
            for n in range(max(0, len(units) - 2), len(units)):
                leave(n).wait()


def forward(plan, sets, scal, winds, theta, thick, top, bottom, tabs):
    count = len(sets[0])
    anywhere = pl.BlockSpec(memory_space=pl.ANY)
    halo = pl.BlockSpec((FIELDS, plan.levels, plan.width), lambda i, s: (0, 0, 0))
    table = pl.BlockSpec((1, plan.width, plan.table), lambda i, s: (s[1], 0, 0))
    heights = plan.heights()
    slots = max(group.slots for groups in plan.roles for group in groups)
    total = max(group.total for groups in plan.roles for group in groups)
    return pl.pallas_call(
        functools.partial(forward_kernel, plan, sets),
        grid_spec=pltpu.PrefetchScalarGridSpec(
            num_scalar_prefetch=1,
            grid=(1,),
            in_specs=[anywhere] * 3 + [halo, halo, table, table],
            out_specs=[anywhere] * len(heights),
            scratch_shapes=[
                pltpu.VMEM((2, slots, plan.levels, plan.width), jnp.float32),
                pltpu.VMEM((2, total, LANES), jnp.float32),
                pltpu.SemaphoreType.DMA((2,)),
                pltpu.SemaphoreType.DMA((2,)),
            ],
        ),
        out_shape=[jax.ShapeDtypeStruct((count, height, LANES), jnp.float32) for height in heights],
        compiler_params=pltpu.CompilerParams(vmem_limit_bytes=VMEM),
        cost_estimate=pl.CostEstimate(
            flops=6 * max(heights) * count * LANES * plan.width, bytes_accessed=15_000_000, transcendentals=0
        ),
        name="partial_spectra",
    )(scal, winds, theta, thick, top, bottom, *tabs)


def edge_kernel(plan, *refs):
    ins, (first, last) = refs[:6], refs[6:]
    lane = lax.broadcasted_iota(jnp.int32, (plan.levels, LANES), 1)
    end = (plan.width - 1) % LANES
    for out, (wind, theta, thick), column in ((first, ins[:3], 0), (last, ins[3:], end)):

        def pick(row, kept, wind=wind, theta=theta, thick=thick, column=column):
            rows = (wind[0, row], wind[1, row], theta[row], thick[row])
            return tuple(
                jnp.where(lane == row, value[:, column : column + 1], old) for value, old in zip(rows, kept)
            )

        kept = lax.fori_loop(0, plan.rows, pick, (jnp.zeros((plan.levels, LANES), jnp.float32),) * FIELDS)
        for field in range(FIELDS):
            out[field] = kept[field]


def edges(plan, winds, theta, thick):
    specs = []
    for at in (0, (plan.width - 1) // LANES):
        specs.append(pl.BlockSpec((2, plan.rows, plan.levels, LANES), lambda i, at=at: (0, 0, 0, at)))
        specs += [pl.BlockSpec((plan.rows, plan.levels, LANES), lambda i, at=at: (0, 0, at))] * 2
    shape = (FIELDS, plan.levels, LANES)
    return pl.pallas_call(
        functools.partial(edge_kernel, plan),
        grid=(1,),
        in_specs=specs,
        out_specs=[pl.BlockSpec(shape, lambda i: (0, 0, 0))] * 2,
        out_shape=[jax.ShapeDtypeStruct(shape, jnp.float32)] * 2,
        compiler_params=pltpu.CompilerParams(vmem_limit_bytes=VMEM),
        cost_estimate=pl.CostEstimate(flops=0, bytes_accessed=6_000_000, transcendentals=0),
        name="edge_columns",
    )(winds, theta, thick, winds, theta, thick)


def step_kernel(plan, step_rows, scal, coef, wind, theta, thick, west, east, top, bottom, cuts, i_high, i_low, *refs):
    places, heights = plan.places(), plan.heights()
    spectra = refs[: FIELDS * len(heights)]
    new_wind, new_theta, new_thick, held, sums, sems = refs[FIELDS * len(heights) :]
    step = pl.program_id(0)
    rows, width, wide, levels = plan.rows, plan.width, plan.wide, plan.levels
    last_step = rows // step_rows

    def inverse(at, groups):
        slot_at = np.cumsum([0] + [group.slots for group in groups])
        row_at = np.cumsum([0] + [group.total for group in groups])

        def copies(g):
            number, offset = places[at, g]
            return [
                pltpu.make_async_copy(
                    spectra[number * FIELDS + u].at[pl.ds(offset, groups[g].total)],
                    sums.at[u, pl.ds(int(row_at[g]), groups[g].total)],
                    sems.at[g, u],
                )
                for u in range(FIELDS)
            ]

        for g in range(len(groups)):
            for copy in copies(g):
                copy.start()
        for g, group in enumerate(groups):
            for copy in copies(g):
                copy.wait()
            height, lanes = group.height, group.blocks * LANES
            from_row = int(slot_at[g]) * levels
            cut = cuts[from_row : from_row + height, :]
            lane = lax.broadcasted_iota(jnp.int32, (height, LANES), 1)
            for u in range(FIELDS):
                spec = jnp.concatenate(
                    [
                        jnp.where(
                            lax.shift_right_logical(lane + (b * LANES + 1), 1) <= cut,
                            sums[u, int(row_at[g]) + b * height : int(row_at[g]) + (b + 1) * height, :],
                            0.0,
                        )
                        for b in range(group.blocks)
                    ],
                    axis=1,
                )
                back = three_pass(split(spec), (i_high[0, :lanes], i_low[0, :lanes]))
                back = back.reshape(group.slots, levels, wide)
                field = u ^ scal[0]
                if group.own:
                    first = jnp.where(scal[3] == 1, rows - group.stop, group.first) + 1
                    held[field, pl.ds(first, group.own)] = back[: group.own]
                for k, name in enumerate(group.extras):
                    slot = group.own + k
                    if name == "farthest":
                        target = scal[4]
                        wanted = target >= 0
                    else:
                        below = scal[3] if name == "near" else 1 - scal[3]
                        target = below * (rows + 1)
                        wanted = jnp.where(below == 1, scal[6], scal[5]) == 1

                    @pl.when(wanted)
                    def _(field=field, target=target, back=back, slot=slot):
                        held[field, target] = back[slot]

    @pl.when(step == 0)
    def _():
        for at, groups in enumerate(plan.roles):
            pl.when(scal[2] == at)(functools.partial(inverse, at, groups))
        for side, line in enumerate((top, bottom)):

            @pl.when(scal[5 + side] == 0)
            def _(side=side, line=line):
                for field in range(FIELDS):
                    held[field, side * (rows + 1), :, :width] = line[field]

    base = step * step_rows
    tail = width % LANES

    @pl.when(step < last_step)
    def _():
        lane = lax.broadcasted_iota(jnp.int32, (levels, LANES), 1)

        def load(row, _):
            at = row - base
            for field in range(FIELDS):
                held[field, row + 1, :, :width] = (
                    wind[field, at] if field < 2 else (theta, thick)[field - 2][at]
                )
                beyond = jnp.where(
                    lane == tail,
                    pltpu.roll(east[field], (tail + LANES - row) & (LANES - 1), 1),
                    pltpu.roll(west[field], (2 * LANES - 1 - row) & (LANES - 1), 1),
                )
                held[field, row + 1, :, width:] = beyond[:, tail:]
            return 0

        lax.fori_loop(jnp.maximum(base, scal[7]), jnp.minimum(base + step_rows, scal[8]), load, 0)

    count = wide // LANES
    lane = lax.broadcasted_iota(jnp.int32, (8, LANES), 1)
    is_first, is_last = lane == 0, lane == LANES - 1

    def diff_lon(pieces):
        up = [pltpu.roll(piece, LANES - 1, 1) for piece in pieces]
        down = [pltpu.roll(piece, 1, 1) for piece in pieces]
        return [
            jnp.where(is_last, up[(k + 1) % count], up[k]) - jnp.where(is_first, down[k - 1], down[k])
            for k in range(count)
        ]

    def stencil(row, _):
        at = base - step_rows + row
        along, across, push, turn, cos_north, cos_south = [coef[k * rows + at] for k in range(6)]
        across_north, across_south = across * cos_north, across * cos_south
        for part in range(levels // 8):
            some = pl.ds(part * 8, 8)

            def line(field, shift):
                return [held[field, at + shift, some, k * LANES : (k + 1) * LANES] for k in range(count)]

            def put(ref, lead, pieces):
                for k, piece in enumerate(pieces):
                    stop = min(width, (k + 1) * LANES)
                    ref[(*lead, row, some, slice(k * LANES, stop))] = piece[:, : stop - k * LANES]

            each = range(count)
            u, v, h = line(0, 1), line(1, 1), line(3, 1)
            advect = [along * u[k] for k in each]
            carry = [0.1 * v[k] for k in each]
            v_n, v_s, h_n, h_s = line(1, 0), line(1, 2), line(3, 0), line(3, 2)
            d_uh, d_h = diff_lon([u[k] * h[k] for k in each]), diff_lon(h)
            put(
                new_thick,
                (),
                [
                    h[k]
                    - along * d_uh[k]
                    - (across_south * (v_s[k] * h_s[k]) - across_north * (v_n[k] * h_n[k]))
                    for k in each
                ],
            )
            d_v = diff_lon(v)
            put(
                new_wind,
                (1,),
                [
                    v[k]
                    - advect[k] * d_v[k]
                    - carry[k] * (v_s[k] - v_n[k])
                    - 0.15 * (h_s[k] - h_n[k])
                    - turn * u[k]
                    for k in each
                ],
            )
            d_u, u_n, u_s = diff_lon(u), line(0, 0), line(0, 2)
            put(
                new_wind,
                (0,),
                [
                    u[k]
                    - advect[k] * d_u[k]
                    - carry[k] * (u_s[k] - u_n[k])
                    - push * d_h[k]
                    + turn * v[k]
                    for k in each
                ],
            )
            t, t_n, t_s = line(2, 1), line(2, 0), line(2, 2)
            d_t = diff_lon(t)
            put(
                new_theta,
                (),
                [t[k] - advect[k] * d_t[k] - carry[k] * (t_s[k] - t_n[k]) for k in each],
            )
        return 0

    @pl.when(step > 0)
    def _():
        lax.fori_loop(0, step_rows, stencil, 0)


def substep(plan, step_rows, scal, coef, winds, theta, thick, west, east, top, bottom, cuts, tabs, spectra):
    rows, width, levels = plan.rows, plan.width, plan.levels
    once = pl.Buffered(1)
    steps = rows // step_rows

    def block(i, s):
        return jnp.clip(i, s[9], s[10])

    def whole(shape):
        return pl.BlockSpec(shape, lambda i, s: (0,) * len(shape), pipeline_mode=once)

    table = pl.BlockSpec((1, plan.table, plan.wide), lambda i, s: (s[1], 0, 0), pipeline_mode=once)
    anywhere = pl.BlockSpec(memory_space=pl.ANY)
    edge, halo = (FIELDS, levels, LANES), (FIELDS, levels, width)
    in_specs = [
        pl.BlockSpec(memory_space=pltpu.SMEM),
        pl.BlockSpec((2, step_rows, levels, width), lambda i, s: (0, block(i, s), 0, 0)),
        pl.BlockSpec((step_rows, levels, width), lambda i, s: (block(i, s), 0, 0)),
        pl.BlockSpec((step_rows, levels, width), lambda i, s: (block(i, s), 0, 0)),
        whole(edge),
        whole(edge),
        whole(halo),
        whole(halo),
        whole((plan.slots * levels, LANES)),
        table,
        table,
    ] + [anywhere] * len(spectra)
    shapes = [(2, rows, levels, width)] + [(rows, levels, width)] * 2
    most = max(sum(group.total for group in groups) for groups in plan.roles)
    return pl.pallas_call(
        functools.partial(step_kernel, plan, step_rows),
        grid_spec=pltpu.PrefetchScalarGridSpec(
            num_scalar_prefetch=1,
            grid=(steps + 1,),
            in_specs=in_specs,
            out_specs=[
                pl.BlockSpec((2, step_rows, levels, width), lambda i, s: (0, jnp.maximum(i - 1, 0), 0, 0)),
                pl.BlockSpec((step_rows, levels, width), lambda i, s: (jnp.maximum(i - 1, 0), 0, 0)),
                pl.BlockSpec((step_rows, levels, width), lambda i, s: (jnp.maximum(i - 1, 0), 0, 0)),
            ],
            scratch_shapes=[
                pltpu.VMEM((FIELDS, rows + 2, levels, plan.wide), jnp.float32),
                pltpu.VMEM((FIELDS, most, LANES), jnp.float32),
                pltpu.SemaphoreType.DMA((max(len(groups) for groups in plan.roles), FIELDS)),
            ],
        ),
        out_shape=[jax.ShapeDtypeStruct(shape, jnp.float32) for shape in shapes],
        compiler_params=pltpu.CompilerParams(vmem_limit_bytes=VMEM),
        cost_estimate=pl.CostEstimate(
            flops=6 * most * FIELDS * LANES * plan.wide, bytes_accessed=40_000_000, transcendentals=0
        ),
        name="inverse_and_substep",
    )(scal, coef, winds, theta, thick, west, east, top, bottom, cuts, *tabs, *spectra)


def lon_swap(plan, value, blocks, bit):
    pairs = [
        (block * plan.lon + place, block * plan.lon + (place ^ (1 << bit)))
        for block in blocks
        for place in range(plan.lon)
    ]
    return lax.ppermute(value, ("lat", "lon"), pairs)


def lat_move(plan, value, sources, targets):
    pairs = [
        (source * plan.lon + place, target * plan.lon + place)
        for source, target in zip(sources, targets)
        for place in range(plan.lon)
    ]
    return lax.ppermute(value, ("lat", "lon"), pairs)


def spread(plan, blocks, slots, order):
    for bit in reversed(order):
        for s in sorted(slots):
            slots[s | (1 << bit)] = lon_swap(plan, slots[s], blocks, bit)
    return slots


def gather_sums(plan, blocks, slots, order):
    slots = dict(slots)
    for bit in order:
        sent = [s for s in slots if s >> bit & 1]
        for s in sorted(sent, key=lambda s: -bin(s).count("1")):
            slots[s ^ (1 << bit)] = slots[s ^ (1 << bit)] + lon_swap(plan, slots.pop(s), blocks, bit)
    return spread(plan, blocks, slots, order)


def field_sets(plan):
    sent, kept = [], []
    for at in range(len(plan.roles)):
        bit = at % 2
        sent.append([u for u in range(FIELDS) if u >> bit & 1])
        kept.append([u for u in range(FIELDS) if not u >> bit & 1])
    return sent, kept


def parcel_sums(plan, place, at, blocks, sent, kept):
    first, second = field_sets(plan)
    parts, own = plan.parts, place % plan.parts
    if parts == 1:
        near, far = at % 2, 1 - at % 2
        moved = lon_swap(plan, sent, blocks, near)
        send = kept[1] + moved[1]
        slots = {0: (kept[0] + moved[0]) + lon_swap(plan, send, blocks, far)}
        slots = spread(plan, blocks, slots, [near, far])
        return [slots[u] for u in range(FIELDS)]
    bits = plan.lon.bit_length() - 1
    slots = {}
    for us, array in ((first[at], sent), (second[at], kept)):
        for i, u in enumerate(us):
            pieces = array[i].reshape(parts, -1, LANES)
            for k in range(parts):
                slots[u * parts + k] = pieces[k ^ own]
    order = list(range(bits)) if at % 2 == 0 else list(reversed(range(bits)))
    slots = gather_sums(plan, blocks, slots, order)
    result = []
    for u in range(FIELDS):
        pieces = jnp.stack([slots[u * parts + k] for k in range(parts)])
        result.append(pieces[jnp.arange(parts) ^ own].reshape(-1, LANES))
    return result


def all_sums(plan, place, sent, kept):
    result, number = [], 0
    for at in range(len(plan.roles)):
        home = plan.blocks(at)
        for k in range(len(plan.parcels(at))):
            first, second = sent[number], kept[number]
            number += 1
            if k == 0:
                result += parcel_sums(plan, place, at, home, first, second)
                continue
            helpers = plan.blocks(at + len(plan.roles))
            first, second = [lat_move(plan, array, home, helpers) for array in (first, second)]
            sums = parcel_sums(plan, place, at, helpers, first, second)
            result += [lat_move(plan, array, helpers, home) for array in sums]
    return result


def body(winds, theta, thick, polar_rows, cutoffs):
    lat, lon = lax.axis_size("lat"), lax.axis_size("lon")
    levels, rows, width = theta.shape
    sizes = (lat, lon, levels, rows, width, polar_rows.shape[0])
    plan = Plan(*sizes)
    t_tabs, i_tabs = [tuple(jnp.asarray(part) for part in pair) for pair in tables(sizes)]
    block, place = lax.axis_index("lat"), lax.axis_index("lon")
    winds = winds.transpose(0, 2, 1, 3)
    theta = theta.transpose(1, 0, 2)
    thick = thick.transpose(1, 0, 2)
    hemi = (block >= lat // 2).astype(jnp.int32)
    role = jnp.where(hemi == 1, lat - 1 - block, block)

    def line(row):
        return jnp.stack([winds[0, row], winds[1, row], theta[row], thick[row]])

    south_pairs = [(b * lon + p, (b + 1) * lon + p) for b in range(lat - 1) for p in range(lon)]
    north_pairs = [(to, at) for at, to in south_pairs]
    top = lax.ppermute(line(rows - 1), ("lat", "lon"), south_pairs)
    bottom = lax.ppermute(line(0), ("lat", "lon"), north_pairs)

    step_rows = max(k for k in range(1, 16) if rows % k == 0)
    listed = polar_rows.shape[0]
    north_run = jnp.sum((polar_rows < plan.total_rows // 2).astype(jnp.int32))
    south_first = plan.total_rows - listed + north_run
    far_row = jnp.where(hemi == 1, south_first, north_run - 1)
    far_at = far_row - block * rows + 1
    far_at = jnp.where((far_at >= 0) & (far_at <= rows + 1), far_at, -1)
    raw_from = jnp.clip(north_run - block * rows, 0, rows)
    raw_to = jnp.clip(south_first - block * rows, 0, rows)
    block_from = jnp.minimum(raw_from, rows - 1) // step_rows
    block_to = jnp.maximum(block_from, jnp.maximum(raw_to - 1, 0) // step_rows)
    above, below = block * rows - 1, (block + 1) * rows

    def is_listed(row):
        return (row >= 0) & (row < plan.total_rows) & ((row < north_run) | (row >= south_first))

    facts = [
        place // plan.parts, place, role, hemi, far_at, is_listed(above), is_listed(below),
        raw_from, raw_to, block_from, block_to,
    ]
    scal = jnp.stack([jnp.asarray(fact).astype(jnp.int32) for fact in facts])

    first, second = field_sets(plan)
    sent = forward(plan, first, scal, winds, theta, thick, top, bottom, t_tabs)
    kept = forward(plan, second, scal, winds, theta, thick, top, bottom, t_tabs)
    sums = all_sums(plan, place, sent, kept)

    first_edge, last_edge = edges(plan, winds, theta, thick)
    west = lax.ppermute(last_edge, "lon", [(i, (i + 1) % lon) for i in range(lon)])
    east = lax.ppermute(first_edge, "lon", [((i + 1) % lon, i) for i in range(lon)])

    slot_rows = jnp.asarray(plan.slot_rows())[jnp.minimum(role, len(plan.roles) - 1), hemi]
    slot_rows = jnp.where(slot_rows == -2, far_at, slot_rows)
    hits = (polar_rows[None, :] == (slot_rows - 1 + block * rows)[:, None]) & (slot_rows >= 0)[:, None]
    cut = jnp.sum(jnp.where(hits, cutoffs[None, :] + 1, 0), axis=1) - 1
    cuts = jnp.broadcast_to(cut.astype(jnp.int32)[:, None, None], (plan.slots, levels, LANES))
    cuts = cuts.reshape(plan.slots * levels, LANES)

    ring = block * rows - 1 + jnp.arange(rows + 2, dtype=jnp.int32)
    centre = (ring.astype(jnp.float32) + 0.5) * (jnp.pi / plan.total_rows)
    cos, sin = jnp.sin(centre), -jnp.cos(centre)
    mid = cos[1:-1]
    coef = jnp.concatenate([0.025 / mid, 0.1 / mid, 0.05 / mid, 0.3 * sin[1:-1], cos[:-2], cos[2:]])

    out = substep(
        plan, step_rows, scal, coef, winds, theta, thick, west, east, top, bottom, cuts, i_tabs, sums
    )
    return (out[0].transpose(0, 2, 1, 3), out[1].transpose(1, 0, 2), out[2].transpose(1, 0, 2))


def solution(mesh):
    in_specs = (P(None, None, "lat", "lon"), P(None, "lat", "lon"), P(None, "lat", "lon"), P(), P())
    out_specs = (P(None, None, "lat", "lon"), P(None, "lat", "lon"), P(None, "lat", "lon"))
    return jax.shard_map(body, mesh=mesh, in_specs=in_specs, out_specs=out_specs, check_vma=False)
```

```python
import functools

import jax
import jax.numpy as jnp
import ml_dtypes
import numpy as np
from jax import lax
from jax.experimental import pallas as pl
from jax.experimental.pallas import tpu as pltpu
from jax.sharding import PartitionSpec as P

FIELDS = 4
LANES = 128
PIECE = 3
VMEM = 60 * 1024 * 1024


def round_up(value, step):
    return -(-value // step) * step


class Group:
    def __init__(self, first, stop, extras, blocks, levels):
        self.first, self.stop, self.extras, self.blocks = first, stop, extras, blocks
        self.own = stop - first
        self.slots = self.own + len(extras)
        self.height = self.slots * levels
        self.total = self.height * blocks


class Plan:
    def __init__(self, lat, lon, levels, rows, width, listed):
        self.lat, self.lon, self.levels, self.rows, self.width = lat, lon, levels, rows, width
        self.total_rows, self.length = lat * rows, lon * width
        self.parts = lon // FIELDS
        self.wide = round_up(width + 2, LANES)
        pole = listed // 2
        self.high = pole + pole // 4
        top = self.length // 4 - 1

        def blocks_of(depth):
            return -(-(2 * min(2 * (depth + 1), top) + 1) // LANES)

        self.roles = []
        last = self.high - 2
        for role in range(lat // 2):
            start = role * rows
            if start - 1 > last:
                break
            need = {}
            for depth in range(start, min(start + rows - 1, last) + 1):
                need.setdefault(blocks_of(depth), []).append(depth - start)
            extras = {}
            if role > 0:
                extras.setdefault(blocks_of(start - 1), []).append("near")
            if start + rows <= last:
                extras.setdefault(blocks_of(start + rows), []).append("far")
            groups = []
            for blocks in sorted(set(need) | set(extras)):
                own = need.get(blocks, [0, -1])
                groups.append(
                    Group(own[0], own[-1] + 1 if blocks in need else 0, extras.get(blocks, []), blocks, levels)
                )
            groups.append(Group(0, 0, ["farthest"], -(-(2 * top + 1) // LANES), levels))
            self.roles.append(groups)
        self.slots = max(sum(group.slots for group in groups) for groups in self.roles)
        self.table = LANES * max(group.blocks for groups in self.roles for group in groups)
        count = len(self.roles)
        self.lent = {}
        if self.parts == 1 and 2 * count <= lat // 2:
            self.lent = {count - 1: len(self.roles[-1]) - 2}

    def blocks(self, role):
        return (role, self.lat - 1 - role)

    def parcels(self, at):
        indices = range(len(self.roles[at]))
        away = self.lent.get(at)
        home = [g for g in indices if g != away]
        return [home] if away is None else [home, [away]]

    def places(self):
        result, number = {}, 0
        for at in range(len(self.roles)):
            for parcel in self.parcels(at):
                offset = 0
                for g in parcel:
                    result[at, g] = (number, offset)
                    offset += self.roles[at][g].total
                number += 1
        return result

    def heights(self):
        return [
            sum(self.roles[at][g].total for g in parcel)
            for at in range(len(self.roles))
            for parcel in self.parcels(at)
        ]

    def slot_rows(self):
        table = np.full((len(self.roles), 2, self.slots), -1, np.int32)
        for at, groups in enumerate(self.roles):
            for hemi in range(2):
                rows = []
                for group in groups:
                    first = group.first if hemi == 0 else self.rows - group.stop
                    rows += [first + 1 + k for k in range(group.own)]
                    ends = (0, self.rows + 1) if hemi == 0 else (self.rows + 1, 0)
                    rows += [{"near": ends[0], "far": ends[1], "farthest": -2}[name] for name in group.extras]
                table[at, hemi, : len(rows)] = rows
        return table


def split_table(table):
    high = table.astype(ml_dtypes.bfloat16)
    low = (table - high.astype(np.float64)).astype(ml_dtypes.bfloat16)
    return high, low


@functools.lru_cache(maxsize=None)
def tables(sizes):
    plan = Plan(*sizes)
    index = np.arange(plan.table)
    wave, odd = (index + 1) // 2, (index % 2 == 0) & (index > 0)
    used = wave < plan.length // 4
    points = np.zeros(plan.wide, np.int64)
    points[: plan.width + 1] = np.arange(plan.width + 1)
    points[-1] = -1
    shown = np.zeros(plan.wide, bool)
    shown[: plan.width + 1] = True
    shown[-1] = True

    def trig(at):
        angle = (wave[:, None] * at[None, :]) % plan.length * (2.0 * np.pi / plan.length)
        return np.where(odd[:, None], np.sin(angle), np.cos(angle)) * used[:, None]

    weight = np.where(wave == 0, 1.0, 2.0) / plan.length
    forward, inverse = [], []
    for place in range(plan.lon):
        forward.append(trig(place * plan.width + np.arange(plan.width)).T)
        inverse.append(trig(place * plan.width + points) * weight[:, None] * shown[None, :])
    shape = (plan.lon, plan.width, plan.table // LANES, LANES)
    forward = np.stack(forward).reshape(shape).transpose(0, 2, 1, 3)
    inverse = np.stack(inverse).reshape(plan.lon, plan.table // LANES, LANES, plan.wide)
    return split_table(forward), split_table(inverse)


def fetch_table(place, tabs, held, sems, blocks):
    return [
        pltpu.make_async_copy(tab.at[place, b], held.at[half, b], sems.at[half, b])
        for b in blocks
        for half, tab in enumerate(tabs)
    ]


def split(value):
    high = value.astype(jnp.bfloat16)
    low = (value - high.astype(jnp.float32)).astype(jnp.bfloat16)
    return high, low


def three_pass(left, right):
    total = jnp.dot(left[0], right[0], preferred_element_type=jnp.float32)
    total += jnp.dot(left[0], right[1], preferred_element_type=jnp.float32)
    total += jnp.dot(left[1], right[0], preferred_element_type=jnp.float32)
    return total


def forward_kernel(plan, sets, scal, winds, theta, thick, top, bottom, t_high, t_low, *refs):
    places, heights = plan.places(), plan.heights()
    outs, (points, spectra, held, in_sems, out_sems, t_sems) = refs[: len(heights)], refs[len(heights) :]
    levels, width = plan.levels, plan.width
    deep = points.shape[0]
    for at, groups in enumerate(plan.roles):

        @pl.when(scal[2] == at)
        def _(at=at, groups=groups):
            order = sorted(range(len(groups)), key=lambda g: groups[g].blocks)
            ready = 0
            units = [(g, i, u) for g in order for i, u in enumerate(sets[at])]

            def first_row(group):
                if "farthest" in group.extras:
                    return jnp.clip(scal[4] - 1, 0, plan.rows - 1), 1
                return jnp.where(scal[3] == 1, plan.rows - group.stop, group.first), group.own

            def fetch(n):
                g, _, u = units[n]
                first, count = first_row(groups[g])
                field = u ^ scal[0]

                def pieces(source):
                    for k in range(0, count, PIECE):
                        size = min(PIECE, count - k)
                        pltpu.make_async_copy(
                            source.at[pl.ds(first + k, size)],
                            points.at[n % deep, pl.ds(k, size)],
                            in_sems.at[n % deep],
                        ).start()

                pl.when(field < 2)(lambda: pieces(winds.at[jnp.minimum(field, 1)]))
                pl.when(field == 2)(lambda: pieces(theta))
                pl.when(field == 3)(lambda: pieces(thick))

            def arrive(n):
                first, count = first_row(groups[units[n][0]])
                pltpu.make_async_copy(
                    theta.at[pl.ds(first, count)], points.at[n % deep, pl.ds(0, count)], in_sems.at[n % deep]
                ).wait()

            def leave(n, parts):
                g, i, _ = units[n]
                number, offset = places[at, g]
                size = groups[g].total // parts
                return [
                    pltpu.make_async_copy(
                        spectra.at[n % 2, pl.ds(k * size, size)],
                        outs[number].at[i, pl.ds(offset + k * size, size)],
                        out_sems.at[n % 2],
                    )
                    for k in range(parts)
                ]

            for n in range(deep - 1):
                fetch(n)
            for copy in fetch_table(scal[1], (t_high, t_low), held, t_sems, range(plan.table // LANES)):
                copy.start()
            for n, (g, i, u) in enumerate(units):
                group = groups[g]
                if n + deep - 1 < len(units):
                    fetch(n + deep - 1)
                arrive(n)
                for copy in fetch_table(scal[1], (t_high, t_low), held, t_sems, range(ready, group.blocks)):
                    copy.wait()
                ready = max(ready, group.blocks)
                field = u ^ scal[0]
                for k, name in enumerate(group.extras):
                    slot = group.own + k
                    if name == "farthest":
                        from_top, from_bottom = scal[4] == 0, scal[4] == plan.rows + 1
                        slot = 0
                    else:
                        from_top = scal[3] == (0 if name == "near" else 1)
                        from_bottom = jnp.logical_not(from_top)

                    @pl.when(from_top)
                    def _(slot=slot, n=n):
                        points[n % deep, slot] = top[field]

                    @pl.when(from_bottom)
                    def _(slot=slot, n=n):
                        points[n % deep, slot] = bottom[field]

                spec = three_pass(
                    split(points[n % deep, : group.slots].reshape(group.height, width)),
                    [jnp.concatenate([held[half, b] for b in range(group.blocks)], axis=1) for half in range(2)],
                )
                if n >= 2:
                    leave(n - 2, 1)[0].wait()
                for b in range(group.blocks):
                    spectra[n % 2, b * group.height : (b + 1) * group.height, :] = spec[
                        :, b * LANES : (b + 1) * LANES
                    ]
                for copy in leave(n, group.blocks):
                    copy.start()
            for n in range(max(0, len(units) - 2), len(units)):
                leave(n, 1)[0].wait()


def forward(plan, sets, scal, winds, theta, thick, top, bottom, tabs):
    count = len(sets[0])
    anywhere = pl.BlockSpec(memory_space=pl.ANY)
    halo = pl.BlockSpec((FIELDS, plan.levels, plan.width), lambda i, s: (0, 0, 0))
    heights = plan.heights()
    slots = max(group.slots for groups in plan.roles for group in groups)
    total = max(group.total for groups in plan.roles for group in groups)
    return pl.pallas_call(
        functools.partial(forward_kernel, plan, sets),
        grid_spec=pltpu.PrefetchScalarGridSpec(
            num_scalar_prefetch=1,
            grid=(1,),
            in_specs=[anywhere] * 3 + [halo, halo, anywhere, anywhere],
            out_specs=[anywhere] * len(heights),
            scratch_shapes=[
                pltpu.VMEM((3, slots, plan.levels, plan.width), jnp.float32),
                pltpu.VMEM((2, total, LANES), jnp.float32),
                pltpu.VMEM((2, plan.table // LANES, plan.width, LANES), jnp.bfloat16),
                pltpu.SemaphoreType.DMA((3,)),
                pltpu.SemaphoreType.DMA((2,)),
                pltpu.SemaphoreType.DMA((2, plan.table // LANES)),
            ],
        ),
        out_shape=[jax.ShapeDtypeStruct((count, height, LANES), jnp.float32) for height in heights],
        compiler_params=pltpu.CompilerParams(vmem_limit_bytes=VMEM),
        cost_estimate=pl.CostEstimate(
            flops=6 * max(heights) * count * LANES * plan.width, bytes_accessed=15_000_000, transcendentals=0
        ),
        name="partial_spectra",
    )(scal, winds, theta, thick, top, bottom, *tabs)


def edge_kernel(plan, count, _, *refs):
    ins, outs = refs[:-2], refs[-2:]
    lane = lax.broadcasted_iota(jnp.int32, (plan.levels, LANES), 1)
    some = plan.rows // count
    for side, column in enumerate((0, (plan.width - 1) % LANES)):
        kept = (jnp.zeros((plan.levels, LANES), jnp.float32),) * FIELDS
        for piece in range(count):
            at = (side * count + piece) * FIELDS
            fields = ins[at : at + FIELDS]

            def pick(row, kept, fields=fields, piece=piece, column=column):
                values = (fields[0][0, row], fields[1][0, row], fields[2][row], fields[3][row])
                return tuple(
                    jnp.where(lane == row + piece * some, value[:, column : column + 1], old)
                    for value, old in zip(values, kept)
                )

            kept = lax.fori_loop(0, some, pick, kept)
        for field in range(FIELDS):
            outs[side][field] = kept[field]


def edges(plan, after, winds, theta, thick):
    count = 3 if plan.rows % 3 == 0 else 1
    some = plan.rows // count
    specs = []
    for at in (0, (plan.width - 1) // LANES):
        for piece in range(count):
            for wind in range(2):
                specs.append(
                    pl.BlockSpec(
                        (1, some, plan.levels, LANES), lambda i, w=wind, p=piece, at=at: (w, p, 0, at)
                    )
                )
            specs += [pl.BlockSpec((some, plan.levels, LANES), lambda i, p=piece, at=at: (p, 0, at))] * 2
    shape = (FIELDS, plan.levels, LANES)
    return pl.pallas_call(
        functools.partial(edge_kernel, plan, count),
        grid=(1,),
        in_specs=[pl.BlockSpec(memory_space=pl.ANY)] + specs,
        out_specs=[pl.BlockSpec(shape, lambda i: (0, 0, 0))] * 2,
        out_shape=[jax.ShapeDtypeStruct(shape, jnp.float32)] * 2,
        compiler_params=pltpu.CompilerParams(vmem_limit_bytes=VMEM),
        cost_estimate=pl.CostEstimate(flops=0, bytes_accessed=6_000_000, transcendentals=0),
        name="edge_columns",
    )(after, *[winds, winds, theta, thick] * (2 * count))


def step_kernel(plan, step_rows, scal, coef, west, east, top, bottom, cuts, i_high, i_low, *refs):
    places, heights = plan.places(), plan.heights()
    halves = plan.levels // 8
    raw, refs = refs[: FIELDS * halves], refs[FIELDS * halves :]
    spectra = refs[: FIELDS * len(heights)]
    new_wind, new_theta, new_thick, held, sums, table, ready, sems, t_sems, out_sems = refs[FIELDS * len(heights) :]
    step = pl.program_id(0)
    rows, width, wide, levels = plan.rows, plan.width, plan.wide, plan.levels
    last_step = rows // step_rows

    def inverse(at, groups):
        slot_at = np.cumsum([0] + [group.slots for group in groups])
        row_at = np.cumsum([0] + [group.total for group in groups])

        def copies(g):
            number, offset = places[at, g]
            return [
                pltpu.make_async_copy(
                    spectra[number * FIELDS + u].at[pl.ds(offset, groups[g].total)],
                    sums.at[u, pl.ds(int(row_at[g]), groups[g].total)],
                    sems.at[g, u],
                )
                for u in range(FIELDS)
            ]

        have = 0
        for g, group in enumerate(groups):
            for copy in copies(g):
                copy.start()
            for copy in fetch_table(scal[1], (i_high, i_low), table, t_sems, range(have, group.blocks)):
                copy.start()
            have = max(have, group.blocks)
        have = 0
        for g, group in enumerate(groups):
            for copy in copies(g):
                copy.wait()
            for copy in fetch_table(scal[1], (i_high, i_low), table, t_sems, range(have, group.blocks)):
                copy.wait()
            have = max(have, group.blocks)
            height, lanes = group.height, group.blocks * LANES
            from_row = int(slot_at[g]) * levels
            cut = cuts[from_row : from_row + height, :]
            lane = lax.broadcasted_iota(jnp.int32, (height, LANES), 1)
            for u in range(FIELDS):
                spec = jnp.concatenate(
                    [
                        jnp.where(
                            lax.shift_right_logical(lane + (b * LANES + 1), 1) <= cut,
                            sums[u, int(row_at[g]) + b * height : int(row_at[g]) + (b + 1) * height, :],
                            0.0,
                        )
                        for b in range(group.blocks)
                    ],
                    axis=1,
                )
                back = three_pass(
                    split(spec), [table[half, : group.blocks].reshape(lanes, wide) for half in range(2)]
                )
                back = back.reshape(group.slots, levels, wide)
                field = u ^ scal[0]
                if group.own:
                    first = jnp.where(scal[3] == 1, rows - group.stop, group.first) + 1
                    held[field, pl.ds(first, group.own)] = back[: group.own]
                for k, name in enumerate(group.extras):
                    slot = group.own + k
                    if name == "farthest":
                        target = scal[4]
                        wanted = target >= 0
                    else:
                        below = scal[3] if name == "near" else 1 - scal[3]
                        target = below * (rows + 1)
                        wanted = jnp.where(below == 1, scal[6], scal[5]) == 1

                    @pl.when(wanted)
                    def _(field=field, target=target, back=back, slot=slot):
                        held[field, target] = back[slot]

    @pl.when(step == 0)
    def _():
        for at, groups in enumerate(plan.roles):
            pl.when(scal[2] == at)(functools.partial(inverse, at, groups))
        for side, line in enumerate((top, bottom)):

            @pl.when(scal[5 + side] == 0)
            def _(side=side, line=line):
                for field in range(FIELDS):
                    held[field, side * (rows + 1), :, :width] = line[field]

    base = step * step_rows
    tail = width % LANES

    @pl.when(step < last_step)
    def _():
        lane = lax.broadcasted_iota(jnp.int32, (levels, LANES), 1)

        def load(row, _):
            at = row - base
            for field in range(FIELDS):
                for half in range(halves):
                    piece = raw[field * halves + half]
                    held[field, row + 1, half * 8 : half * 8 + 8, :width] = piece[0, at] if field < 2 else piece[at]
                beyond = jnp.where(
                    lane == tail,
                    pltpu.roll(east[field], (tail + LANES - row) & (LANES - 1), 1),
                    pltpu.roll(west[field], (2 * LANES - 1 - row) & (LANES - 1), 1),
                )
                held[field, row + 1, :, width:] = beyond[:, tail:]
            return 0

        lax.fori_loop(jnp.maximum(base, scal[7]), jnp.minimum(base + step_rows, scal[8]), load, 0)

    slot = step % 2
    count = wide // LANES
    lane = lax.broadcasted_iota(jnp.int32, (8, LANES), 1)
    is_first, is_last = lane == 0, lane == LANES - 1

    def diff_lon(pieces):
        up = [pltpu.roll(piece, LANES - 1, 1) for piece in pieces]
        down = [pltpu.roll(piece, 1, 1) for piece in pieces]
        return [
            jnp.where(is_last, up[(k + 1) % count], up[k]) - jnp.where(is_first, down[k - 1], down[k])
            for k in range(count)
        ]

    def stencil(row, _):
        at = base - step_rows + row
        along, across, push, turn, cos_north, cos_south = [coef[k * rows + at] for k in range(6)]
        across_north, across_south = across * cos_north, across * cos_south
        for part in range(levels // 8):
            some = pl.ds(part * 8, 8)

            def line(field, shift):
                return [held[field, at + shift, some, k * LANES : (k + 1) * LANES] for k in range(count)]

            def put(field, pieces):
                for k, piece in enumerate(pieces):
                    stop = min(width, (k + 1) * LANES)
                    ready[slot, field, row, some, k * LANES : stop] = piece[:, : stop - k * LANES]

            each = range(count)
            u, v, h = line(0, 1), line(1, 1), line(3, 1)
            advect = [along * u[k] for k in each]
            carry = [0.1 * v[k] for k in each]
            v_n, v_s, h_n, h_s = line(1, 0), line(1, 2), line(3, 0), line(3, 2)
            d_uh, d_h = diff_lon([u[k] * h[k] for k in each]), diff_lon(h)
            put(
                3,
                [
                    h[k]
                    - along * d_uh[k]
                    - (across_south * (v_s[k] * h_s[k]) - across_north * (v_n[k] * h_n[k]))
                    for k in each
                ],
            )
            d_v = diff_lon(v)
            put(
                1,
                [
                    v[k]
                    - advect[k] * d_v[k]
                    - carry[k] * (v_s[k] - v_n[k])
                    - 0.15 * (h_s[k] - h_n[k])
                    - turn * u[k]
                    for k in each
                ],
            )
            d_u, u_n, u_s = diff_lon(u), line(0, 0), line(0, 2)
            put(
                0,
                [
                    u[k]
                    - advect[k] * d_u[k]
                    - carry[k] * (u_s[k] - u_n[k])
                    - push * d_h[k]
                    + turn * v[k]
                    for k in each
                ],
            )
            t, t_n, t_s = line(2, 1), line(2, 0), line(2, 2)
            d_t = diff_lon(t)
            put(
                2,
                [t[k] - advect[k] * d_t[k] - carry[k] * (t_s[k] - t_n[k]) for k in each],
            )
        return 0

    outs = (new_wind.at[0], new_wind.at[1], new_theta, new_thick)

    def leave(at_step, size, act):
        for field, out in enumerate(outs):
            for k in range(0, step_rows, size):
                act(
                    pltpu.make_async_copy(
                        ready.at[at_step % 2, field, pl.ds(k, size)],
                        out.at[pl.ds((at_step - 1) * step_rows + k, size)],
                        out_sems.at[at_step % 2, field],
                    )
                )

    @pl.when(step > 2)
    def _():
        leave(step - 2, step_rows, lambda copy: copy.wait())

    @pl.when(step > 0)
    def _():
        lax.fori_loop(0, step_rows, stencil, 0)
        leave(step, PIECE if step_rows % PIECE == 0 else step_rows, lambda copy: copy.start())

    @pl.when(step == last_step)
    def _():
        if last_step > 1:
            leave(step - 1, step_rows, lambda copy: copy.wait())
        leave(step, step_rows, lambda copy: copy.wait())


def substep(plan, step_rows, scal, coef, winds, theta, thick, west, east, top, bottom, cuts, tabs, spectra):
    rows, width, levels = plan.rows, plan.width, plan.levels
    once = pl.Buffered(1)
    steps = rows // step_rows

    def block(i, s):
        return jnp.clip(i, s[9], s[10])

    def whole(shape):
        return pl.BlockSpec(shape, lambda i, s: (0,) * len(shape), pipeline_mode=once)

    anywhere = pl.BlockSpec(memory_space=pl.ANY)
    halves = range(levels // 8)
    raw_specs = [
        pl.BlockSpec((1, step_rows, 8, width), lambda i, s, w=wind, h=half: (w, block(i, s), h, 0))
        for wind in range(2)
        for half in halves
    ] + [
        pl.BlockSpec((step_rows, 8, width), lambda i, s, h=half: (block(i, s), h, 0))
        for _ in range(2)
        for half in halves
    ]
    raw = [array for array in (winds, winds, theta, thick) for _ in halves]
    edge, halo = (FIELDS, levels, LANES), (FIELDS, levels, width)
    in_specs = [
        pl.BlockSpec(memory_space=pltpu.SMEM),
        whole(edge),
        whole(edge),
        whole(halo),
        whole(halo),
        whole((plan.slots * levels, LANES)),
        anywhere,
        anywhere,
    ] + raw_specs + [anywhere] * len(spectra)
    shapes = [(2, rows, levels, width)] + [(rows, levels, width)] * 2
    most = max(sum(group.total for group in groups) for groups in plan.roles)
    return pl.pallas_call(
        functools.partial(step_kernel, plan, step_rows),
        grid_spec=pltpu.PrefetchScalarGridSpec(
            num_scalar_prefetch=1,
            grid=(steps + 1,),
            in_specs=in_specs,
            out_specs=[anywhere] * 3,
            scratch_shapes=[
                pltpu.VMEM((FIELDS, rows + 2, levels, plan.wide), jnp.float32),
                pltpu.VMEM((FIELDS, most, LANES), jnp.float32),
                pltpu.VMEM((2, plan.table // LANES, LANES, plan.wide), jnp.bfloat16),
                pltpu.VMEM((2, FIELDS, step_rows, levels, width), jnp.float32),
                pltpu.SemaphoreType.DMA((max(len(groups) for groups in plan.roles), FIELDS)),
                pltpu.SemaphoreType.DMA((2, plan.table // LANES)),
                pltpu.SemaphoreType.DMA((2, FIELDS)),
            ],
        ),
        out_shape=[jax.ShapeDtypeStruct(shape, jnp.float32) for shape in shapes],
        compiler_params=pltpu.CompilerParams(vmem_limit_bytes=VMEM),
        cost_estimate=pl.CostEstimate(
            flops=6 * most * FIELDS * LANES * plan.wide, bytes_accessed=40_000_000, transcendentals=0
        ),
        name="inverse_and_substep",
    )(scal, coef, west, east, top, bottom, cuts, *tabs, *raw, *spectra)


def lon_swap(plan, value, blocks, bit):
    pairs = [
        (block * plan.lon + place, block * plan.lon + (place ^ (1 << bit)))
        for block in blocks
        for place in range(plan.lon)
    ]
    return lax.ppermute(value, ("lat", "lon"), pairs)


def lat_move(plan, value, sources, targets):
    pairs = [
        (source * plan.lon + place, target * plan.lon + place)
        for source, target in zip(sources, targets)
        for place in range(plan.lon)
    ]
    return lax.ppermute(value, ("lat", "lon"), pairs)


def spread(plan, blocks, slots, order):
    for bit in reversed(order):
        for s in sorted(slots):
            slots[s | (1 << bit)] = lon_swap(plan, slots[s], blocks, bit)
    return slots


def gather_sums(plan, blocks, slots, order):
    slots = dict(slots)
    for bit in order:
        sent = [s for s in slots if s >> bit & 1]
        for s in sorted(sent, key=lambda s: -bin(s).count("1")):
            slots[s ^ (1 << bit)] = slots[s ^ (1 << bit)] + lon_swap(plan, slots.pop(s), blocks, bit)
    return spread(plan, blocks, slots, order)


def field_sets(plan):
    sent, kept = [], []
    for at in range(len(plan.roles)):
        bit = at % 2
        sent.append([u for u in range(FIELDS) if u >> bit & 1])
        kept.append([u for u in range(FIELDS) if not u >> bit & 1])
    return sent, kept


def parcel_sums(plan, place, at, blocks, sent, kept):
    first, second = field_sets(plan)
    parts, own = plan.parts, place % plan.parts
    if parts == 1:
        near, far = at % 2, 1 - at % 2
        moved = lon_swap(plan, sent, blocks, near)
        send = kept[1] + moved[1]
        slots = {0: (kept[0] + moved[0]) + lon_swap(plan, send, blocks, far)}
        slots = spread(plan, blocks, slots, [near, far])
        return [slots[u] for u in range(FIELDS)]
    bits = plan.lon.bit_length() - 1
    slots = {}
    for us, array in ((first[at], sent), (second[at], kept)):
        for i, u in enumerate(us):
            pieces = array[i].reshape(parts, -1, LANES)
            for k in range(parts):
                slots[u * parts + k] = pieces[k ^ own]
    order = list(range(bits)) if at % 2 == 0 else list(reversed(range(bits)))
    slots = gather_sums(plan, blocks, slots, order)
    result = []
    for u in range(FIELDS):
        pieces = jnp.stack([slots[u * parts + k] for k in range(parts)])
        result.append(pieces[jnp.arange(parts) ^ own].reshape(-1, LANES))
    return result


def all_sums(plan, place, sent, kept):
    result, number = [], 0
    for at in range(len(plan.roles)):
        home = plan.blocks(at)
        for k in range(len(plan.parcels(at))):
            first, second = sent[number], kept[number]
            number += 1
            if k == 0:
                result += parcel_sums(plan, place, at, home, first, second)
                continue
            helpers = plan.blocks(at + len(plan.roles))
            first, second = [lat_move(plan, array, home, helpers) for array in (first, second)]
            sums = parcel_sums(plan, place, at, helpers, first, second)
            result += [lat_move(plan, array, helpers, home) for array in sums]
    return result


def body(winds, theta, thick, polar_rows, cutoffs):
    lat, lon = lax.axis_size("lat"), lax.axis_size("lon")
    levels, rows, width = theta.shape
    sizes = (lat, lon, levels, rows, width, polar_rows.shape[0])
    plan = Plan(*sizes)
    t_tabs, i_tabs = [tuple(jnp.asarray(part) for part in pair) for pair in tables(sizes)]
    block, place = lax.axis_index("lat"), lax.axis_index("lon")
    winds = winds.transpose(0, 2, 1, 3)
    theta = theta.transpose(1, 0, 2)
    thick = thick.transpose(1, 0, 2)
    hemi = (block >= lat // 2).astype(jnp.int32)
    role = jnp.where(hemi == 1, lat - 1 - block, block)

    def line(row):
        return jnp.stack([winds[0, row], winds[1, row], theta[row], thick[row]])

    south_pairs = [(b * lon + p, (b + 1) * lon + p) for b in range(lat - 1) for p in range(lon)]
    north_pairs = [(to, at) for at, to in south_pairs]
    top = lax.ppermute(line(rows - 1), ("lat", "lon"), south_pairs)
    bottom = lax.ppermute(line(0), ("lat", "lon"), north_pairs)

    step_rows = max(k for k in range(1, 16) if rows % k == 0)
    listed = polar_rows.shape[0]
    north_run = jnp.sum((polar_rows < plan.total_rows // 2).astype(jnp.int32))
    south_first = plan.total_rows - listed + north_run
    far_row = jnp.where(hemi == 1, south_first, north_run - 1)
    far_at = far_row - block * rows + 1
    far_at = jnp.where((far_at >= 0) & (far_at <= rows + 1), far_at, -1)
    raw_from = jnp.clip(north_run - block * rows, 0, rows)
    raw_to = jnp.clip(south_first - block * rows, 0, rows)
    block_from = jnp.minimum(raw_from, rows - 1) // step_rows
    block_to = jnp.maximum(block_from, jnp.maximum(raw_to - 1, 0) // step_rows)
    above, below = block * rows - 1, (block + 1) * rows

    def is_listed(row):
        return (row >= 0) & (row < plan.total_rows) & ((row < north_run) | (row >= south_first))

    facts = [
        place // plan.parts, place, role, hemi, far_at, is_listed(above), is_listed(below),
        raw_from, raw_to, block_from, block_to,
    ]
    scal = jnp.stack([jnp.asarray(fact).astype(jnp.int32) for fact in facts])

    first, second = field_sets(plan)
    sent = forward(plan, first, scal, winds, theta, thick, top, bottom, t_tabs)
    kept = forward(plan, second, scal, winds, theta, thick, top, bottom, t_tabs)
    first_edge, last_edge = edges(plan, kept[0], winds, theta, thick)
    west = lax.ppermute(last_edge, "lon", [(i, (i + 1) % lon) for i in range(lon)])
    east = lax.ppermute(first_edge, "lon", [((i + 1) % lon, i) for i in range(lon)])

    kept, west, east = lax.optimization_barrier((kept, west, east))
    sums = all_sums(plan, place, sent, kept)

    slot_rows = jnp.asarray(plan.slot_rows())[jnp.minimum(role, len(plan.roles) - 1), hemi]
    slot_rows = jnp.where(slot_rows == -2, far_at, slot_rows)
    hits = (polar_rows[None, :] == (slot_rows - 1 + block * rows)[:, None]) & (slot_rows >= 0)[:, None]
    cut = jnp.sum(jnp.where(hits, cutoffs[None, :] + 1, 0), axis=1) - 1
    cuts = jnp.broadcast_to(cut.astype(jnp.int32)[:, None, None], (plan.slots, levels, LANES))
    cuts = cuts.reshape(plan.slots * levels, LANES)

    ring = block * rows - 1 + jnp.arange(rows + 2, dtype=jnp.int32)
    centre = (ring.astype(jnp.float32) + 0.5) * (jnp.pi / plan.total_rows)
    cos, sin = jnp.sin(centre), -jnp.cos(centre)
    mid = cos[1:-1]
    coef = jnp.concatenate([0.025 / mid, 0.1 / mid, 0.05 / mid, 0.3 * sin[1:-1], cos[:-2], cos[2:]])

    out = substep(
        plan, step_rows, scal, coef, winds, theta, thick, west, east, top, bottom, cuts, i_tabs, sums
    )
    return (out[0].transpose(0, 2, 1, 3), out[1].transpose(1, 0, 2), out[2].transpose(1, 0, 2))


def solution(mesh):
    in_specs = (P(None, None, "lat", "lon"), P(None, "lat", "lon"), P(None, "lat", "lon"), P(), P())
    out_specs = (P(None, None, "lat", "lon"), P(None, "lat", "lon"), P(None, "lat", "lon"))
    return jax.shard_map(body, mesh=mesh, in_specs=in_specs, out_specs=out_specs, check_vma=False)
```

```python
import functools

import jax
import jax.numpy as jnp
import ml_dtypes
import numpy as np
from jax import lax
from jax.experimental import pallas as pl
from jax.experimental.pallas import tpu as pltpu
from jax.sharding import PartitionSpec as P

FIELDS = 4
LANES = 128
PIECE = 3
VMEM = 60 * 1024 * 1024


def round_up(value, step):
    return -(-value // step) * step


class Group:
    def __init__(self, first, stop, near, far, blocks, levels):
        self.first, self.stop, self.blocks = first, stop, blocks
        self.near, self.far = int(near), int(far)
        self.own = stop - first
        self.farthest = self.own == 0
        self.slots = 1 if self.farthest else self.own + self.near + self.far
        self.height = self.slots * levels
        self.total = self.height * blocks
        parts = max(1, round(self.slots / 16))
        self.chunk = -(-self.slots // parts)
        self.parts = -(-self.slots // self.chunk)

    def start(self, hemi, rows):
        return jnp.where(hemi == 1, rows - self.stop + 1 - self.far, self.first + 1 - self.near)

    def chunk_at(self, part):
        return jnp.minimum(part * self.chunk, self.slots - self.chunk)


class Plan:
    def __init__(self, lat, lon, levels, rows, width, listed):
        self.lat, self.lon, self.levels, self.rows, self.width = lat, lon, levels, rows, width
        self.total_rows, self.length = lat * rows, lon * width
        self.parts = lon // FIELDS
        self.wide = round_up(width + 2, LANES)
        pole = listed // 2
        self.high = pole + pole // 4
        top = self.length // 4 - 1

        def blocks_of(depth):
            return -(-(2 * min(2 * (depth + 1), top) + 1) // LANES)

        self.roles = []
        last = self.high - 2
        for role in range(lat // 2):
            start = role * rows
            if start > last:
                break
            need = {}
            for depth in range(start, min(start + rows - 1, last) + 1):
                need.setdefault(blocks_of(depth), []).append(depth - start)
            groups = [
                Group(need[k][0], need[k][-1] + 1, False, False, k, levels) for k in sorted(need)
            ]
            ends = groups[0], groups[-1]
            if role > 0:
                most = max(ends[0].blocks, blocks_of(start - 1))
                groups[0] = Group(ends[0].first, ends[0].stop, True, ends[0].far, most, levels)
            if start + rows <= last:
                most = max(groups[-1].blocks, blocks_of(start + rows))
                groups[-1] = Group(groups[-1].first, groups[-1].stop, groups[-1].near, True, most, levels)
            groups.append(Group(0, 0, False, False, -(-(2 * top + 1) // LANES), levels))
            self.roles.append(groups)
        self.slots = max(sum(group.slots for group in groups) for groups in self.roles)
        self.table = LANES * max(group.blocks for groups in self.roles for group in groups)
        count = len(self.roles)
        self.lent = {}
        if self.parts == 1 and 2 * count <= lat // 2:
            self.lent = {count - 1: len(self.roles[-1]) - 2}

    def blocks(self, role):
        return (role, self.lat - 1 - role)

    def parcels(self, at):
        indices = range(len(self.roles[at]))
        away = self.lent.get(at)
        home = [g for g in indices if g != away]
        return [home] if away is None else [home, [away]]

    def places(self):
        result, number = {}, 0
        for at in range(len(self.roles)):
            for parcel in self.parcels(at):
                offset = 0
                for g in parcel:
                    result[at, g] = (number, offset)
                    offset += self.roles[at][g].total
                number += 1
        return result

    def heights(self):
        return [
            sum(self.roles[at][g].total for g in parcel)
            for at in range(len(self.roles))
            for parcel in self.parcels(at)
        ]

    def slot_rows(self):
        table = np.full((len(self.roles), 2, self.slots), -1, np.int32)
        for at, groups in enumerate(self.roles):
            for hemi in range(2):
                rows = []
                for group in groups:
                    first = group.first + 1 - group.near if hemi == 0 else self.rows - group.stop + 1 - group.far
                    rows += [-2] if group.farthest else [first + k for k in range(group.slots)]
                table[at, hemi, : len(rows)] = rows
        return table


def split_table(table):
    high = table.astype(ml_dtypes.bfloat16)
    low = (table - high.astype(np.float64)).astype(ml_dtypes.bfloat16)
    return high, low


@functools.lru_cache(maxsize=None)
def tables(sizes):
    plan = Plan(*sizes)
    index = np.arange(plan.table)
    wave, odd = (index + 1) // 2, (index % 2 == 0) & (index > 0)
    used = wave < plan.length // 4
    points = np.zeros(plan.wide, np.int64)
    points[: plan.width + 1] = np.arange(plan.width + 1)
    points[-1] = -1
    shown = np.zeros(plan.wide, bool)
    shown[: plan.width + 1] = True
    shown[-1] = True

    def trig(at):
        angle = (wave[:, None] * at[None, :]) % plan.length * (2.0 * np.pi / plan.length)
        return np.where(odd[:, None], np.sin(angle), np.cos(angle)) * used[:, None]

    weight = np.where(wave == 0, 1.0, 2.0) / plan.length
    forward, inverse = [], []
    for place in range(plan.lon):
        forward.append(trig(place * plan.width + np.arange(plan.width)).T)
        inverse.append(trig(place * plan.width + points) * weight[:, None] * shown[None, :])
    shape = (plan.lon, plan.width, plan.table // LANES, LANES)
    forward = np.stack(forward).reshape(shape).transpose(0, 2, 1, 3)
    inverse = np.stack(inverse).reshape(plan.lon, plan.table // LANES, LANES, plan.wide)
    return split_table(forward), split_table(inverse)


def fetch_table(place, tabs, held, sems, blocks):
    return [
        pltpu.make_async_copy(tab.at[place, b], held.at[half, b], sems.at[half, b])
        for b in blocks
        for half, tab in enumerate(tabs)
    ]


def split(value):
    high = value.astype(jnp.bfloat16)
    low = (value - high.astype(jnp.float32)).astype(jnp.bfloat16)
    return high, low


def three_pass(left, right):
    total = jnp.dot(left[0], right[0], preferred_element_type=jnp.float32)
    total += jnp.dot(left[0], right[1], preferred_element_type=jnp.float32)
    total += jnp.dot(left[1], right[0], preferred_element_type=jnp.float32)
    return total


def forward_kernel(plan, sets, scal, winds, theta, thick, top, bottom, t_high, t_low, *refs):
    places, heights = plan.places(), plan.heights()
    outs, (points, spectra, held, in_sems, out_sems, t_sems) = refs[: len(heights)], refs[len(heights) :]
    levels, width = plan.levels, plan.width
    for at, groups in enumerate(plan.roles):

        @pl.when(scal[2] == at)
        def _(at=at, groups=groups):
            fields = [u ^ scal[0] for u in sets[at]]
            ready = 0

            def first_row(group):
                if group.farthest:
                    return jnp.clip(scal[4] - 1, 0, plan.rows - 1), 0, 1
                first = jnp.where(scal[3] == 1, plan.rows - group.stop, group.first)
                return first, jnp.where(scal[3] == 1, group.far, group.near), group.own

            def fetch(g):
                first, slot, count = first_row(groups[g])
                for i, field in enumerate(fields):

                    def pieces(source, i=i):
                        for k in range(0, count, PIECE):
                            size = min(PIECE, count - k)
                            pltpu.make_async_copy(
                                source.at[pl.ds(first + k, size)],
                                points.at[g % 2, i, pl.ds(slot + k, size)],
                                in_sems.at[g % 2, i],
                            ).start()

                    pl.when(field < 2)(lambda: pieces(winds.at[jnp.minimum(field, 1)]))
                    pl.when(field == 2)(lambda: pieces(theta))
                    pl.when(field == 3)(lambda: pieces(thick))

            def arrive(g):
                first, slot, count = first_row(groups[g])
                for i in range(len(fields)):
                    pltpu.make_async_copy(
                        theta.at[pl.ds(first, count)],
                        points.at[g % 2, i, pl.ds(slot, count)],
                        in_sems.at[g % 2, i],
                    ).wait()

            def leave(g, parts):
                number, offset = places[at, g]
                size = groups[g].total // parts
                return [
                    pltpu.make_async_copy(
                        spectra.at[g % 2, i, pl.ds(k * size, size)],
                        outs[number].at[i, pl.ds(offset + k * size, size)],
                        out_sems.at[g % 2, i],
                    )
                    for i in range(len(fields))
                    for k in range(parts)
                ]

            def halo(g, slot, line, wanted):
                @pl.when(wanted)
                def _():
                    for i, field in enumerate(fields):
                        points[g % 2, i, slot] = line[field]

            fetch(0)
            for copy in fetch_table(scal[1], (t_high, t_low), held, t_sems, range(plan.table // LANES)):
                copy.start()
            for g, group in enumerate(groups):
                if g + 1 < len(groups):
                    fetch(g + 1)
                arrive(g)
                for copy in fetch_table(scal[1], (t_high, t_low), held, t_sems, range(ready, group.blocks)):
                    copy.wait()
                ready = max(ready, group.blocks)
                if group.farthest:
                    halo(g, 0, top, scal[4] == 0)
                    halo(g, 0, bottom, scal[4] == plan.rows + 1)
                if group.near:
                    halo(g, 0, top, scal[3] == 0)
                    halo(g, group.slots - 1, bottom, scal[3] == 1)
                if group.far:
                    halo(g, group.slots - 1, bottom, scal[3] == 0)
                    halo(g, 0, top, scal[3] == 1)
                if g >= 2:
                    for copy in leave(g - 2, 1):
                        copy.wait()

                def transform(value, group=group):
                    return three_pass(
                        split(value),
                        [
                            jnp.concatenate([held[half, b] for b in range(group.blocks)], axis=1)
                            for half in range(2)
                        ],
                    )

                if group.farthest:
                    spec = transform(points[g % 2, :, 0].reshape(len(fields) * levels, width))
                    for i in range(len(fields)):
                        for b in range(group.blocks):
                            spectra[g % 2, i, b * levels : (b + 1) * levels, :] = spec[
                                i * levels : (i + 1) * levels, b * LANES : (b + 1) * LANES
                            ]
                else:

                    def part(n, _, g=g, group=group, transform=transform):
                        i, slot = n // group.parts, group.chunk_at(lax.rem(n, group.parts))
                        size = group.chunk * levels
                        spec = transform(points[g % 2, i, pl.ds(slot, group.chunk)].reshape(size, width))
                        for b in range(group.blocks):
                            target = pl.multiple_of(b * group.height + slot * levels, 8)
                            spectra[g % 2, i, pl.ds(target, size), :] = spec[:, b * LANES : (b + 1) * LANES]
                        return 0

                    lax.fori_loop(0, len(fields) * group.parts, part, 0)
                for copy in leave(g, group.blocks):
                    copy.start()
            for g in range(max(0, len(groups) - 2), len(groups)):
                for copy in leave(g, 1):
                    copy.wait()


def forward(plan, sets, scal, winds, theta, thick, top, bottom, tabs):
    count = len(sets[0])
    anywhere = pl.BlockSpec(memory_space=pl.ANY)
    halo = pl.BlockSpec((FIELDS, plan.levels, plan.width), lambda i, s: (0, 0, 0))
    heights = plan.heights()
    slots = max(group.slots for groups in plan.roles for group in groups)
    total = max(group.total for groups in plan.roles for group in groups)
    return pl.pallas_call(
        functools.partial(forward_kernel, plan, sets),
        grid_spec=pltpu.PrefetchScalarGridSpec(
            num_scalar_prefetch=1,
            grid=(1,),
            in_specs=[anywhere] * 3 + [halo, halo, anywhere, anywhere],
            out_specs=[anywhere] * len(heights),
            scratch_shapes=[
                pltpu.VMEM((2, count, slots, plan.levels, plan.width), jnp.float32),
                pltpu.VMEM((2, count, total, LANES), jnp.float32),
                pltpu.VMEM((2, plan.table // LANES, plan.width, LANES), jnp.bfloat16),
                pltpu.SemaphoreType.DMA((2, count)),
                pltpu.SemaphoreType.DMA((2, count)),
                pltpu.SemaphoreType.DMA((2, plan.table // LANES)),
            ],
        ),
        out_shape=[jax.ShapeDtypeStruct((count, height, LANES), jnp.float32) for height in heights],
        compiler_params=pltpu.CompilerParams(vmem_limit_bytes=VMEM),
        cost_estimate=pl.CostEstimate(
            flops=6 * max(heights) * count * LANES * plan.width, bytes_accessed=15_000_000, transcendentals=0
        ),
        name="partial_spectra",
    )(scal, winds, theta, thick, top, bottom, *tabs)


def edge_kernel(plan, count, *refs):
    ins, outs = refs[:-2], refs[-2:]
    lane = lax.broadcasted_iota(jnp.int32, (plan.levels, LANES), 1)
    some = plan.rows // count
    for side, column in enumerate((0, (plan.width - 1) % LANES)):
        kept = (jnp.zeros((plan.levels, LANES), jnp.float32),) * FIELDS
        for piece in range(count):
            at = (side * count + piece) * FIELDS
            fields = ins[at : at + FIELDS]

            def pick(row, kept, fields=fields, piece=piece, column=column):
                values = (fields[0][0, row], fields[1][0, row], fields[2][row], fields[3][row])
                return tuple(
                    jnp.where(lane == row + piece * some, value[:, column : column + 1], old)
                    for value, old in zip(values, kept)
                )

            kept = lax.fori_loop(0, some, pick, kept, unroll=max(k for k in range(1, 11) if some % k == 0))
        for field in range(FIELDS):
            outs[side][field] = kept[field]


def edges(plan, winds, theta, thick):
    count = 3 if plan.rows % 3 == 0 else 1
    some = plan.rows // count
    specs = []
    for at in (0, (plan.width - 1) // LANES):
        for piece in range(count):
            for wind in range(2):
                specs.append(
                    pl.BlockSpec(
                        (1, some, plan.levels, LANES), lambda i, w=wind, p=piece, at=at: (w, p, 0, at)
                    )
                )
            specs += [pl.BlockSpec((some, plan.levels, LANES), lambda i, p=piece, at=at: (p, 0, at))] * 2
    shape = (FIELDS, plan.levels, LANES)
    return pl.pallas_call(
        functools.partial(edge_kernel, plan, count),
        grid=(1,),
        in_specs=specs,
        out_specs=[pl.BlockSpec(shape, lambda i: (0, 0, 0))] * 2,
        out_shape=[jax.ShapeDtypeStruct(shape, jnp.float32)] * 2,
        compiler_params=pltpu.CompilerParams(vmem_limit_bytes=VMEM),
        cost_estimate=pl.CostEstimate(flops=0, bytes_accessed=6_000_000, transcendentals=0),
        name="edge_columns",
    )(*[winds, winds, theta, thick] * (2 * count))


def step_kernel(plan, step_rows, scal, coef, west, east, top, bottom, cuts, i_high, i_low, *refs):
    places, heights = plan.places(), plan.heights()
    halves = plan.levels // 8
    raw, refs = refs[: FIELDS * halves], refs[FIELDS * halves :]
    spectra = refs[: FIELDS * len(heights)]
    new_wind, new_theta, new_thick, held, sums, table, ready, sems, t_sems, out_sems = refs[FIELDS * len(heights) :]
    step = pl.program_id(0)
    rows, width, wide, levels = plan.rows, plan.width, plan.wide, plan.levels
    last_step = rows // step_rows

    def inverse(at, groups):
        slot_at = np.cumsum([0] + [group.slots for group in groups])
        row_at = np.cumsum([0] + [group.total for group in groups])

        def copies(g):
            number, offset = places[at, g]
            return [
                pltpu.make_async_copy(
                    spectra[number * FIELDS + u].at[pl.ds(offset, groups[g].total)],
                    sums.at[u, pl.ds(int(row_at[g]), groups[g].total)],
                    sems.at[g, u],
                )
                for u in range(FIELDS)
            ]

        have = 0
        for g, group in enumerate(groups):
            for copy in copies(g):
                copy.start()
            for copy in fetch_table(scal[1], (i_high, i_low), table, t_sems, range(have, group.blocks)):
                copy.start()
            have = max(have, group.blocks)
        have = 0
        for g, group in enumerate(groups):
            for copy in copies(g):
                copy.wait()
            for copy in fetch_table(scal[1], (i_high, i_low), table, t_sems, range(have, group.blocks)):
                copy.wait()
            have = max(have, group.blocks)
            lanes = group.blocks * LANES
            first_slot, first_sum = int(slot_at[g]), int(row_at[g])

            def back_of(spec, size, lanes=lanes, group=group):
                back = three_pass(
                    split(spec), [table[half, : group.blocks].reshape(lanes, wide) for half in range(2)]
                )
                return back.reshape(size, levels, wide)

            def masked(u, slot, size, group=group, first_slot=first_slot, first_sum=first_sum):
                rows_at = pl.ds(pl.multiple_of((first_slot + slot) * levels, 8), size)
                cut = cuts[rows_at, :]
                lane = lax.broadcasted_iota(jnp.int32, (size, LANES), 1)
                pieces = []
                for b in range(group.blocks):
                    keep = lax.shift_right_logical(lane + (b * LANES + 1), 1) <= cut
                    source = pl.multiple_of(first_sum + b * group.height + slot * levels, 8)
                    pieces.append(jnp.where(keep, sums[u, pl.ds(source, size), :], 0.0))
                return jnp.concatenate(pieces, axis=1)

            if group.farthest:
                spec = jnp.concatenate([masked(u, 0, levels) for u in range(FIELDS)], axis=0)
                back = back_of(spec, FIELDS)

                @pl.when(scal[4] >= 0)
                def _(back=back):
                    for u in range(FIELDS):
                        held[u ^ scal[0], scal[4]] = back[u]
            else:
                start = group.start(scal[3], rows)

                def part(n, _, group=group, start=start, masked=masked, back_of=back_of):
                    u, slot = n // group.parts, group.chunk_at(lax.rem(n, group.parts))
                    back = back_of(masked(u, slot, group.chunk * levels), group.chunk)
                    held[u ^ scal[0], pl.ds(start + slot, group.chunk)] = back
                    return 0

                lax.fori_loop(0, FIELDS * group.parts, part, 0)

    @pl.when(step == 0)
    def _():
        for at, groups in enumerate(plan.roles):
            pl.when(scal[2] == at)(functools.partial(inverse, at, groups))
        for side, line in enumerate((top, bottom)):

            @pl.when(scal[5 + side] == 0)
            def _(side=side, line=line):
                for field in range(FIELDS):
                    held[field, side * (rows + 1), :, :width] = line[field]

    base = step * step_rows
    tail = width % LANES

    @pl.when(step < last_step)
    def _():
        lane = lax.broadcasted_iota(jnp.int32, (levels, LANES), 1)

        def load(n, _):
            at = n
            row = base + n
            is_raw = (row >= scal[7]) & (row < scal[8])
            for field in range(FIELDS):
                for half in range(halves):
                    piece = raw[field * halves + half]
                    some = slice(half * 8, half * 8 + 8)
                    value = piece[0, at] if field < 2 else piece[at]
                    held[field, row + 1, some, :width] = jnp.where(
                        is_raw, value, held[field, row + 1, some, :width]
                    )
                beyond = jnp.where(
                    lane == tail,
                    pltpu.roll(east[field], (tail + LANES - row) & (LANES - 1), 1),
                    pltpu.roll(west[field], (2 * LANES - 1 - row) & (LANES - 1), 1),
                )
                held[field, row + 1, :, width:] = jnp.where(
                    is_raw, beyond[:, tail:], held[field, row + 1, :, width:]
                )
            return 0

        @pl.when((base < scal[8]) & (base + step_rows > scal[7]))
        def _():
            lax.fori_loop(0, step_rows, load, 0, unroll=3 if step_rows % 3 == 0 else 1)

    slot = step % 2
    count = wide // LANES
    lane = lax.broadcasted_iota(jnp.int32, (8, LANES), 1)
    is_first, is_last = lane == 0, lane == LANES - 1

    def stencil(row, _):
        at = base - step_rows + row
        along, across, push, turn, cos_north, cos_south = [coef[k * rows + at] for k in range(6)]
        across_north, across_south = across * cos_north, across * cos_south
        for part in range(levels // 8):
            some = pl.ds(part * 8, 8)

            def load(field, shift, k):
                return held[field, at + shift, some, k * LANES : (k + 1) * LANES]

            here = [
                functools.lru_cache(maxsize=None)(lambda k, field=field: load(field, 1, k))
                for field in range(FIELDS)
            ]
            here.append(functools.lru_cache(maxsize=None)(lambda k: here[0](k) * here[3](k)))
            up = [functools.lru_cache(maxsize=None)(lambda k, f=f: pltpu.roll(f(k), LANES - 1, 1)) for f in here]
            down = [functools.lru_cache(maxsize=None)(lambda k, f=f: pltpu.roll(f(k), 1, 1)) for f in here]

            def diff_lon(which, k):
                return jnp.where(is_last, up[which]((k + 1) % count), up[which](k)) - jnp.where(
                    is_first, down[which]((k - 1) % count), down[which](k)
                )

            for k in range(count):
                stop = min(width, (k + 1) * LANES)

                def put(field, piece, k=k, stop=stop):
                    ready[slot, field, row, some, k * LANES : stop] = piece[:, : stop - k * LANES]

                u, v, t, h = [here[field](k) for field in range(FIELDS)]
                advect, carry = along * u, 0.1 * v
                v_n, v_s, h_n, h_s = load(1, 0, k), load(1, 2, k), load(3, 0, k), load(3, 2, k)
                put(
                    3,
                    h
                    - along * diff_lon(4, k)
                    - (across_south * (v_s * h_s) - across_north * (v_n * h_n)),
                )
                put(
                    1,
                    v
                    - advect * diff_lon(1, k)
                    - carry * (v_s - v_n)
                    - 0.15 * (h_s - h_n)
                    - turn * u,
                )
                put(
                    0,
                    u
                    - advect * diff_lon(0, k)
                    - carry * (load(0, 2, k) - load(0, 0, k))
                    - push * diff_lon(3, k)
                    + turn * v,
                )
                put(2, t - advect * diff_lon(2, k) - carry * (load(2, 2, k) - load(2, 0, k)))
        return 0

    outs = (new_wind.at[0], new_wind.at[1], new_theta, new_thick)

    def leave(at_step, size, act):
        for field, out in enumerate(outs):
            for k in range(0, step_rows, size):
                act(
                    pltpu.make_async_copy(
                        ready.at[at_step % 2, field, pl.ds(k, size)],
                        out.at[pl.ds((at_step - 1) * step_rows + k, size)],
                        out_sems.at[at_step % 2, field],
                    )
                )

    @pl.when(step > 2)
    def _():
        leave(step - 2, step_rows, lambda copy: copy.wait())

    @pl.when(step > 0)
    def _():
        lax.fori_loop(0, step_rows, stencil, 0)
        leave(step, PIECE if step_rows % PIECE == 0 else step_rows, lambda copy: copy.start())

    @pl.when(step == last_step)
    def _():
        if last_step > 1:
            leave(step - 1, step_rows, lambda copy: copy.wait())
        leave(step, step_rows, lambda copy: copy.wait())


def substep(plan, step_rows, scal, coef, winds, theta, thick, west, east, top, bottom, cuts, tabs, spectra):
    rows, width, levels = plan.rows, plan.width, plan.levels
    once = pl.Buffered(1)
    steps = rows // step_rows

    def block(i, s):
        return jnp.clip(i, s[9], s[10])

    def whole(shape):
        return pl.BlockSpec(shape, lambda i, s: (0,) * len(shape), pipeline_mode=once)

    anywhere = pl.BlockSpec(memory_space=pl.ANY)
    halves = range(levels // 8)
    raw_specs = [
        pl.BlockSpec((1, step_rows, 8, width), lambda i, s, w=wind, h=half: (w, block(i, s), h, 0))
        for wind in range(2)
        for half in halves
    ] + [
        pl.BlockSpec((step_rows, 8, width), lambda i, s, h=half: (block(i, s), h, 0))
        for _ in range(2)
        for half in halves
    ]
    raw = [array for array in (winds, winds, theta, thick) for _ in halves]
    edge, halo = (FIELDS, levels, LANES), (FIELDS, levels, width)
    in_specs = [
        pl.BlockSpec(memory_space=pltpu.SMEM),
        whole(edge),
        whole(edge),
        whole(halo),
        whole(halo),
        whole((plan.slots * levels, LANES)),
        anywhere,
        anywhere,
    ] + raw_specs + [anywhere] * len(spectra)
    shapes = [(2, rows, levels, width)] + [(rows, levels, width)] * 2
    most = max(sum(group.total for group in groups) for groups in plan.roles)
    return pl.pallas_call(
        functools.partial(step_kernel, plan, step_rows),
        grid_spec=pltpu.PrefetchScalarGridSpec(
            num_scalar_prefetch=1,
            grid=(steps + 1,),
            in_specs=in_specs,
            out_specs=[anywhere] * 3,
            scratch_shapes=[
                pltpu.VMEM((FIELDS, rows + 2, levels, plan.wide), jnp.float32),
                pltpu.VMEM((FIELDS, most, LANES), jnp.float32),
                pltpu.VMEM((2, plan.table // LANES, LANES, plan.wide), jnp.bfloat16),
                pltpu.VMEM((2, FIELDS, step_rows, levels, width), jnp.float32),
                pltpu.SemaphoreType.DMA((max(len(groups) for groups in plan.roles), FIELDS)),
                pltpu.SemaphoreType.DMA((2, plan.table // LANES)),
                pltpu.SemaphoreType.DMA((2, FIELDS)),
            ],
        ),
        out_shape=[jax.ShapeDtypeStruct(shape, jnp.float32) for shape in shapes],
        compiler_params=pltpu.CompilerParams(vmem_limit_bytes=VMEM),
        cost_estimate=pl.CostEstimate(
            flops=6 * most * FIELDS * LANES * plan.wide, bytes_accessed=40_000_000, transcendentals=0
        ),
        name="inverse_and_substep",
    )(scal, coef, west, east, top, bottom, cuts, *tabs, *raw, *spectra)


def lon_swap(plan, value, blocks, bit):
    pairs = [
        (block * plan.lon + place, block * plan.lon + (place ^ (1 << bit)))
        for block in blocks
        for place in range(plan.lon)
    ]
    return lax.ppermute(value, ("lat", "lon"), pairs)


def lat_move(plan, value, sources, targets):
    pairs = [
        (source * plan.lon + place, target * plan.lon + place)
        for source, target in zip(sources, targets)
        for place in range(plan.lon)
    ]
    return lax.ppermute(value, ("lat", "lon"), pairs)


def spread(plan, blocks, slots, order):
    for bit in reversed(order):
        for s in sorted(slots):
            slots[s | (1 << bit)] = lon_swap(plan, slots[s], blocks, bit)
    return slots


def gather_sums(plan, blocks, slots, order):
    slots = dict(slots)
    for bit in order:
        sent = [s for s in slots if s >> bit & 1]
        for s in sorted(sent, key=lambda s: -bin(s).count("1")):
            slots[s ^ (1 << bit)] = slots[s ^ (1 << bit)] + lon_swap(plan, slots.pop(s), blocks, bit)
    return spread(plan, blocks, slots, order)


def field_sets(plan):
    sent, kept = [], []
    for at in range(len(plan.roles)):
        bit = at % 2
        sent.append([u for u in range(FIELDS) if u >> bit & 1])
        kept.append([u for u in range(FIELDS) if not u >> bit & 1])
    return sent, kept


def parcel_sums(plan, place, at, blocks, sent, kept):
    first, second = field_sets(plan)
    parts, own = plan.parts, place % plan.parts
    if parts == 1:
        near, far = at % 2, 1 - at % 2
        moved = lon_swap(plan, sent, blocks, near)
        send = kept[1] + moved[1]
        slots = {0: (kept[0] + moved[0]) + lon_swap(plan, send, blocks, far)}
        slots = spread(plan, blocks, slots, [near, far])
        return [slots[u] for u in range(FIELDS)]
    bits = plan.lon.bit_length() - 1
    slots = {}
    for us, array in ((first[at], sent), (second[at], kept)):
        for i, u in enumerate(us):
            pieces = array[i].reshape(parts, -1, LANES)
            for k in range(parts):
                slots[u * parts + k] = pieces[k ^ own]
    order = list(range(bits)) if at % 2 == 0 else list(reversed(range(bits)))
    slots = gather_sums(plan, blocks, slots, order)
    result = []
    for u in range(FIELDS):
        pieces = jnp.stack([slots[u * parts + k] for k in range(parts)])
        result.append(pieces[jnp.arange(parts) ^ own].reshape(-1, LANES))
    return result


def all_sums(plan, place, sent, kept):
    result, number = [], 0
    for at in range(len(plan.roles)):
        home = plan.blocks(at)
        for k in range(len(plan.parcels(at))):
            first, second = sent[number], kept[number]
            number += 1
            if k == 0:
                result += parcel_sums(plan, place, at, home, first, second)
                continue
            helpers = plan.blocks(at + len(plan.roles))
            first, second = [lat_move(plan, array, home, helpers) for array in (first, second)]
            sums = parcel_sums(plan, place, at, helpers, first, second)
            result += [lat_move(plan, array, helpers, home) for array in sums]
    return result


def body(winds, theta, thick, polar_rows, cutoffs):
    lat, lon = lax.axis_size("lat"), lax.axis_size("lon")
    levels, rows, width = theta.shape
    sizes = (lat, lon, levels, rows, width, polar_rows.shape[0])
    plan = Plan(*sizes)
    t_tabs, i_tabs = [tuple(jnp.asarray(part) for part in pair) for pair in tables(sizes)]
    block, place = lax.axis_index("lat"), lax.axis_index("lon")
    winds = winds.transpose(0, 2, 1, 3)
    theta = theta.transpose(1, 0, 2)
    thick = thick.transpose(1, 0, 2)
    hemi = (block >= lat // 2).astype(jnp.int32)
    role = jnp.where(hemi == 1, lat - 1 - block, block)

    def line(row):
        return jnp.stack([winds[0, row], winds[1, row], theta[row], thick[row]])

    south_pairs = [(b * lon + p, (b + 1) * lon + p) for b in range(lat - 1) for p in range(lon)]
    north_pairs = [(to, at) for at, to in south_pairs]
    top = lax.ppermute(line(rows - 1), ("lat", "lon"), south_pairs)
    bottom = lax.ppermute(line(0), ("lat", "lon"), north_pairs)

    step_rows = max(k for k in range(1, 16) if rows % k == 0)
    listed = polar_rows.shape[0]
    north_run = jnp.sum((polar_rows < plan.total_rows // 2).astype(jnp.int32))
    south_first = plan.total_rows - listed + north_run
    far_row = jnp.where(hemi == 1, south_first, north_run - 1)
    far_at = far_row - block * rows + 1
    far_at = jnp.where((far_at >= 0) & (far_at <= rows + 1), far_at, -1)
    raw_from = jnp.clip(north_run - block * rows, 0, rows)
    raw_to = jnp.clip(south_first - block * rows, 0, rows)
    block_from = jnp.minimum(raw_from, rows - 1) // step_rows
    block_to = jnp.maximum(block_from, jnp.maximum(raw_to - 1, 0) // step_rows)
    above, below = block * rows - 1, (block + 1) * rows

    def is_listed(row):
        return (row >= 0) & (row < plan.total_rows) & ((row < north_run) | (row >= south_first))

    facts = [
        place // plan.parts, place, role, hemi, far_at, is_listed(above), is_listed(below),
        raw_from, raw_to, block_from, block_to,
    ]
    scal = jnp.stack([jnp.asarray(fact).astype(jnp.int32) for fact in facts])

    first_edge, last_edge = edges(plan, winds, theta, thick)
    west = lax.ppermute(last_edge, "lon", [(i, (i + 1) % lon) for i in range(lon)])
    east = lax.ppermute(first_edge, "lon", [((i + 1) % lon, i) for i in range(lon)])
    scal, _ = lax.optimization_barrier((scal, first_edge))

    first, second = field_sets(plan)
    sent = forward(plan, first, scal, winds, theta, thick, top, bottom, t_tabs)
    kept = forward(plan, second, scal, winds, theta, thick, top, bottom, t_tabs)
    sums = all_sums(plan, place, sent, kept)

    slot_rows = jnp.asarray(plan.slot_rows())[jnp.minimum(role, len(plan.roles) - 1), hemi]
    slot_rows = jnp.where(slot_rows == -2, far_at, slot_rows)
    hits = (polar_rows[None, :] == (slot_rows - 1 + block * rows)[:, None]) & (slot_rows >= 0)[:, None]
    cut = jnp.sum(jnp.where(hits, cutoffs[None, :] + 1, 0), axis=1) - 1
    cuts = jnp.broadcast_to(cut.astype(jnp.int32)[:, None, None], (plan.slots, levels, LANES))
    cuts = cuts.reshape(plan.slots * levels, LANES)

    ring = block * rows - 1 + jnp.arange(rows + 2, dtype=jnp.int32)
    centre = (ring.astype(jnp.float32) + 0.5) * (jnp.pi / plan.total_rows)
    cos, sin = jnp.sin(centre), -jnp.cos(centre)
    mid = cos[1:-1]
    coef = jnp.concatenate([0.025 / mid, 0.1 / mid, 0.05 / mid, 0.3 * sin[1:-1], cos[:-2], cos[2:]])

    out = substep(
        plan, step_rows, scal, coef, winds, theta, thick, west, east, top, bottom, cuts, i_tabs, sums
    )
    return (out[0].transpose(0, 2, 1, 3), out[1].transpose(1, 0, 2), out[2].transpose(1, 0, 2))


def solution(mesh):
    in_specs = (P(None, None, "lat", "lon"), P(None, "lat", "lon"), P(None, "lat", "lon"), P(), P())
    out_specs = (P(None, None, "lat", "lon"), P(None, "lat", "lon"), P(None, "lat", "lon"))
    return jax.shard_map(body, mesh=mesh, in_specs=in_specs, out_specs=out_specs, check_vma=False)
```

```python
import functools

import jax
import jax.numpy as jnp
import ml_dtypes
import numpy as np
from jax import lax
from jax.experimental import pallas as pl
from jax.experimental.pallas import tpu as pltpu
from jax.sharding import PartitionSpec as P

FIELDS = 4
LANES = 128
PIECE = 3
VMEM = 60 * 1024 * 1024


def round_up(value, step):
    return -(-value // step) * step


class Group:
    def __init__(self, first, stop, near, far, blocks, levels, quarters):
        self.first, self.stop, self.blocks, self.levels = first, stop, blocks, levels
        self.near, self.far = int(near), int(far)
        self.own = stop - first
        self.farthest = self.own == 0
        self.slots = 1 if self.farthest else self.own + self.near + self.far
        self.height = self.slots * levels
        self.quarters = list(quarters)
        assert sum(self.quarters) == self.slots
        one, two, three, four = self.quarters
        self.beside = max(one, three) if one and three else 0
        self.half = -(-two // 2)
        self.packed = self.beside > 0 or two > 1
        self.pieces = []
        if self.packed:
            if not self.beside:
                for start, count in ((0, one), (one + two, three)):
                    if count:
                        self.pieces.append((0, start, count))
            if four:
                self.pieces.append((0, one + two + three, four))
        self.whole_rows = sum(piece[2] for piece in self.pieces)
        self.full = self.height * (blocks - 1 if self.packed else blocks)
        self.packed_rows = (self.whole_rows + self.beside + self.half) * levels if self.packed else 0
        self.total = self.full + self.packed_rows
        parts = max(1, round(self.slots / 16))
        self.chunk = -(-self.slots // parts)
        self.parts = -(-self.slots // self.chunk)

    def start(self, hemi, rows):
        return jnp.where(hemi == 1, rows - self.stop + 1 - self.far, self.first + 1 - self.near)

    def chunk_at(self, part):
        return jnp.minimum(part * self.chunk, self.slots - self.chunk)

    def slot(self, hemi, first, count):
        first = min(first, self.slots - count)
        return jnp.where(hemi == 1, self.slots - count - first, first)

    def pairs(self):
        one, two, three, _ = self.quarters
        result = []
        if self.beside:
            result.append((one + two, 0, self.beside, 96))
        if two:
            result.append((one, one + two - self.half, self.half, 64))
        return result

    def pack(self, hemi, last, to):
        row = 0
        for _, first, count in self.pieces:
            to(row, count, last(self.slot(hemi, first, count), count))
            row += count
        for left, right, count, lanes in self.pairs():
            lane = lax.broadcasted_iota(jnp.int32, (count * self.levels, LANES), 1)
            beside = pltpu.roll(last(self.slot(hemi, right, count), count), lanes, 1)
            to(row, count, jnp.where(lane < lanes, last(self.slot(hemi, left, count), count), beside))
            row += count

    def unpack(self, hemi, packed, to):
        row = self.whole_rows
        for left, right, count, lanes in self.pairs():
            value = packed(row, count)
            to(self.slot(hemi, left, count), count, value)
            to(self.slot(hemi, right, count), count, pltpu.roll(value, LANES - lanes, 1))
            row += count
        row = 0
        for _, first, count in self.pieces:
            to(self.slot(hemi, first, count), count, packed(row, count))
            row += count


class Plan:
    def __init__(self, lat, lon, levels, rows, width, listed):
        self.lat, self.lon, self.levels, self.rows, self.width = lat, lon, levels, rows, width
        self.total_rows, self.length = lat * rows, lon * width
        self.parts = lon // FIELDS
        self.wide = round_up(width + 2, LANES)
        pole = listed // 2
        self.high = pole + pole // 4
        top = self.length // 4 - 1

        def blocks_of(depth):
            return -(-(2 * min(2 * (depth + 1), top) + 1) // LANES)

        self.roles = []
        last = self.high - 2
        for role in range(lat // 2):
            start = role * rows
            if start > last:
                break
            need = {}
            for depth in range(start, min(start + rows - 1, last) + 1):
                need.setdefault(blocks_of(depth), []).append(depth - start)
            spans = [[need[k][0], need[k][-1] + 1, False, False, k] for k in sorted(need)]
            if role > 0:
                spans[0][2], spans[0][4] = True, max(spans[0][4], blocks_of(start - 1))
            if start + rows <= last:
                spans[-1][3], spans[-1][4] = True, max(spans[-1][4], blocks_of(start + rows))
            groups = []
            for first, stop, near, far, blocks in spans:
                depths = range(start + first - int(near), start + stop + int(far))
                quarters = [0] * 4
                for depth in depths:
                    lanes = 2 * min(2 * (depth + 1), top) + 1 - (blocks - 1) * LANES
                    quarters[max(0, -(-lanes // (LANES // 4)) - 1)] += 1
                groups.append(Group(first, stop, near, far, blocks, levels, quarters))
            groups.append(Group(0, 0, False, False, -(-(2 * top + 1) // LANES), levels, (0, 0, 0, 1)))
            self.roles.append(groups)
        self.slots = max(sum(group.slots for group in groups) for groups in self.roles)
        self.table = LANES * max(group.blocks for groups in self.roles for group in groups)
        count = len(self.roles)
        self.lent = {}
        if self.parts == 1 and 2 * count <= lat // 2:
            self.lent = {count - 1: len(self.roles[-1]) - 2}

    def blocks(self, role):
        return (role, self.lat - 1 - role)

    def parcels(self, at):
        indices = range(len(self.roles[at]))
        away = self.lent.get(at)
        home = [g for g in indices if g != away]
        return [home] if away is None else [home, [away]]

    def arrays(self):
        calls = [[], []]
        for at in range(len(self.roles)):
            if at in self.lent:
                calls[0] += [(at, 1, 0), (at, 1, 1)]
                calls[1] += [(at, 0, 0), (at, 0, 1)]
            else:
                calls[0].append((at, 0, 0))
                calls[1].append((at, 0, 1))
        return calls

    def places(self):
        result, number = {}, 0
        for at in range(len(self.roles)):
            for parcel in self.parcels(at):
                offset = 0
                for g in parcel:
                    result[at, g] = (number, offset)
                    offset += self.roles[at][g].total
                number += 1
        return result

    def height_of(self, at, parcel):
        return sum(self.roles[at][g].total for g in self.parcels(at)[parcel])

    def heights(self):
        return [
            self.height_of(at, parcel) for at in range(len(self.roles)) for parcel in range(len(self.parcels(at)))
        ]

    def slot_rows(self):
        table = np.full((len(self.roles), 2, self.slots), -1, np.int32)
        for at, groups in enumerate(self.roles):
            for hemi in range(2):
                rows = []
                for group in groups:
                    first = group.first + 1 - group.near if hemi == 0 else self.rows - group.stop + 1 - group.far
                    rows += [-2] if group.farthest else [first + k for k in range(group.slots)]
                table[at, hemi, : len(rows)] = rows
        return table


def split_table(table):
    high = table.astype(ml_dtypes.bfloat16)
    low = (table - high.astype(np.float64)).astype(ml_dtypes.bfloat16)
    return high, low


@functools.lru_cache(maxsize=None)
def tables(sizes):
    plan = Plan(*sizes)
    index = np.arange(plan.table)
    wave, odd = (index + 1) // 2, (index % 2 == 0) & (index > 0)
    used = wave < plan.length // 4
    points = np.zeros(plan.wide, np.int64)
    points[: plan.width + 1] = np.arange(plan.width + 1)
    points[-1] = -1
    shown = np.zeros(plan.wide, bool)
    shown[: plan.width + 1] = True
    shown[-1] = True

    def trig(at):
        angle = (wave[:, None] * at[None, :]) % plan.length * (2.0 * np.pi / plan.length)
        return np.where(odd[:, None], np.sin(angle), np.cos(angle)) * used[:, None]

    weight = np.where(wave == 0, 1.0, 2.0) / plan.length
    forward, inverse = [], []
    for place in range(plan.lon):
        forward.append(trig(place * plan.width + np.arange(plan.width)).T)
        inverse.append(trig(place * plan.width + points) * weight[:, None] * shown[None, :])
    shape = (plan.lon, plan.width, plan.table // LANES, LANES)
    forward = np.stack(forward).reshape(shape).transpose(0, 2, 1, 3)
    inverse = np.stack(inverse).reshape(plan.lon, plan.table // LANES, LANES, plan.wide)
    return split_table(forward), split_table(inverse)


def fetch_table(place, tabs, held, sems, blocks):
    return [
        pltpu.make_async_copy(tab.at[place, b], held.at[half, b], sems.at[half, b])
        for b in blocks
        for half, tab in enumerate(tabs)
    ]


def split(value):
    high = value.astype(jnp.bfloat16)
    low = (value - high.astype(jnp.float32)).astype(jnp.bfloat16)
    return high, low


def three_pass(left, right):
    total = jnp.dot(left[0], right[0], preferred_element_type=jnp.float32)
    total += jnp.dot(left[0], right[1], preferred_element_type=jnp.float32)
    total += jnp.dot(left[1], right[0], preferred_element_type=jnp.float32)
    return total


def forward_kernel(plan, call, scal, winds, theta, thick, top, bottom, t_high, t_low, *refs):
    places, sets, arrays = plan.places(), field_sets(plan), plan.arrays()[call]
    outs, (points, spectra, held, in_sems, out_sems, t_sems) = refs[: len(arrays)], refs[len(arrays) :]
    levels, width = plan.levels, plan.width
    hemi = scal[3]
    for at, groups in enumerate(plan.roles):

        @pl.when(scal[2] == at)
        def _(at=at, groups=groups):
            mine = [(number, array[1:]) for number, array in enumerate(arrays) if array[0] == at]
            order = [g for g in range(len(groups)) if any(g in plan.parcels(at)[a[0]] for _, a in mine)]
            targets = {}
            for g in order:
                targets[g] = [
                    (number, i, u)
                    for number, (parcel, which) in mine
                    if g in plan.parcels(at)[parcel]
                    for i, u in enumerate(sets[which][at])
                ]
            some_fields = {g: [u ^ scal[0] for _, _, u in targets[g]] for g in order}
            turn_of = {g: n % 2 for n, g in enumerate(order)}
            ready = 0

            def first_row(group):
                if group.farthest:
                    return jnp.clip(scal[4] - 1, 0, plan.rows - 1), 0, 1
                first = jnp.where(hemi == 1, plan.rows - group.stop, group.first)
                return first, jnp.where(hemi == 1, group.far, group.near), group.own

            def fetch(g):
                first, slot, count = first_row(groups[g])
                for i, field in enumerate(some_fields[g]):

                    def pieces(source, i=i):
                        for k in range(0, count, PIECE):
                            size = min(PIECE, count - k)
                            pltpu.make_async_copy(
                                source.at[pl.ds(first + k, size)],
                                points.at[turn_of[g], i, pl.ds(slot + k, size)],
                                in_sems.at[turn_of[g], i],
                            ).start()

                    pl.when(field < 2)(lambda: pieces(winds.at[jnp.minimum(field, 1)]))
                    pl.when(field == 2)(lambda: pieces(theta))
                    pl.when(field == 3)(lambda: pieces(thick))

            def arrive(g):
                first, slot, count = first_row(groups[g])
                for i in range(len(targets[g])):
                    pltpu.make_async_copy(
                        theta.at[pl.ds(first, count)],
                        points.at[turn_of[g], i, pl.ds(slot, count)],
                        in_sems.at[turn_of[g], i],
                    ).wait()

            def leave(g, parts):
                group, turn, copies = groups[g], turn_of[g], []
                _, offset = places[at, g]
                size = group.full // parts
                for i, (number, place, _) in enumerate(targets[g]):
                    for k in range(parts if group.full else 0):
                        copies.append(
                            pltpu.make_async_copy(
                                spectra.at[turn, i, pl.ds(k * size, size)],
                                outs[number].at[place, pl.ds(offset + k * size, size)],
                                out_sems.at[turn, i, 0],
                            )
                        )
                    if group.packed:
                        copies.append(
                            pltpu.make_async_copy(
                                spectra.at[turn, i, pl.ds(group.blocks * group.height, group.packed_rows)],
                                outs[number].at[place, pl.ds(offset + group.full, group.packed_rows)],
                                out_sems.at[turn, i, 1],
                            )
                        )
                return copies

            def pack(g, i):
                group, turn = groups[g], turn_of[g]

                def last(slot, count):
                    at_row = pl.multiple_of((group.blocks - 1) * group.height + slot * levels, 8)
                    return spectra[turn, i, pl.ds(at_row, count * levels), :]

                def to(row, count, value):
                    at_row = group.blocks * group.height + row * levels
                    spectra[turn, i, at_row : at_row + count * levels, :] = value

                group.pack(hemi, last, to)

            def halo(g, slot, line, wanted):
                @pl.when(wanted)
                def _():
                    for i, field in enumerate(some_fields[g]):
                        points[turn_of[g], i, slot] = line[field]

            fetch(order[0])
            needed = range(max(groups[g].blocks for g in order))
            for copy in fetch_table(scal[1], (t_high, t_low), held, t_sems, needed):
                copy.start()
            for n, g in enumerate(order):
                group = groups[g]
                if n + 1 < len(order):
                    fetch(order[n + 1])
                arrive(g)
                for copy in fetch_table(scal[1], (t_high, t_low), held, t_sems, range(ready, group.blocks)):
                    copy.wait()
                ready = max(ready, group.blocks)
                if group.farthest:
                    halo(g, 0, top, scal[4] == 0)
                    halo(g, 0, bottom, scal[4] == plan.rows + 1)
                if group.near:
                    halo(g, 0, top, hemi == 0)
                    halo(g, group.slots - 1, bottom, hemi == 1)
                if group.far:
                    halo(g, group.slots - 1, bottom, hemi == 0)
                    halo(g, 0, top, hemi == 1)
                if n >= 2:
                    for copy in leave(order[n - 2], 1):
                        copy.wait()

                def transform(value, group=group):
                    return three_pass(
                        split(value),
                        [
                            jnp.concatenate([held[half, b] for b in range(group.blocks)], axis=1)
                            for half in range(2)
                        ],
                    )

                if group.farthest:
                    spec = transform(points[turn_of[g], : len(targets[g]), 0].reshape(len(targets[g]) * levels, width))
                    for i in range(len(targets[g])):
                        for b in range(group.blocks):
                            spectra[turn_of[g], i, b * levels : (b + 1) * levels, :] = spec[
                                i * levels : (i + 1) * levels, b * LANES : (b + 1) * LANES
                            ]
                else:

                    def part(n, _, g=g, group=group, transform=transform):
                        i, slot = n // group.parts, group.chunk_at(lax.rem(n, group.parts))
                        size = group.chunk * levels
                        spec = transform(points[turn_of[g], i, pl.ds(slot, group.chunk)].reshape(size, width))
                        for b in range(group.blocks):
                            target = pl.multiple_of(b * group.height + slot * levels, 8)
                            spectra[turn_of[g], i, pl.ds(target, size), :] = spec[:, b * LANES : (b + 1) * LANES]
                        return 0

                    lax.fori_loop(0, len(targets[g]) * group.parts, part, 0)
                if group.packed:
                    lax.fori_loop(0, len(targets[g]), lambda i, _, g=g: (pack(g, i), 0)[1], 0)
                for copy in leave(g, max(1, group.full // group.height)):
                    copy.start()
            for g in order[-2:]:
                for copy in leave(g, 1):
                    copy.wait()


def forward(plan, call, scal, winds, theta, thick, top, bottom, tabs):
    arrays = plan.arrays()[call]
    count = FIELDS if plan.lent else FIELDS // 2
    shapes = [(FIELDS // 2, plan.height_of(at, parcel), LANES) for at, parcel, _ in arrays]
    anywhere = pl.BlockSpec(memory_space=pl.ANY)
    halo = pl.BlockSpec((FIELDS, plan.levels, plan.width), lambda i, s: (0, 0, 0))
    slots = max(group.slots for groups in plan.roles for group in groups)
    total = max(group.height * group.blocks + group.packed_rows for groups in plan.roles for group in groups)
    outs = pl.pallas_call(
        functools.partial(forward_kernel, plan, call),
        grid_spec=pltpu.PrefetchScalarGridSpec(
            num_scalar_prefetch=1,
            grid=(1,),
            in_specs=[anywhere] * 3 + [halo, halo, anywhere, anywhere],
            out_specs=[anywhere] * len(arrays),
            scratch_shapes=[
                pltpu.VMEM((2, count, slots, plan.levels, plan.width), jnp.float32),
                pltpu.VMEM((2, count, total, LANES), jnp.float32),
                pltpu.VMEM((2, plan.table // LANES, plan.width, LANES), jnp.bfloat16),
                pltpu.SemaphoreType.DMA((2, count)),
                pltpu.SemaphoreType.DMA((2, count, 2)),
                pltpu.SemaphoreType.DMA((2, plan.table // LANES)),
            ],
        ),
        out_shape=[jax.ShapeDtypeStruct(shape, jnp.float32) for shape in shapes],
        compiler_params=pltpu.CompilerParams(vmem_limit_bytes=VMEM),
        cost_estimate=pl.CostEstimate(
            flops=6 * max(shape[1] for shape in shapes) * count * LANES * plan.width, bytes_accessed=15_000_000, transcendentals=0
        ),
        name="partial_spectra",
    )(scal, winds, theta, thick, top, bottom, *tabs)
    return dict(zip(arrays, outs))


def edge_kernel(plan, count, _, *refs):
    ins, outs = refs[:-2], refs[-2:]
    lane = lax.broadcasted_iota(jnp.int32, (plan.levels, LANES), 1)
    some = plan.rows // count
    for side, column in enumerate((0, (plan.width - 1) % LANES)):
        kept = (jnp.zeros((plan.levels, LANES), jnp.float32),) * FIELDS
        for piece in range(count):
            at = (side * count + piece) * FIELDS
            fields = ins[at : at + FIELDS]

            def pick(row, kept, fields=fields, piece=piece, column=column):
                values = (fields[0][0, row], fields[1][0, row], fields[2][row], fields[3][row])
                return tuple(
                    jnp.where(lane == row + piece * some, value[:, column : column + 1], old)
                    for value, old in zip(values, kept)
                )

            kept = lax.fori_loop(0, some, pick, kept, unroll=max(k for k in range(1, 11) if some % k == 0))
        for field in range(FIELDS):
            outs[side][field] = kept[field]


def edges(plan, after, winds, theta, thick):
    count = 3 if plan.rows % 3 == 0 else 1
    some = plan.rows // count
    specs = []
    for at in (0, (plan.width - 1) // LANES):
        for piece in range(count):
            for wind in range(2):
                specs.append(
                    pl.BlockSpec(
                        (1, some, plan.levels, LANES), lambda i, w=wind, p=piece, at=at: (w, p, 0, at)
                    )
                )
            specs += [pl.BlockSpec((some, plan.levels, LANES), lambda i, p=piece, at=at: (p, 0, at))] * 2
    shape = (FIELDS, plan.levels, LANES)
    return pl.pallas_call(
        functools.partial(edge_kernel, plan, count),
        grid=(1,),
        in_specs=[pl.BlockSpec(memory_space=pl.ANY)] + specs,
        out_specs=[pl.BlockSpec(shape, lambda i: (0, 0, 0))] * 2,
        out_shape=[jax.ShapeDtypeStruct(shape, jnp.float32)] * 2,
        compiler_params=pltpu.CompilerParams(vmem_limit_bytes=VMEM),
        cost_estimate=pl.CostEstimate(flops=0, bytes_accessed=6_000_000, transcendentals=0),
        name="edge_columns",
    )(after, *[winds, winds, theta, thick] * (2 * count))


def step_kernel(plan, step_rows, scal, coef, west, east, top, bottom, cuts, i_high, i_low, *refs):
    places, heights = plan.places(), plan.heights()
    halves = plan.levels // 8
    raw, refs = refs[: FIELDS * halves], refs[FIELDS * halves :]
    spectra = refs[: FIELDS * len(heights)]
    new_wind, new_theta, new_thick, held, sums, unpacked, table, ready, sems, t_sems, out_sems = refs[FIELDS * len(heights) :]
    step = pl.program_id(0)
    rows, width, wide, levels = plan.rows, plan.width, plan.wide, plan.levels
    last_step = rows // step_rows

    def inverse(at, groups):
        slot_at = np.cumsum([0] + [group.slots for group in groups])
        row_at = np.cumsum([0] + [group.total for group in groups])

        def copies(g):
            number, offset = places[at, g]
            return [
                pltpu.make_async_copy(
                    spectra[number * FIELDS + u].at[pl.ds(offset, groups[g].total)],
                    sums.at[u, pl.ds(int(row_at[g]), groups[g].total)],
                    sems.at[g, u],
                )
                for u in range(FIELDS)
            ]

        have = 0
        for g, group in enumerate(groups):
            for copy in copies(g):
                copy.start()
            for copy in fetch_table(scal[1], (i_high, i_low), table, t_sems, range(have, group.blocks)):
                copy.start()
            have = max(have, group.blocks)
        have = 0
        for g, group in enumerate(groups):
            for copy in copies(g):
                copy.wait()
            for copy in fetch_table(scal[1], (i_high, i_low), table, t_sems, range(have, group.blocks)):
                copy.wait()
            have = max(have, group.blocks)
            lanes = group.blocks * LANES
            first_slot, first_sum = int(slot_at[g]), int(row_at[g])

            def back_of(spec, size, lanes=lanes, group=group):
                back = three_pass(
                    split(spec), [table[half, : group.blocks].reshape(lanes, wide) for half in range(2)]
                )
                return back.reshape(size, levels, wide)

            def masked(u, slot, size, group=group, first_slot=first_slot, first_sum=first_sum):
                rows_at = pl.ds(pl.multiple_of((first_slot + slot) * levels, 8), size)
                cut = cuts[rows_at, :]
                lane = lax.broadcasted_iota(jnp.int32, (size, LANES), 1)
                pieces = []
                for b in range(group.blocks):
                    keep = lax.shift_right_logical(lane + (b * LANES + 1), 1) <= cut
                    if group.packed and b == group.blocks - 1:
                        value = unpacked[u, pl.ds(pl.multiple_of(slot * levels, 8), size), :]
                    else:
                        source = pl.multiple_of(first_sum + b * group.height + slot * levels, 8)
                        value = sums[u, pl.ds(source, size), :]
                    pieces.append(jnp.where(keep, value, 0.0))
                return jnp.concatenate(pieces, axis=1)

            def unpack(u, _, group=group, first_sum=first_sum):
                def packed(row, count):
                    at_row = first_sum + group.full + row * levels
                    return sums[u, at_row : at_row + count * levels, :]

                def to(slot, count, value):
                    at_row = pl.multiple_of(slot * levels, 8)
                    unpacked[u, pl.ds(at_row, count * levels), :] = value

                group.unpack(scal[3], packed, to)
                return 0

            if group.packed:
                lax.fori_loop(0, FIELDS, unpack, 0)
            if group.farthest:
                spec = jnp.concatenate([masked(u, 0, levels) for u in range(FIELDS)], axis=0)
                back = back_of(spec, FIELDS)

                @pl.when(scal[4] >= 0)
                def _(back=back):
                    for u in range(FIELDS):
                        held[u ^ scal[0], scal[4]] = back[u]
            else:
                start = group.start(scal[3], rows)

                def part(n, _, group=group, start=start, masked=masked, back_of=back_of):
                    u, slot = n // group.parts, group.chunk_at(lax.rem(n, group.parts))
                    back = back_of(masked(u, slot, group.chunk * levels), group.chunk)
                    held[u ^ scal[0], pl.ds(start + slot, group.chunk)] = back
                    return 0

                lax.fori_loop(0, FIELDS * group.parts, part, 0)

    @pl.when(step == 0)
    def _():
        for at, groups in enumerate(plan.roles):
            pl.when(scal[2] == at)(functools.partial(inverse, at, groups))
        for side, line in enumerate((top, bottom)):

            @pl.when(scal[5 + side] == 0)
            def _(side=side, line=line):
                for field in range(FIELDS):
                    held[field, side * (rows + 1), :, :width] = line[field]

    base = step * step_rows
    tail = width % LANES

    @pl.when(step < last_step)
    def _():
        lane = lax.broadcasted_iota(jnp.int32, (levels, LANES), 1)

        def load(n, _):
            at = n
            row = base + n
            is_raw = (row >= scal[7]) & (row < scal[8])
            for field in range(FIELDS):
                for half in range(halves):
                    piece = raw[field * halves + half]
                    some = slice(half * 8, half * 8 + 8)
                    value = piece[0, at] if field < 2 else piece[at]
                    held[field, row + 1, some, :width] = jnp.where(
                        is_raw, value, held[field, row + 1, some, :width]
                    )
                beyond = jnp.where(
                    lane == tail,
                    pltpu.roll(east[field], (tail + LANES - row) & (LANES - 1), 1),
                    pltpu.roll(west[field], (2 * LANES - 1 - row) & (LANES - 1), 1),
                )
                held[field, row + 1, :, width:] = jnp.where(
                    is_raw, beyond[:, tail:], held[field, row + 1, :, width:]
                )
            return 0

        @pl.when((base < scal[8]) & (base + step_rows > scal[7]))
        def _():
            lax.fori_loop(0, step_rows, load, 0, unroll=3 if step_rows % 3 == 0 else 1)

    slot = step % 2
    count = wide // LANES
    lane = lax.broadcasted_iota(jnp.int32, (8, LANES), 1)
    is_first, is_last = lane == 0, lane == LANES - 1

    def stencil(row, _):
        at = base - step_rows + row
        along, across, push, turn, cos_north, cos_south = [coef[k * rows + at] for k in range(6)]
        across_north, across_south = across * cos_north, across * cos_south
        for part in range(levels // 8):
            some = pl.ds(part * 8, 8)

            def load(field, shift, k):
                return held[field, at + shift, some, k * LANES : (k + 1) * LANES]

            here = [
                functools.lru_cache(maxsize=None)(lambda k, field=field: load(field, 1, k))
                for field in range(FIELDS)
            ]
            up = [functools.lru_cache(maxsize=None)(lambda k, f=f: pltpu.roll(f(k), LANES - 1, 1)) for f in here]
            down = [functools.lru_cache(maxsize=None)(lambda k, f=f: pltpu.roll(f(k), 1, 1)) for f in here]

            def shifted(which, k):
                return (
                    jnp.where(is_last, up[which]((k + 1) % count), up[which](k)),
                    jnp.where(is_first, down[which]((k - 1) % count), down[which](k)),
                )

            for k in range(count):
                stop = min(width, (k + 1) * LANES)

                def put(field, piece, k=k, stop=stop):
                    ready[slot, field, row, some, k * LANES : stop] = piece[:, : stop - k * LANES]

                u, v, t, h = [here[field](k) for field in range(FIELDS)]
                advect, carry = along * u, 0.1 * v
                (u_e, u_w), (v_e, v_w), (t_e, t_w), (h_e, h_w) = [shifted(field, k) for field in range(FIELDS)]
                v_n, v_s, h_n, h_s = load(1, 0, k), load(1, 2, k), load(3, 0, k), load(3, 2, k)
                put(
                    3,
                    h
                    - along * (u_e * h_e - u_w * h_w)
                    - (across_south * (v_s * h_s) - across_north * (v_n * h_n)),
                )
                put(
                    1,
                    v
                    - advect * (v_e - v_w)
                    - carry * (v_s - v_n)
                    - 0.15 * (h_s - h_n)
                    - turn * u,
                )
                put(
                    0,
                    u
                    - advect * (u_e - u_w)
                    - carry * (load(0, 2, k) - load(0, 0, k))
                    - push * (h_e - h_w)
                    + turn * v,
                )
                put(2, t - advect * (t_e - t_w) - carry * (load(2, 2, k) - load(2, 0, k)))
        return 0

    outs = (new_wind.at[0], new_wind.at[1], new_theta, new_thick)

    def leave(at_step, size, act):
        for field, out in enumerate(outs):
            for k in range(0, step_rows, size):
                act(
                    pltpu.make_async_copy(
                        ready.at[at_step % 2, field, pl.ds(k, size)],
                        out.at[pl.ds((at_step - 1) * step_rows + k, size)],
                        out_sems.at[at_step % 2, field],
                    )
                )

    @pl.when(step > 2)
    def _():
        leave(step - 2, step_rows, lambda copy: copy.wait())

    @pl.when(step > 0)
    def _():
        lax.fori_loop(0, step_rows, stencil, 0)
        leave(step, PIECE if step_rows % PIECE == 0 else step_rows, lambda copy: copy.start())

    @pl.when(step == last_step)
    def _():
        if last_step > 1:
            leave(step - 1, step_rows, lambda copy: copy.wait())
        leave(step, step_rows, lambda copy: copy.wait())


def substep(plan, step_rows, scal, coef, winds, theta, thick, west, east, top, bottom, cuts, tabs, spectra):
    rows, width, levels = plan.rows, plan.width, plan.levels
    once = pl.Buffered(1)
    steps = rows // step_rows

    def block(i, s):
        return jnp.clip(i, s[9], s[10])

    def whole(shape):
        return pl.BlockSpec(shape, lambda i, s: (0,) * len(shape), pipeline_mode=once)

    anywhere = pl.BlockSpec(memory_space=pl.ANY)
    halves = range(levels // 8)
    raw_specs = [
        pl.BlockSpec((1, step_rows, 8, width), lambda i, s, w=wind, h=half: (w, block(i, s), h, 0))
        for wind in range(2)
        for half in halves
    ] + [
        pl.BlockSpec((step_rows, 8, width), lambda i, s, h=half: (block(i, s), h, 0))
        for _ in range(2)
        for half in halves
    ]
    raw = [array for array in (winds, winds, theta, thick) for _ in halves]
    edge, halo = (FIELDS, levels, LANES), (FIELDS, levels, width)
    in_specs = [
        pl.BlockSpec(memory_space=pltpu.SMEM),
        whole(edge),
        whole(edge),
        whole(halo),
        whole(halo),
        whole((plan.slots * levels, LANES)),
        anywhere,
        anywhere,
    ] + raw_specs + [anywhere] * len(spectra)
    shapes = [(2, rows, levels, width)] + [(rows, levels, width)] * 2
    most = max(sum(group.total for group in groups) for groups in plan.roles)
    return pl.pallas_call(
        functools.partial(step_kernel, plan, step_rows),
        grid_spec=pltpu.PrefetchScalarGridSpec(
            num_scalar_prefetch=1,
            grid=(steps + 1,),
            in_specs=in_specs,
            out_specs=[anywhere] * 3,
            scratch_shapes=[
                pltpu.VMEM((FIELDS, rows + 2, levels, plan.wide), jnp.float32),
                pltpu.VMEM((FIELDS, most, LANES), jnp.float32),
                pltpu.VMEM((FIELDS, max(group.height for groups in plan.roles for group in groups), LANES), jnp.float32),
                pltpu.VMEM((2, plan.table // LANES, LANES, plan.wide), jnp.bfloat16),
                pltpu.VMEM((2, FIELDS, step_rows, levels, width), jnp.float32),
                pltpu.SemaphoreType.DMA((max(len(groups) for groups in plan.roles), FIELDS)),
                pltpu.SemaphoreType.DMA((2, plan.table // LANES)),
                pltpu.SemaphoreType.DMA((2, FIELDS)),
            ],
        ),
        out_shape=[jax.ShapeDtypeStruct(shape, jnp.float32) for shape in shapes],
        compiler_params=pltpu.CompilerParams(vmem_limit_bytes=VMEM),
        cost_estimate=pl.CostEstimate(
            flops=6 * most * FIELDS * LANES * plan.wide, bytes_accessed=40_000_000, transcendentals=0
        ),
        name="inverse_and_substep",
    )(scal, coef, west, east, top, bottom, cuts, *tabs, *raw, *spectra)


def lon_swap(plan, value, blocks, bit):
    pairs = [
        (block * plan.lon + place, block * plan.lon + (place ^ (1 << bit)))
        for block in blocks
        for place in range(plan.lon)
    ]
    return lax.ppermute(value, ("lat", "lon"), pairs)


def lat_move(plan, value, sources, targets):
    pairs = [
        (source * plan.lon + place, target * plan.lon + place)
        for source, target in zip(sources, targets)
        for place in range(plan.lon)
    ]
    return lax.ppermute(value, ("lat", "lon"), pairs)


def spread(plan, blocks, slots, order):
    for bit in reversed(order):
        for s in sorted(slots):
            slots[s | (1 << bit)] = lon_swap(plan, slots[s], blocks, bit)
    return slots


def gather_sums(plan, blocks, slots, order):
    slots = dict(slots)
    for bit in order:
        sent = [s for s in slots if s >> bit & 1]
        for s in sorted(sent, key=lambda s: -bin(s).count("1")):
            slots[s ^ (1 << bit)] = slots[s ^ (1 << bit)] + lon_swap(plan, slots.pop(s), blocks, bit)
    return spread(plan, blocks, slots, order)


def field_sets(plan):
    sent, kept = [], []
    for at in range(len(plan.roles)):
        bit = at % 2
        sent.append([u for u in range(FIELDS) if u >> bit & 1])
        kept.append([u for u in range(FIELDS) if not u >> bit & 1])
    return sent, kept


def parcel_sums(plan, place, at, blocks, sent, kept):
    first, second = field_sets(plan)
    parts, own = plan.parts, place % plan.parts
    if parts == 1:
        near, far = at % 2, 1 - at % 2
        moved = lon_swap(plan, sent, blocks, near)
        send = kept[1] + moved[1]
        slots = {0: (kept[0] + moved[0]) + lon_swap(plan, send, blocks, far)}
        slots = spread(plan, blocks, slots, [near, far])
        return [slots[u] for u in range(FIELDS)]
    bits = plan.lon.bit_length() - 1
    slots = {}
    for us, array in ((first[at], sent), (second[at], kept)):
        for i, u in enumerate(us):
            pieces = array[i].reshape(parts, -1, LANES)
            for k in range(parts):
                slots[u * parts + k] = pieces[k ^ own]
    order = list(range(bits)) if at % 2 == 0 else list(reversed(range(bits)))
    slots = gather_sums(plan, blocks, slots, order)
    result = []
    for u in range(FIELDS):
        pieces = jnp.stack([slots[u * parts + k] for k in range(parts)])
        result.append(pieces[jnp.arange(parts) ^ own].reshape(-1, LANES))
    return result


def all_sums(plan, place, arrays):
    result = []
    for at in range(len(plan.roles)):
        home = plan.blocks(at)
        for parcel in range(len(plan.parcels(at))):
            first, second = arrays[at, parcel, 0], arrays[at, parcel, 1]
            if parcel == 0:
                result += parcel_sums(plan, place, at, home, first, second)
                continue
            helpers = plan.blocks(at + len(plan.roles))
            first, second = [lat_move(plan, array, home, helpers) for array in (first, second)]
            sums = parcel_sums(plan, place, at, helpers, first, second)
            result += [lat_move(plan, array, helpers, home) for array in sums]
    return result


def body(winds, theta, thick, polar_rows, cutoffs):
    lat, lon = lax.axis_size("lat"), lax.axis_size("lon")
    levels, rows, width = theta.shape
    sizes = (lat, lon, levels, rows, width, polar_rows.shape[0])
    plan = Plan(*sizes)
    t_tabs, i_tabs = [tuple(jnp.asarray(part) for part in pair) for pair in tables(sizes)]
    block, place = lax.axis_index("lat"), lax.axis_index("lon")
    winds = winds.transpose(0, 2, 1, 3)
    theta = theta.transpose(1, 0, 2)
    thick = thick.transpose(1, 0, 2)
    hemi = (block >= lat // 2).astype(jnp.int32)
    role = jnp.where(hemi == 1, lat - 1 - block, block)

    def line(row):
        return jnp.stack([winds[0, row], winds[1, row], theta[row], thick[row]])

    south_pairs = [(b * lon + p, (b + 1) * lon + p) for b in range(lat - 1) for p in range(lon)]
    north_pairs = [(to, at) for at, to in south_pairs]
    top = lax.ppermute(line(rows - 1), ("lat", "lon"), south_pairs)
    bottom = lax.ppermute(line(0), ("lat", "lon"), north_pairs)

    step_rows = max(k for k in range(1, 16) if rows % k == 0)
    listed = polar_rows.shape[0]
    north_run = jnp.sum((polar_rows < plan.total_rows // 2).astype(jnp.int32))
    south_first = plan.total_rows - listed + north_run
    far_row = jnp.where(hemi == 1, south_first, north_run - 1)
    far_at = far_row - block * rows + 1
    far_at = jnp.where((far_at >= 0) & (far_at <= rows + 1), far_at, -1)
    raw_from = jnp.clip(north_run - block * rows, 0, rows)
    raw_to = jnp.clip(south_first - block * rows, 0, rows)
    block_from = jnp.minimum(raw_from, rows - 1) // step_rows
    block_to = jnp.maximum(block_from, jnp.maximum(raw_to - 1, 0) // step_rows)
    above, below = block * rows - 1, (block + 1) * rows

    def is_listed(row):
        return (row >= 0) & (row < plan.total_rows) & ((row < north_run) | (row >= south_first))

    facts = [
        place // plan.parts, place, role, hemi, far_at, is_listed(above), is_listed(below),
        raw_from, raw_to, block_from, block_to,
    ]
    scal = jnp.stack([jnp.asarray(fact).astype(jnp.int32) for fact in facts])

    arrays = forward(plan, 0, scal, winds, theta, thick, top, bottom, t_tabs)
    later = forward(plan, 1, scal, winds, theta, thick, top, bottom, t_tabs)

    first_edge, last_edge = edges(plan, later[plan.arrays()[1][0]], winds, theta, thick)
    west = lax.ppermute(last_edge, "lon", [(i, (i + 1) % lon) for i in range(lon)])
    east = lax.ppermute(first_edge, "lon", [((i + 1) % lon, i) for i in range(lon)])
    added = {key: array for key, array in later.items() if key[2] == 1}
    added, west, east = lax.optimization_barrier((added, west, east))
    arrays = {**arrays, **later, **added}
    sums = all_sums(plan, place, arrays)

    slot_rows = jnp.asarray(plan.slot_rows())[jnp.minimum(role, len(plan.roles) - 1), hemi]
    slot_rows = jnp.where(slot_rows == -2, far_at, slot_rows)
    hits = (polar_rows[None, :] == (slot_rows - 1 + block * rows)[:, None]) & (slot_rows >= 0)[:, None]
    cut = jnp.sum(jnp.where(hits, cutoffs[None, :] + 1, 0), axis=1) - 1
    cuts = jnp.broadcast_to(cut.astype(jnp.int32)[:, None, None], (plan.slots, levels, LANES))
    cuts = cuts.reshape(plan.slots * levels, LANES)

    ring = block * rows - 1 + jnp.arange(rows + 2, dtype=jnp.int32)
    centre = (ring.astype(jnp.float32) + 0.5) * (jnp.pi / plan.total_rows)
    cos, sin = jnp.sin(centre), -jnp.cos(centre)
    mid = cos[1:-1]
    coef = jnp.concatenate([0.025 / mid, 0.1 / mid, 0.05 / mid, 0.3 * sin[1:-1], cos[:-2], cos[2:]])

    out = substep(
        plan, step_rows, scal, coef, winds, theta, thick, west, east, top, bottom, cuts, i_tabs, sums
    )
    return (out[0].transpose(0, 2, 1, 3), out[1].transpose(1, 0, 2), out[2].transpose(1, 0, 2))


def solution(mesh):
    in_specs = (P(None, None, "lat", "lon"), P(None, "lat", "lon"), P(None, "lat", "lon"), P(), P())
    out_specs = (P(None, None, "lat", "lon"), P(None, "lat", "lon"), P(None, "lat", "lon"))
    return jax.shard_map(body, mesh=mesh, in_specs=in_specs, out_specs=out_specs, check_vma=False)
```

```python
import functools

import jax
import jax.numpy as jnp
import ml_dtypes
import numpy as np
from jax import lax
from jax.experimental import pallas as pl
from jax.experimental.pallas import tpu as pltpu
from jax.sharding import PartitionSpec as P

FIELDS = 4
LANES = 128
PIECE = 3
VMEM = 60 * 1024 * 1024


def round_up(value, step):
    return -(-value // step) * step


class Group:
    def __init__(self, first, stop, near, far, blocks, levels, quarters):
        self.first, self.stop, self.blocks, self.levels = first, stop, blocks, levels
        self.near, self.far = int(near), int(far)
        self.own = stop - first
        self.farthest = self.own == 0
        self.slots = 1 if self.farthest else self.own + self.near + self.far
        self.height = self.slots * levels
        self.quarters = list(quarters)
        assert sum(self.quarters) == self.slots
        one, two, three, four = self.quarters
        self.beside = max(one, three) if one and three else 0
        self.half = -(-two // 2)
        self.packed = self.beside > 0 or two > 1
        self.pieces = []
        if self.packed:
            if not self.beside:
                for start, count in ((0, one), (one + two, three)):
                    if count:
                        self.pieces.append((0, start, count))
            if four:
                self.pieces.append((0, one + two + three, four))
        self.whole_rows = sum(piece[2] for piece in self.pieces)
        self.full = self.height * (blocks - 1 if self.packed else blocks)
        self.packed_rows = (self.whole_rows + self.beside + self.half) * levels if self.packed else 0
        self.total = self.full + self.packed_rows
        parts = max(1, round(self.slots / 16))
        self.chunk = -(-self.slots // parts)
        self.parts = -(-self.slots // self.chunk)

    def start(self, hemi, rows):
        return jnp.where(hemi == 1, rows - self.stop + 1 - self.far, self.first + 1 - self.near)

    def chunk_at(self, part):
        return jnp.minimum(part * self.chunk, self.slots - self.chunk)

    def slot(self, hemi, first, count):
        first = min(first, self.slots - count)
        return jnp.where(hemi == 1, self.slots - count - first, first)

    def pairs(self):
        one, two, three, _ = self.quarters
        result = []
        if self.beside:
            result.append((one + two, 0, self.beside, 96))
        if two:
            result.append((one, one + two - self.half, self.half, 64))
        return result

    def pack(self, hemi, last, to):
        row = 0
        for _, first, count in self.pieces:
            to(row, count, last(self.slot(hemi, first, count), count))
            row += count
        for left, right, count, lanes in self.pairs():
            lane = lax.broadcasted_iota(jnp.int32, (count * self.levels, LANES), 1)
            beside = pltpu.roll(last(self.slot(hemi, right, count), count), lanes, 1)
            to(row, count, jnp.where(lane < lanes, last(self.slot(hemi, left, count), count), beside))
            row += count

    def unpack(self, hemi, packed, to):
        row = self.whole_rows
        for left, right, count, lanes in self.pairs():
            value = packed(row, count)
            to(self.slot(hemi, left, count), count, value)
            to(self.slot(hemi, right, count), count, pltpu.roll(value, LANES - lanes, 1))
            row += count
        row = 0
        for _, first, count in self.pieces:
            to(self.slot(hemi, first, count), count, packed(row, count))
            row += count


class Plan:
    def __init__(self, lat, lon, levels, rows, width, listed):
        self.lat, self.lon, self.levels, self.rows, self.width = lat, lon, levels, rows, width
        self.total_rows, self.length = lat * rows, lon * width
        self.parts = lon // FIELDS
        self.wide = round_up(width + 2, LANES)
        pole = listed // 2
        self.low, self.high = pole - pole // 4, pole + pole // 4
        top = self.length // 4 - 1

        def blocks_of(depth):
            return -(-(2 * min(2 * (depth + 1), top) + 1) // LANES)

        self.roles = []
        last = self.high - 2
        for role in range(lat // 2):
            start = role * rows
            if start > last:
                break
            need = {}
            for depth in range(start, min(start + rows - 1, last) + 1):
                need.setdefault(blocks_of(depth), []).append(depth - start)
            spans = [[need[k][0], need[k][-1] + 1, False, False, k] for k in sorted(need)]
            if role > 0:
                spans[0][2], spans[0][4] = True, max(spans[0][4], blocks_of(start - 1))
            if start + rows <= last:
                spans[-1][3], spans[-1][4] = True, max(spans[-1][4], blocks_of(start + rows))
            groups = []
            for first, stop, near, far, blocks in spans:
                depths = range(start + first - int(near), start + stop + int(far))
                quarters = [0] * 4
                for depth in depths:
                    lanes = 2 * min(2 * (depth + 1), top) + 1 - (blocks - 1) * LANES
                    quarters[max(0, -(-lanes // (LANES // 4)) - 1)] += 1
                groups.append(Group(first, stop, near, far, blocks, levels, quarters))
            groups.append(Group(0, 0, False, False, -(-(2 * top + 1) // LANES), levels, (0, 0, 0, 1)))
            self.roles.append(groups)
        self.slots = max(sum(group.slots for group in groups) for groups in self.roles)
        self.table = LANES * max(group.blocks for groups in self.roles for group in groups)
        count = len(self.roles)
        self.lent = {}
        if self.parts == 1 and 2 * count <= lat // 2:
            self.lent = {count - 1: len(self.roles[-1]) - 2}

    def blocks(self, role):
        return (role, self.lat - 1 - role)

    def parcels(self, at):
        indices = range(len(self.roles[at]))
        away = self.lent.get(at)
        home = [g for g in indices if g != away]
        return [home] if away is None else [home, [away]]

    def arrays(self):
        calls = [[], []]
        for at in range(len(self.roles)):
            if at in self.lent:
                calls[0] += [(at, 1, 0), (at, 1, 1)]
                calls[1] += [(at, 0, 0), (at, 0, 1)]
            else:
                calls[0].append((at, 0, 0))
                calls[1].append((at, 0, 1))
        return calls

    def places(self):
        result, number = {}, 0
        for at in range(len(self.roles)):
            for parcel in self.parcels(at):
                offset = 0
                for g in parcel:
                    result[at, g] = (number, offset)
                    offset += self.roles[at][g].total
                number += 1
        return result

    def height_of(self, at, parcel):
        return sum(self.roles[at][g].total for g in self.parcels(at)[parcel])

    def heights(self):
        return [
            self.height_of(at, parcel) for at in range(len(self.roles)) for parcel in range(len(self.parcels(at)))
        ]

    def slot_rows(self):
        table = np.full((len(self.roles), 2, self.slots), -1, np.int32)
        for at, groups in enumerate(self.roles):
            for hemi in range(2):
                rows = []
                for group in groups:
                    first = group.first + 1 - group.near if hemi == 0 else self.rows - group.stop + 1 - group.far
                    rows += [-2] if group.farthest else [first + k for k in range(group.slots)]
                table[at, hemi, : len(rows)] = rows
        return table


def split_table(table):
    high = table.astype(ml_dtypes.bfloat16)
    low = (table - high.astype(np.float64)).astype(ml_dtypes.bfloat16)
    return high, low


@functools.lru_cache(maxsize=None)
def tables(sizes):
    plan = Plan(*sizes)
    index = np.arange(plan.table)
    wave, odd = (index + 1) // 2, (index % 2 == 0) & (index > 0)
    used = wave < plan.length // 4
    points = np.zeros(plan.wide, np.int64)
    points[: plan.width + 1] = np.arange(plan.width + 1)
    points[-1] = -1
    shown = np.zeros(plan.wide, bool)
    shown[: plan.width + 1] = True
    shown[-1] = True

    def trig(at):
        angle = (wave[:, None] * at[None, :]) % plan.length * (2.0 * np.pi / plan.length)
        return np.where(odd[:, None], np.sin(angle), np.cos(angle)) * used[:, None]

    weight = np.where(wave == 0, 1.0, 2.0) / plan.length
    forward, inverse = [], []
    for place in range(plan.lon):
        forward.append(trig(place * plan.width + np.arange(plan.width)).T)
        inverse.append(trig(place * plan.width + points) * weight[:, None] * shown[None, :])
    shape = (plan.lon, plan.width, plan.table // LANES, LANES)
    forward = np.stack(forward).reshape(shape).transpose(0, 2, 1, 3)
    inverse = np.stack(inverse).reshape(plan.lon, plan.table // LANES, LANES, plan.wide)
    return split_table(forward), split_table(inverse)


def fetch_table(place, tabs, held, sems, blocks):
    return [
        pltpu.make_async_copy(tab.at[place, b], held.at[b, k], sems.at[b, k])
        for b in blocks
        for k, tab in enumerate(tabs)
    ]


def split(value):
    high = value.astype(jnp.bfloat16)
    low = (value - high.astype(jnp.float32)).astype(jnp.bfloat16)
    return high, low


def dot(left, right):
    return jnp.dot(left, right, preferred_element_type=jnp.float32)


def three_pass_out(left, right):
    columns = right[0].shape[1]
    both = dot(left[0], jnp.concatenate(right, axis=1))
    return both[:, :columns] + (both[:, columns:] + dot(left[1], right[0]))


def three_pass_in(value, table):
    terms = []
    for at in range(0, value.shape[1], LANES):
        high, low = split(value[:, at : at + LANES])
        terms += [high, low, high]
    return dot(jnp.concatenate(terms, axis=1), table)


def forward_kernel(plan, call, scal, winds, theta, thick, top, bottom, t_high, t_low, *refs):
    places, sets, arrays = plan.places(), field_sets(plan), plan.arrays()[call]
    outs, (points, spectra, held, in_sems, out_sems, t_sems) = refs[: len(arrays)], refs[len(arrays) :]
    levels, width = plan.levels, plan.width
    hemi = scal[3]
    for at, groups in enumerate(plan.roles):

        @pl.when(scal[2] == at)
        def _(at=at, groups=groups):
            mine = [(number, array[1:]) for number, array in enumerate(arrays) if array[0] == at]
            order = [g for g in range(len(groups)) if any(g in plan.parcels(at)[a[0]] for _, a in mine)]
            targets = {}
            for g in order:
                targets[g] = [
                    (number, i, u)
                    for number, (parcel, which) in mine
                    if g in plan.parcels(at)[parcel]
                    for i, u in enumerate(sets[which][at])
                ]
            some_fields = {g: [u ^ scal[0] for _, _, u in targets[g]] for g in order}
            turn_of = {g: n % 2 for n, g in enumerate(order)}
            ready = 0

            def first_row(group):
                if group.farthest:
                    return jnp.clip(scal[4] - 1, 0, plan.rows - 1), 0, 1
                first = jnp.where(hemi == 1, plan.rows - group.stop, group.first)
                return first, jnp.where(hemi == 1, group.far, group.near), group.own

            def fetch(g):
                first, slot, count = first_row(groups[g])
                for i, field in enumerate(some_fields[g]):

                    def pieces(source, i=i):
                        for k in range(0, count, PIECE):
                            size = min(PIECE, count - k)
                            pltpu.make_async_copy(
                                source.at[pl.ds(first + k, size)],
                                points.at[turn_of[g], i, pl.ds(slot + k, size)],
                                in_sems.at[turn_of[g], i],
                            ).start()

                    pl.when(field < 2)(lambda: pieces(winds.at[jnp.minimum(field, 1)]))
                    pl.when(field == 2)(lambda: pieces(theta))
                    pl.when(field == 3)(lambda: pieces(thick))

            def arrive(g):
                first, slot, count = first_row(groups[g])
                for i in range(len(targets[g])):
                    pltpu.make_async_copy(
                        theta.at[pl.ds(first, count)],
                        points.at[turn_of[g], i, pl.ds(slot, count)],
                        in_sems.at[turn_of[g], i],
                    ).wait()

            def leave(g, parts):
                group, turn, copies = groups[g], turn_of[g], []
                _, offset = places[at, g]
                size = group.full // parts
                for i, (number, place, _) in enumerate(targets[g]):
                    for k in range(parts if group.full else 0):
                        copies.append(
                            pltpu.make_async_copy(
                                spectra.at[turn, i, pl.ds(k * size, size)],
                                outs[number].at[place, pl.ds(offset + k * size, size)],
                                out_sems.at[turn, i, 0],
                            )
                        )
                    if group.packed:
                        copies.append(
                            pltpu.make_async_copy(
                                spectra.at[turn, i, pl.ds(group.blocks * group.height, group.packed_rows)],
                                outs[number].at[place, pl.ds(offset + group.full, group.packed_rows)],
                                out_sems.at[turn, i, 1],
                            )
                        )
                return copies

            def pack(g, i):
                group, turn = groups[g], turn_of[g]

                def last(slot, count):
                    at_row = pl.multiple_of((group.blocks - 1) * group.height + slot * levels, 8)
                    return spectra[turn, i, pl.ds(at_row, count * levels), :]

                def to(row, count, value):
                    at_row = group.blocks * group.height + row * levels
                    spectra[turn, i, at_row : at_row + count * levels, :] = value

                group.pack(hemi, last, to)

            def halo(g, slot, line, wanted):
                @pl.when(wanted)
                def _():
                    for i, field in enumerate(some_fields[g]):
                        points[turn_of[g], i, slot] = line[field]

            fetch(order[0])
            needed = range(max(groups[g].blocks for g in order))
            for copy in fetch_table(scal[1], (t_high, t_low), held, t_sems, needed):
                copy.start()
            for n, g in enumerate(order):
                group = groups[g]
                if n + 1 < len(order):
                    fetch(order[n + 1])
                arrive(g)
                for copy in fetch_table(scal[1], (t_high, t_low), held, t_sems, range(ready, group.blocks)):
                    copy.wait()
                ready = max(ready, group.blocks)
                if group.farthest:
                    halo(g, 0, top, scal[4] == 0)
                    halo(g, 0, bottom, scal[4] == plan.rows + 1)
                if group.near:
                    halo(g, 0, top, hemi == 0)
                    halo(g, group.slots - 1, bottom, hemi == 1)
                if group.far:
                    halo(g, group.slots - 1, bottom, hemi == 0)
                    halo(g, 0, top, hemi == 1)
                if n >= 2:
                    for copy in leave(order[n - 2], 1):
                        copy.wait()

                def transform(value, group=group):
                    return three_pass_out(
                        split(value),
                        [
                            jnp.concatenate([held[b, half] for b in range(group.blocks)], axis=1)
                            for half in range(2)
                        ],
                    )

                if group.farthest:
                    spec = transform(points[turn_of[g], : len(targets[g]), 0].reshape(len(targets[g]) * levels, width))
                    for i in range(len(targets[g])):
                        for b in range(group.blocks):
                            spectra[turn_of[g], i, b * levels : (b + 1) * levels, :] = spec[
                                i * levels : (i + 1) * levels, b * LANES : (b + 1) * LANES
                            ]
                else:

                    def part(n, _, g=g, group=group, transform=transform):
                        i, slot = n // group.parts, group.chunk_at(lax.rem(n, group.parts))
                        size = group.chunk * levels
                        spec = transform(points[turn_of[g], i, pl.ds(slot, group.chunk)].reshape(size, width))
                        for b in range(group.blocks):
                            target = pl.multiple_of(b * group.height + slot * levels, 8)
                            spectra[turn_of[g], i, pl.ds(target, size), :] = spec[:, b * LANES : (b + 1) * LANES]
                        return 0

                    lax.fori_loop(0, len(targets[g]) * group.parts, part, 0)
                if group.packed:
                    lax.fori_loop(0, len(targets[g]), lambda i, _, g=g: (pack(g, i), 0)[1], 0)
                for copy in leave(g, max(1, group.full // group.height)):
                    copy.start()
            for g in order[-2:]:
                for copy in leave(g, 1):
                    copy.wait()


def forward(plan, call, scal, winds, theta, thick, top, bottom, tabs):
    arrays = plan.arrays()[call]
    count = FIELDS if plan.lent else FIELDS // 2
    shapes = [(FIELDS // 2, plan.height_of(at, parcel), LANES) for at, parcel, _ in arrays]
    anywhere = pl.BlockSpec(memory_space=pl.ANY)
    halo = pl.BlockSpec((FIELDS, plan.levels, plan.width), lambda i, s: (0, 0, 0))
    slots = max(group.slots for groups in plan.roles for group in groups)
    total = max(group.height * group.blocks + group.packed_rows for groups in plan.roles for group in groups)
    outs = pl.pallas_call(
        functools.partial(forward_kernel, plan, call),
        grid_spec=pltpu.PrefetchScalarGridSpec(
            num_scalar_prefetch=1,
            grid=(1,),
            in_specs=[anywhere] * 3 + [halo, halo, anywhere, anywhere],
            out_specs=[anywhere] * len(arrays),
            scratch_shapes=[
                pltpu.VMEM((2, count, slots, plan.levels, plan.width), jnp.float32),
                pltpu.VMEM((2, count, total, LANES), jnp.float32),
                pltpu.VMEM((plan.table // LANES, 2, plan.width, LANES), jnp.bfloat16),
                pltpu.SemaphoreType.DMA((2, count)),
                pltpu.SemaphoreType.DMA((2, count, 2)),
                pltpu.SemaphoreType.DMA((plan.table // LANES, 2)),
            ],
        ),
        out_shape=[jax.ShapeDtypeStruct(shape, jnp.float32) for shape in shapes],
        compiler_params=pltpu.CompilerParams(vmem_limit_bytes=VMEM),
        cost_estimate=pl.CostEstimate(
            flops=6 * max(shape[1] for shape in shapes) * count * LANES * plan.width, bytes_accessed=15_000_000, transcendentals=0
        ),
        name="partial_spectra",
    )(scal, winds, theta, thick, top, bottom, *tabs)
    return dict(zip(arrays, outs))


def edge_kernel(plan, count, _, *refs):
    ins, outs = refs[:-2], refs[-2:]
    lane = lax.broadcasted_iota(jnp.int32, (plan.levels, LANES), 1)
    some = plan.rows // count
    for side, column in enumerate((0, (plan.width - 1) % LANES)):
        kept = (jnp.zeros((plan.levels, LANES), jnp.float32),) * FIELDS
        for piece in range(count):
            at = (side * count + piece) * FIELDS
            fields = ins[at : at + FIELDS]

            def pick(row, kept, fields=fields, piece=piece, column=column):
                values = (fields[0][0, row], fields[1][0, row], fields[2][row], fields[3][row])
                return tuple(
                    jnp.where(lane == row + piece * some, value[:, column : column + 1], old)
                    for value, old in zip(values, kept)
                )

            kept = lax.fori_loop(0, some, pick, kept, unroll=max(k for k in range(1, 11) if some % k == 0))
        for field in range(FIELDS):
            outs[side][field] = kept[field]


def edges(plan, after, winds, theta, thick):
    count = 3 if plan.rows % 3 == 0 else 1
    some = plan.rows // count
    specs = []
    for at in (0, (plan.width - 1) // LANES):
        for piece in range(count):
            for wind in range(2):
                specs.append(
                    pl.BlockSpec(
                        (1, some, plan.levels, LANES), lambda i, w=wind, p=piece, at=at: (w, p, 0, at)
                    )
                )
            specs += [pl.BlockSpec((some, plan.levels, LANES), lambda i, p=piece, at=at: (p, 0, at))] * 2
    shape = (FIELDS, plan.levels, LANES)
    return pl.pallas_call(
        functools.partial(edge_kernel, plan, count),
        grid=(1,),
        in_specs=[pl.BlockSpec(memory_space=pl.ANY)] + specs,
        out_specs=[pl.BlockSpec(shape, lambda i: (0, 0, 0))] * 2,
        out_shape=[jax.ShapeDtypeStruct(shape, jnp.float32)] * 2,
        compiler_params=pltpu.CompilerParams(vmem_limit_bytes=VMEM),
        cost_estimate=pl.CostEstimate(flops=0, bytes_accessed=6_000_000, transcendentals=0),
        name="edge_columns",
    )(after, *[winds, winds, theta, thick] * (2 * count))


def step_kernel(plan, step_rows, scal, coef, west, east, top, bottom, cuts, i_high, i_low, *refs):
    places, heights = plan.places(), plan.heights()
    halves = plan.levels // 8
    raw, refs = refs[: FIELDS * halves], refs[FIELDS * halves :]
    spectra = refs[: FIELDS * len(heights)]
    new_wind, new_theta, new_thick, held, sums, unpacked, table, ready, sems, t_sems, out_sems = refs[FIELDS * len(heights) :]
    step = pl.program_id(0)
    rows, width, wide, levels = plan.rows, plan.width, plan.wide, plan.levels
    last_step = rows // step_rows

    def inverse(at, groups):
        slot_at = np.cumsum([0] + [group.slots for group in groups])
        row_at = np.cumsum([0] + [group.total for group in groups])

        def copies(g):
            number, offset = places[at, g]
            return [
                pltpu.make_async_copy(
                    spectra[number * FIELDS + u].at[pl.ds(offset, groups[g].total)],
                    sums.at[u, pl.ds(int(row_at[g]), groups[g].total)],
                    sems.at[g, u],
                )
                for u in range(FIELDS)
            ]

        have = 0
        for g, group in enumerate(groups):
            for copy in copies(g):
                copy.start()
            for copy in fetch_table(scal[1], (i_high, i_high, i_low), table, t_sems, range(have, group.blocks)):
                copy.start()
            have = max(have, group.blocks)
        have = 0
        for g, group in enumerate(groups):
            for copy in copies(g):
                copy.wait()
            for copy in fetch_table(scal[1], (i_high, i_high, i_low), table, t_sems, range(have, group.blocks)):
                copy.wait()
            have = max(have, group.blocks)
            lanes = group.blocks * LANES
            first_slot, first_sum = int(slot_at[g]), int(row_at[g])

            def back_of(spec, size, lanes=lanes, group=group):
                back = three_pass_in(spec, table[: group.blocks].reshape(3 * lanes, wide))
                return back.reshape(size, levels, wide)

            def masked(u, slot, size, group=group, first_slot=first_slot, first_sum=first_sum):
                rows_at = pl.ds(pl.multiple_of((first_slot + slot) * levels, 8), size)
                cut = cuts[rows_at, :]
                lane = lax.broadcasted_iota(jnp.int32, (size, LANES), 1)
                pieces = []
                for b in range(group.blocks):
                    keep = lax.shift_right_logical(lane + (b * LANES + 1), 1) <= cut
                    if group.packed and b == group.blocks - 1:
                        value = unpacked[u, pl.ds(pl.multiple_of(slot * levels, 8), size), :]
                    else:
                        source = pl.multiple_of(first_sum + b * group.height + slot * levels, 8)
                        value = sums[u, pl.ds(source, size), :]
                    pieces.append(jnp.where(keep, value, 0.0))
                return jnp.concatenate(pieces, axis=1)

            def unpack(u, _, group=group, first_sum=first_sum):
                def packed(row, count):
                    at_row = first_sum + group.full + row * levels
                    return sums[u, at_row : at_row + count * levels, :]

                def to(slot, count, value):
                    at_row = pl.multiple_of(slot * levels, 8)
                    unpacked[u, pl.ds(at_row, count * levels), :] = value

                group.unpack(scal[3], packed, to)
                return 0

            if group.packed:
                lax.fori_loop(0, FIELDS, unpack, 0)
            if group.farthest:
                spec = jnp.concatenate([masked(u, 0, levels) for u in range(FIELDS)], axis=0)
                back = back_of(spec, FIELDS)

                @pl.when(scal[4] >= 0)
                def _(back=back):
                    for u in range(FIELDS):
                        held[u ^ scal[0], scal[4]] = back[u]
            else:
                start = group.start(scal[3], rows)

                def part(n, _, group=group, start=start, masked=masked, back_of=back_of):
                    u, slot = n // group.parts, group.chunk_at(lax.rem(n, group.parts))
                    back = back_of(masked(u, slot, group.chunk * levels), group.chunk)
                    held[u ^ scal[0], pl.ds(start + slot, group.chunk)] = back
                    return 0

                lax.fori_loop(0, FIELDS * group.parts, part, 0)

    @pl.when(step == 0)
    def _():
        for at, groups in enumerate(plan.roles):
            pl.when(scal[2] == at)(functools.partial(inverse, at, groups))
        for side, line in enumerate((top, bottom)):

            @pl.when(scal[5 + side] == 0)
            def _(side=side, line=line):
                for field in range(FIELDS):
                    held[field, side * (rows + 1), :, :width] = line[field]

    base = step * step_rows
    tail = width % LANES

    @pl.when(step < last_step)
    def _():
        lane = lax.broadcasted_iota(jnp.int32, (levels, LANES), 1)

        def load(n, _):
            at = n
            row = base + n
            is_raw = (row >= scal[7]) & (row < scal[8])
            for field in range(FIELDS):
                for half in range(halves):
                    piece = raw[field * halves + half]
                    some = slice(half * 8, half * 8 + 8)
                    value = piece[0, at] if field < 2 else piece[at]
                    held[field, row + 1, some, :width] = jnp.where(
                        is_raw, value, held[field, row + 1, some, :width]
                    )
                beyond = jnp.where(
                    lane == tail,
                    pltpu.roll(east[field], (tail + LANES - row) & (LANES - 1), 1),
                    pltpu.roll(west[field], (2 * LANES - 1 - row) & (LANES - 1), 1),
                )
                held[field, row + 1, :, width:] = jnp.where(
                    is_raw, beyond[:, tail:], held[field, row + 1, :, width:]
                )
            return 0

        @pl.when((base < scal[8]) & (base + step_rows > scal[7]))
        def _():
            lax.fori_loop(0, step_rows, load, 0, unroll=3 if step_rows % 3 == 0 else 1)

    slot = step % 2
    count = wide // LANES
    lane = lax.broadcasted_iota(jnp.int32, (8, LANES), 1)
    is_first, is_last = lane == 0, lane == LANES - 1

    def stencil(row, _):
        at = base - step_rows + row
        along, across, push, turn, cos_north, cos_south = [coef[k * rows + at] for k in range(6)]
        across_north, across_south = across * cos_north, across * cos_south
        for part in range(levels // 8):
            some = pl.ds(part * 8, 8)

            def load(field, shift, k):
                return held[field, at + shift, some, k * LANES : (k + 1) * LANES]

            here = [
                functools.lru_cache(maxsize=None)(lambda k, field=field: load(field, 1, k))
                for field in range(FIELDS)
            ]
            up = [functools.lru_cache(maxsize=None)(lambda k, f=f: pltpu.roll(f(k), LANES - 1, 1)) for f in here]
            down = [functools.lru_cache(maxsize=None)(lambda k, f=f: pltpu.roll(f(k), 1, 1)) for f in here]

            def shifted(which, k):
                return (
                    jnp.where(is_last, up[which]((k + 1) % count), up[which](k)),
                    jnp.where(is_first, down[which]((k - 1) % count), down[which](k)),
                )

            for k in range(count):
                stop = min(width, (k + 1) * LANES)

                def put(field, piece, k=k, stop=stop):
                    ready[slot, field, row, some, k * LANES : stop] = piece[:, : stop - k * LANES]

                u, v, t, h = [here[field](k) for field in range(FIELDS)]
                advect, carry = along * u, 0.1 * v
                (u_e, u_w), (v_e, v_w), (t_e, t_w), (h_e, h_w) = [shifted(field, k) for field in range(FIELDS)]
                v_n, v_s, h_n, h_s = load(1, 0, k), load(1, 2, k), load(3, 0, k), load(3, 2, k)
                put(
                    3,
                    h
                    - along * (u_e * h_e - u_w * h_w)
                    - (across_south * (v_s * h_s) - across_north * (v_n * h_n)),
                )
                put(
                    1,
                    v
                    - advect * (v_e - v_w)
                    - carry * (v_s - v_n)
                    - 0.15 * (h_s - h_n)
                    - turn * u,
                )
                put(
                    0,
                    u
                    - advect * (u_e - u_w)
                    - carry * (load(0, 2, k) - load(0, 0, k))
                    - push * (h_e - h_w)
                    + turn * v,
                )
                put(2, t - advect * (t_e - t_w) - carry * (load(2, 2, k) - load(2, 0, k)))
        return 0

    outs = (new_wind.at[0], new_wind.at[1], new_theta, new_thick)

    def leave(at_step, size, act):
        for field, out in enumerate(outs):
            for k in range(0, step_rows, size):
                act(
                    pltpu.make_async_copy(
                        ready.at[at_step % 2, field, pl.ds(k, size)],
                        out.at[pl.ds((at_step - 1) * step_rows + k, size)],
                        out_sems.at[at_step % 2, field],
                    )
                )

    @pl.when(step > 2)
    def _():
        leave(step - 2, step_rows, lambda copy: copy.wait())

    @pl.when(step > 0)
    def _():
        lax.fori_loop(0, step_rows, stencil, 0)
        leave(step, PIECE if step_rows % PIECE == 0 else step_rows, lambda copy: copy.start())

    @pl.when(step == last_step)
    def _():
        if last_step > 1:
            leave(step - 1, step_rows, lambda copy: copy.wait())
        leave(step, step_rows, lambda copy: copy.wait())


def substep(plan, step_rows, scal, coef, winds, theta, thick, west, east, top, bottom, cuts, tabs, spectra):
    rows, width, levels = plan.rows, plan.width, plan.levels
    once = pl.Buffered(1)
    steps = rows // step_rows

    def block(i, s):
        return jnp.clip(i, s[9], s[10])

    def whole(shape):
        return pl.BlockSpec(shape, lambda i, s: (0,) * len(shape), pipeline_mode=once)

    anywhere = pl.BlockSpec(memory_space=pl.ANY)
    halves = range(levels // 8)
    raw_specs = [
        pl.BlockSpec((1, step_rows, 8, width), lambda i, s, w=wind, h=half: (w, block(i, s), h, 0))
        for wind in range(2)
        for half in halves
    ] + [
        pl.BlockSpec((step_rows, 8, width), lambda i, s, h=half: (block(i, s), h, 0))
        for _ in range(2)
        for half in halves
    ]
    raw = [array for array in (winds, winds, theta, thick) for _ in halves]
    edge, halo = (FIELDS, levels, LANES), (FIELDS, levels, width)
    in_specs = [
        pl.BlockSpec(memory_space=pltpu.SMEM),
        whole(edge),
        whole(edge),
        whole(halo),
        whole(halo),
        whole((plan.slots * levels, LANES)),
        anywhere,
        anywhere,
    ] + raw_specs + [anywhere] * len(spectra)
    shapes = [(2, rows, levels, width)] + [(rows, levels, width)] * 2
    most = max(sum(group.total for group in groups) for groups in plan.roles)
    return pl.pallas_call(
        functools.partial(step_kernel, plan, step_rows),
        grid_spec=pltpu.PrefetchScalarGridSpec(
            num_scalar_prefetch=1,
            grid=(steps + 1,),
            in_specs=in_specs,
            out_specs=[anywhere] * 3,
            scratch_shapes=[
                pltpu.VMEM((FIELDS, rows + 2, levels, plan.wide), jnp.float32),
                pltpu.VMEM((FIELDS, most, LANES), jnp.float32),
                pltpu.VMEM((FIELDS, max(group.height for groups in plan.roles for group in groups), LANES), jnp.float32),
                pltpu.VMEM((plan.table // LANES, 3, LANES, plan.wide), jnp.bfloat16),
                pltpu.VMEM((2, FIELDS, step_rows, levels, width), jnp.float32),
                pltpu.SemaphoreType.DMA((max(len(groups) for groups in plan.roles), FIELDS)),
                pltpu.SemaphoreType.DMA((plan.table // LANES, 3)),
                pltpu.SemaphoreType.DMA((2, FIELDS)),
            ],
        ),
        out_shape=[jax.ShapeDtypeStruct(shape, jnp.float32) for shape in shapes],
        compiler_params=pltpu.CompilerParams(vmem_limit_bytes=VMEM),
        cost_estimate=pl.CostEstimate(
            flops=6 * most * FIELDS * LANES * plan.wide, bytes_accessed=40_000_000, transcendentals=0
        ),
        name="inverse_and_substep",
    )(scal, coef, west, east, top, bottom, cuts, *tabs, *raw, *spectra)


def lon_swap(plan, value, blocks, bit):
    pairs = [
        (block * plan.lon + place, block * plan.lon + (place ^ (1 << bit)))
        for block in blocks
        for place in range(plan.lon)
    ]
    return lax.ppermute(value, ("lat", "lon"), pairs)


def lat_move(plan, value, sources, targets):
    pairs = [
        (source * plan.lon + place, target * plan.lon + place)
        for source, target in zip(sources, targets)
        for place in range(plan.lon)
    ]
    return lax.ppermute(value, ("lat", "lon"), pairs)


def spread(plan, blocks, slots, order):
    for bit in reversed(order):
        for s in sorted(slots):
            slots[s | (1 << bit)] = lon_swap(plan, slots[s], blocks, bit)
    return slots


def gather_sums(plan, blocks, slots, order):
    slots = dict(slots)
    for bit in order:
        sent = [s for s in slots if s >> bit & 1]
        for s in sorted(sent, key=lambda s: -bin(s).count("1")):
            slots[s ^ (1 << bit)] = slots[s ^ (1 << bit)] + lon_swap(plan, slots.pop(s), blocks, bit)
    return spread(plan, blocks, slots, order)


def field_sets(plan):
    sent, kept = [], []
    for at in range(len(plan.roles)):
        bit = at % 2
        sent.append([u for u in range(FIELDS) if u >> bit & 1])
        kept.append([u for u in range(FIELDS) if not u >> bit & 1])
    return sent, kept


def parcel_sums(plan, place, at, blocks, sent, kept):
    first, second = field_sets(plan)
    parts, own = plan.parts, place % plan.parts
    if parts == 1:
        near, far = at % 2, 1 - at % 2
        moved = lon_swap(plan, sent, blocks, near)
        send = kept[1] + moved[1]
        slots = {0: (kept[0] + moved[0]) + lon_swap(plan, send, blocks, far)}
        slots = spread(plan, blocks, slots, [near, far])
        return [slots[u] for u in range(FIELDS)]
    bits = plan.lon.bit_length() - 1
    slots = {}
    for us, array in ((first[at], sent), (second[at], kept)):
        for i, u in enumerate(us):
            pieces = array[i].reshape(parts, -1, LANES)
            for k in range(parts):
                slots[u * parts + k] = pieces[k ^ own]
    order = list(range(bits)) if at % 2 == 0 else list(reversed(range(bits)))
    slots = gather_sums(plan, blocks, slots, order)
    result = []
    for u in range(FIELDS):
        pieces = jnp.stack([slots[u * parts + k] for k in range(parts)])
        result.append(pieces[jnp.arange(parts) ^ own].reshape(-1, LANES))
    return result


def all_sums(plan, place, arrays):
    result = []
    for at in range(len(plan.roles)):
        home = plan.blocks(at)
        for parcel in range(len(plan.parcels(at))):
            first, second = arrays[at, parcel, 0], arrays[at, parcel, 1]
            if parcel == 0:
                result += parcel_sums(plan, place, at, home, first, second)
                continue
            helpers = plan.blocks(at + len(plan.roles))
            first, second = [lat_move(plan, array, home, helpers) for array in (first, second)]
            sums = parcel_sums(plan, place, at, helpers, first, second)
            result += [lat_move(plan, array, helpers, home) for array in sums]
    return result


def body(winds, theta, thick, polar_rows, cutoffs):
    lat, lon = lax.axis_size("lat"), lax.axis_size("lon")
    levels, rows, width = theta.shape
    sizes = (lat, lon, levels, rows, width, polar_rows.shape[0])
    plan = Plan(*sizes)
    t_tabs, i_tabs = [tuple(jnp.asarray(part) for part in pair) for pair in tables(sizes)]
    block, place = lax.axis_index("lat"), lax.axis_index("lon")
    winds = winds.transpose(0, 2, 1, 3)
    theta = theta.transpose(1, 0, 2)
    thick = thick.transpose(1, 0, 2)
    hemi = (block >= lat // 2).astype(jnp.int32)
    role = jnp.where(hemi == 1, lat - 1 - block, block)

    def line(row):
        return jnp.stack([winds[0, row], winds[1, row], theta[row], thick[row]])

    south_pairs = [(b * lon + p, (b + 1) * lon + p) for b in range(lat - 1) for p in range(lon)]
    north_pairs = [(to, at) for at, to in south_pairs]
    top = lax.ppermute(line(rows - 1), ("lat", "lon"), south_pairs)
    bottom = lax.ppermute(line(0), ("lat", "lon"), north_pairs)

    step_rows = max(k for k in range(1, 16) if rows % k == 0)
    listed = polar_rows.shape[0]
    north_run = jnp.sum((polar_rows < plan.total_rows // 2).astype(jnp.int32))
    south_first = plan.total_rows - listed + north_run
    far_row = jnp.where(hemi == 1, south_first, north_run - 1)
    far_at = far_row - block * rows + 1
    far_at = jnp.where((far_at >= 0) & (far_at <= rows + 1), far_at, -1)
    raw_from = jnp.clip(north_run - block * rows, 0, rows)
    raw_to = jnp.clip(south_first - block * rows, 0, rows)
    block_from = jnp.minimum(raw_from, rows - 1) // step_rows
    block_to = jnp.maximum(block_from, jnp.maximum(raw_to - 1, 0) // step_rows)
    above, below = block * rows - 1, (block + 1) * rows

    def is_listed(row):
        return (row >= 0) & (row < plan.total_rows) & ((row < north_run) | (row >= south_first))

    facts = [
        place // plan.parts, place, role, hemi, far_at, is_listed(above), is_listed(below),
        raw_from, raw_to, block_from, block_to,
    ]
    scal = jnp.stack([jnp.asarray(fact).astype(jnp.int32) for fact in facts])

    arrays = forward(plan, 0, scal, winds, theta, thick, top, bottom, t_tabs)
    scal, arrays = lax.optimization_barrier((scal, arrays))
    later = forward(plan, 1, scal, winds, theta, thick, top, bottom, t_tabs)

    first_edge, last_edge = edges(plan, later[plan.arrays()[1][0]], winds, theta, thick)
    some = [b for b in range(lat) if (min(b, lat - 1 - b) + 1) * rows > plan.low]
    east_pairs = [(b * lon + i, b * lon + (i + 1) % lon) for b in some for i in range(lon)]
    west = lax.ppermute(last_edge, ("lat", "lon"), east_pairs)
    east = lax.ppermute(first_edge, ("lat", "lon"), [(to, at) for at, to in east_pairs])
    added = {key: array for key, array in later.items() if key[2] == 1}
    added, west, east = lax.optimization_barrier((added, west, east))
    arrays = {**arrays, **later, **added}
    sums = all_sums(plan, place, arrays)

    slot_rows = jnp.asarray(plan.slot_rows())[jnp.minimum(role, len(plan.roles) - 1), hemi]
    slot_rows = jnp.where(slot_rows == -2, far_at, slot_rows)
    hits = (polar_rows[None, :] == (slot_rows - 1 + block * rows)[:, None]) & (slot_rows >= 0)[:, None]
    cut = jnp.sum(jnp.where(hits, cutoffs[None, :] + 1, 0), axis=1) - 1
    cuts = jnp.broadcast_to(cut.astype(jnp.int32)[:, None, None], (plan.slots, levels, LANES))
    cuts = cuts.reshape(plan.slots * levels, LANES)

    ring = block * rows - 1 + jnp.arange(rows + 2, dtype=jnp.int32)
    centre = (ring.astype(jnp.float32) + 0.5) * (jnp.pi / plan.total_rows)
    cos, sin = jnp.sin(centre), -jnp.cos(centre)
    mid = cos[1:-1]
    coef = jnp.concatenate([0.025 / mid, 0.1 / mid, 0.05 / mid, 0.3 * sin[1:-1], cos[:-2], cos[2:]])

    out = substep(
        plan, step_rows, scal, coef, winds, theta, thick, west, east, top, bottom, cuts, i_tabs, sums
    )
    return (out[0].transpose(0, 2, 1, 3), out[1].transpose(1, 0, 2), out[2].transpose(1, 0, 2))


def solution(mesh):
    in_specs = (P(None, None, "lat", "lon"), P(None, "lat", "lon"), P(None, "lat", "lon"), P(), P())
    out_specs = (P(None, None, "lat", "lon"), P(None, "lat", "lon"), P(None, "lat", "lon"))
    return jax.shard_map(body, mesh=mesh, in_specs=in_specs, out_specs=out_specs, check_vma=False)
```

```python
import functools

import jax
import jax.numpy as jnp
import ml_dtypes
import numpy as np
from jax import lax
from jax.experimental import pallas as pl
from jax.experimental.pallas import tpu as pltpu
from jax.sharding import PartitionSpec as P

FIELDS = 4
LANES = 128
PIECE = 3
VMEM = 60 * 1024 * 1024
FORWARD_COST, EDGE_COST = 5_000_000_000, 5_000_000_000


def round_up(value, step):
    return -(-value // step) * step


class Group:
    def __init__(self, first, stop, near, far, blocks, levels, quarters):
        self.first, self.stop, self.blocks, self.levels = first, stop, blocks, levels
        self.near, self.far = int(near), int(far)
        self.own = stop - first
        self.farthest = self.own == 0
        self.slots = 1 if self.farthest else self.own + self.near + self.far
        self.height = self.slots * levels
        self.quarters = list(quarters)
        assert sum(self.quarters) == self.slots
        one, two, three, four = self.quarters
        self.beside = max(one, three) if one and three else 0
        self.half = -(-two // 2)
        self.packed = self.beside > 0 or two > 1
        self.pieces = []
        if self.packed:
            if not self.beside:
                for start, count in ((0, one), (one + two, three)):
                    if count:
                        self.pieces.append((0, start, count))
            if four:
                self.pieces.append((0, one + two + three, four))
        self.whole_rows = sum(piece[2] for piece in self.pieces)
        self.full = self.height * (blocks - 1 if self.packed else blocks)
        self.packed_rows = (self.whole_rows + self.beside + self.half) * levels if self.packed else 0
        self.total = self.full + self.packed_rows
        parts = max(1, round(self.slots / 16))
        self.chunk = -(-self.slots // parts)
        self.parts = -(-self.slots // self.chunk)

    def start(self, hemi, rows):
        return jnp.where(hemi == 1, rows - self.stop + 1 - self.far, self.first + 1 - self.near)

    def chunk_at(self, part):
        return jnp.minimum(part * self.chunk, self.slots - self.chunk)

    def slot(self, hemi, first, count):
        first = min(first, self.slots - count)
        return jnp.where(hemi == 1, self.slots - count - first, first)

    def pairs(self):
        one, two, three, _ = self.quarters
        result = []
        if self.beside:
            result.append((one + two, 0, self.beside, 96))
        if two:
            result.append((one, one + two - self.half, self.half, 64))
        return result

    def pack(self, hemi, last, to):
        row = 0
        for _, first, count in self.pieces:
            to(row, count, last(self.slot(hemi, first, count), count))
            row += count
        for left, right, count, lanes in self.pairs():
            lane = lax.broadcasted_iota(jnp.int32, (count * self.levels, LANES), 1)
            beside = pltpu.roll(last(self.slot(hemi, right, count), count), lanes, 1)
            to(row, count, jnp.where(lane < lanes, last(self.slot(hemi, left, count), count), beside))
            row += count

    def unpack(self, hemi, packed, to):
        row = self.whole_rows
        for left, right, count, lanes in self.pairs():
            value = packed(row, count)
            to(self.slot(hemi, left, count), count, value)
            to(self.slot(hemi, right, count), count, pltpu.roll(value, LANES - lanes, 1))
            row += count
        row = 0
        for _, first, count in self.pieces:
            to(self.slot(hemi, first, count), count, packed(row, count))
            row += count


class Plan:
    def __init__(self, lat, lon, levels, rows, width, listed):
        self.lat, self.lon, self.levels, self.rows, self.width = lat, lon, levels, rows, width
        self.total_rows, self.length = lat * rows, lon * width
        self.parts = lon // FIELDS
        self.wide = round_up(width + 2, LANES)
        pole = listed // 2
        self.low, self.high = pole - pole // 4, pole + pole // 4
        top = self.length // 4 - 1

        def blocks_of(depth):
            return -(-(2 * min(2 * (depth + 1), top) + 1) // LANES)

        self.roles = []
        last = self.high - 2
        for role in range(lat // 2):
            start = role * rows
            if start > last:
                break
            need = {}
            for depth in range(start, min(start + rows - 1, last) + 1):
                need.setdefault(blocks_of(depth), []).append(depth - start)
            spans = [[need[k][0], need[k][-1] + 1, False, False, k] for k in sorted(need)]
            if role > 0:
                spans[0][2], spans[0][4] = True, max(spans[0][4], blocks_of(start - 1))
            if start + rows <= last:
                spans[-1][3], spans[-1][4] = True, max(spans[-1][4], blocks_of(start + rows))
            groups = []
            for first, stop, near, far, blocks in spans:
                depths = range(start + first - int(near), start + stop + int(far))
                quarters = [0] * 4
                for depth in depths:
                    lanes = 2 * min(2 * (depth + 1), top) + 1 - (blocks - 1) * LANES
                    quarters[max(0, -(-lanes // (LANES // 4)) - 1)] += 1
                groups.append(Group(first, stop, near, far, blocks, levels, quarters))
            groups.append(Group(0, 0, False, False, -(-(2 * top + 1) // LANES), levels, (0, 0, 0, 1)))
            self.roles.append(groups)
        self.slots = max(sum(group.slots for group in groups) for groups in self.roles)
        self.table = LANES * max(group.blocks for groups in self.roles for group in groups)
        count = len(self.roles)
        self.lent = {}
        if self.parts == 1 and 2 * count <= lat // 2:
            self.lent = {count - 1: len(self.roles[-1]) - 2}

    def blocks(self, role):
        return (role, self.lat - 1 - role)

    def parcels(self, at):
        indices = range(len(self.roles[at]))
        away = self.lent.get(at)
        home = [g for g in indices if g != away]
        return [home] if away is None else [home, [away]]

    def arrays(self):
        held = [(at, parcel) for at in range(len(self.roles)) for parcel in range(len(self.parcels(at)))]
        return [[key + (which,) for key in held] for which in range(2)]

    def places(self):
        result, number = {}, 0
        for at in range(len(self.roles)):
            for parcel in self.parcels(at):
                offset = 0
                for g in parcel:
                    result[at, g] = (number, offset)
                    offset += self.roles[at][g].total
                number += 1
        return result

    def height_of(self, at, parcel):
        return sum(self.roles[at][g].total for g in self.parcels(at)[parcel])

    def heights(self):
        return [
            self.height_of(at, parcel) for at in range(len(self.roles)) for parcel in range(len(self.parcels(at)))
        ]

    def slot_rows(self):
        table = np.full((len(self.roles), 2, self.slots), -1, np.int32)
        for at, groups in enumerate(self.roles):
            for hemi in range(2):
                rows = []
                for group in groups:
                    first = group.first + 1 - group.near if hemi == 0 else self.rows - group.stop + 1 - group.far
                    rows += [-2] if group.farthest else [first + k for k in range(group.slots)]
                table[at, hemi, : len(rows)] = rows
        return table


def split_table(table):
    high = table.astype(ml_dtypes.bfloat16)
    low = (table - high.astype(np.float64)).astype(ml_dtypes.bfloat16)
    return high, low


@functools.lru_cache(maxsize=None)
def tables(sizes):
    plan = Plan(*sizes)
    index = np.arange(plan.table)
    wave, odd = (index + 1) // 2, (index % 2 == 0) & (index > 0)
    used = wave < plan.length // 4
    points = np.zeros(plan.wide, np.int64)
    points[: plan.width + 1] = np.arange(plan.width + 1)
    points[-1] = -1
    shown = np.zeros(plan.wide, bool)
    shown[: plan.width + 1] = True
    shown[-1] = True

    def trig(at):
        angle = (wave[:, None] * at[None, :]) % plan.length * (2.0 * np.pi / plan.length)
        return np.where(odd[:, None], np.sin(angle), np.cos(angle)) * used[:, None]

    weight = np.where(wave == 0, 1.0, 2.0) / plan.length
    forward, inverse = [], []
    for place in range(plan.lon):
        forward.append(trig(place * plan.width + np.arange(plan.width)).T)
        inverse.append(trig(place * plan.width + points) * weight[:, None] * shown[None, :])
    shape = (plan.lon, plan.width, plan.table // LANES, LANES)
    forward = np.stack(forward).reshape(shape).transpose(0, 2, 1, 3)
    inverse = np.stack(inverse).reshape(plan.lon, plan.table // LANES, LANES, plan.wide)
    return split_table(forward), split_table(inverse)


def fetch_table(place, tabs, held, sems, blocks):
    return [
        pltpu.make_async_copy(tab.at[place, b], held.at[b, k], sems.at[b, k])
        for b in blocks
        for k, tab in enumerate(tabs)
    ]


def split(value):
    high = value.astype(jnp.bfloat16)
    low = (value - high.astype(jnp.float32)).astype(jnp.bfloat16)
    return high, low


def dot(left, right):
    return jnp.dot(left, right, preferred_element_type=jnp.float32)


def three_pass_out(left, right):
    columns = right[0].shape[1]
    both = dot(left[0], jnp.concatenate(right, axis=1))
    return both[:, :columns] + (both[:, columns:] + dot(left[1], right[0]))


def three_pass_in(value, table):
    terms = []
    for at in range(0, value.shape[1], LANES):
        high, low = split(value[:, at : at + LANES])
        terms += [high, low, high]
    return dot(jnp.concatenate(terms, axis=1), table)


def forward_kernel(plan, call, scal, winds, theta, thick, top, bottom, t_high, t_low, *refs):
    places, sets, arrays = plan.places(), field_sets(plan), plan.arrays()[call]
    outs, (points, spectra, held, in_sems, out_sems, t_sems) = refs[: len(arrays)], refs[len(arrays) :]
    levels, width = plan.levels, plan.width
    hemi = scal[3]
    for at, groups in enumerate(plan.roles):

        @pl.when(scal[2] == at)
        def _(at=at, groups=groups):
            mine = [(number, array[1:]) for number, array in enumerate(arrays) if array[0] == at]
            order = [g for g in range(len(groups)) if any(g in plan.parcels(at)[a[0]] for _, a in mine)]
            targets = {}
            for g in order:
                targets[g] = [
                    (number, i, u)
                    for number, (parcel, which) in mine
                    if g in plan.parcels(at)[parcel]
                    for i, u in enumerate(sets[which][at])
                ]
            some_fields = {g: [u ^ scal[0] for _, _, u in targets[g]] for g in order}
            turn_of = {g: n % 2 for n, g in enumerate(order)}
            ready = 0

            def first_row(group):
                if group.farthest:
                    return jnp.clip(scal[4] - 1, 0, plan.rows - 1), 0, 1
                first = jnp.where(hemi == 1, plan.rows - group.stop, group.first)
                return first, jnp.where(hemi == 1, group.far, group.near), group.own

            def fetch(g):
                first, slot, count = first_row(groups[g])
                for i, field in enumerate(some_fields[g]):

                    def pieces(source, i=i):
                        for k in range(0, count, PIECE):
                            size = min(PIECE, count - k)
                            pltpu.make_async_copy(
                                source.at[pl.ds(first + k, size)],
                                points.at[turn_of[g], i, pl.ds(slot + k, size)],
                                in_sems.at[turn_of[g], i],
                            ).start()

                    pl.when(field < 2)(lambda: pieces(winds.at[jnp.minimum(field, 1)]))
                    pl.when(field == 2)(lambda: pieces(theta))
                    pl.when(field == 3)(lambda: pieces(thick))

            def arrive(g):
                first, slot, count = first_row(groups[g])
                for i in range(len(targets[g])):
                    pltpu.make_async_copy(
                        theta.at[pl.ds(first, count)],
                        points.at[turn_of[g], i, pl.ds(slot, count)],
                        in_sems.at[turn_of[g], i],
                    ).wait()

            def leave(g, parts):
                group, turn, copies = groups[g], turn_of[g], []
                _, offset = places[at, g]
                size = group.full // parts
                for i, (number, place, _) in enumerate(targets[g]):
                    for k in range(parts if group.full else 0):
                        copies.append(
                            pltpu.make_async_copy(
                                spectra.at[turn, i, pl.ds(k * size, size)],
                                outs[number].at[place, pl.ds(offset + k * size, size)],
                                out_sems.at[turn, i, 0],
                            )
                        )
                    if group.packed:
                        copies.append(
                            pltpu.make_async_copy(
                                spectra.at[turn, i, pl.ds(group.blocks * group.height, group.packed_rows)],
                                outs[number].at[place, pl.ds(offset + group.full, group.packed_rows)],
                                out_sems.at[turn, i, 1],
                            )
                        )
                return copies

            def pack(g, i):
                group, turn = groups[g], turn_of[g]

                def last(slot, count):
                    at_row = pl.multiple_of((group.blocks - 1) * group.height + slot * levels, 8)
                    return spectra[turn, i, pl.ds(at_row, count * levels), :]

                def to(row, count, value):
                    at_row = group.blocks * group.height + row * levels
                    spectra[turn, i, at_row : at_row + count * levels, :] = value

                group.pack(hemi, last, to)

            def halo(g, slot, line, wanted):
                @pl.when(wanted)
                def _():
                    for i, field in enumerate(some_fields[g]):
                        points[turn_of[g], i, slot] = line[field]

            fetch(order[0])
            needed = range(max(groups[g].blocks for g in order))
            for copy in fetch_table(scal[1], (t_high, t_low), held, t_sems, needed):
                copy.start()
            for n, g in enumerate(order):
                group = groups[g]
                if n + 1 < len(order):
                    fetch(order[n + 1])
                arrive(g)
                for copy in fetch_table(scal[1], (t_high, t_low), held, t_sems, range(ready, group.blocks)):
                    copy.wait()
                ready = max(ready, group.blocks)
                if group.farthest:
                    halo(g, 0, top, scal[4] == 0)
                    halo(g, 0, bottom, scal[4] == plan.rows + 1)
                if group.near:
                    halo(g, 0, top, hemi == 0)
                    halo(g, group.slots - 1, bottom, hemi == 1)
                if group.far:
                    halo(g, group.slots - 1, bottom, hemi == 0)
                    halo(g, 0, top, hemi == 1)
                if n >= 2:
                    for copy in leave(order[n - 2], 1):
                        copy.wait()

                def transform(value, group=group):
                    return three_pass_out(
                        split(value),
                        [
                            jnp.concatenate([held[b, half] for b in range(group.blocks)], axis=1)
                            for half in range(2)
                        ],
                    )

                if group.farthest:
                    spec = transform(points[turn_of[g], : len(targets[g]), 0].reshape(len(targets[g]) * levels, width))
                    for i in range(len(targets[g])):
                        for b in range(group.blocks):
                            spectra[turn_of[g], i, b * levels : (b + 1) * levels, :] = spec[
                                i * levels : (i + 1) * levels, b * LANES : (b + 1) * LANES
                            ]
                else:

                    def part(n, _, g=g, group=group, transform=transform):
                        i, slot = n // group.parts, group.chunk_at(lax.rem(n, group.parts))
                        size = group.chunk * levels
                        spec = transform(points[turn_of[g], i, pl.ds(slot, group.chunk)].reshape(size, width))
                        for b in range(group.blocks):
                            target = pl.multiple_of(b * group.height + slot * levels, 8)
                            spectra[turn_of[g], i, pl.ds(target, size), :] = spec[:, b * LANES : (b + 1) * LANES]
                        return 0

                    lax.fori_loop(0, len(targets[g]) * group.parts, part, 0)
                if group.packed:
                    lax.fori_loop(0, len(targets[g]), lambda i, _, g=g: (pack(g, i), 0)[1], 0)
                for copy in leave(g, max(1, group.full // group.height)):
                    copy.start()
            for g in order[-2:]:
                for copy in leave(g, 1):
                    copy.wait()


def forward(plan, call, scal, winds, theta, thick, top, bottom, tabs):
    arrays = plan.arrays()[call]
    count = FIELDS // 2
    shapes = [(FIELDS // 2, plan.height_of(at, parcel), LANES) for at, parcel, _ in arrays]
    anywhere = pl.BlockSpec(memory_space=pl.ANY)
    halo = pl.BlockSpec((FIELDS, plan.levels, plan.width), lambda i, s: (0, 0, 0))
    slots = max(group.slots for groups in plan.roles for group in groups)
    total = max(group.height * group.blocks + group.packed_rows for groups in plan.roles for group in groups)
    outs = pl.pallas_call(
        functools.partial(forward_kernel, plan, call),
        grid_spec=pltpu.PrefetchScalarGridSpec(
            num_scalar_prefetch=1,
            grid=(1,),
            in_specs=[anywhere] * 3 + [halo, halo, anywhere, anywhere],
            out_specs=[anywhere] * len(arrays),
            scratch_shapes=[
                pltpu.VMEM((2, count, slots, plan.levels, plan.width), jnp.float32),
                pltpu.VMEM((2, count, total, LANES), jnp.float32),
                pltpu.VMEM((plan.table // LANES, 2, plan.width, LANES), jnp.bfloat16),
                pltpu.SemaphoreType.DMA((2, count)),
                pltpu.SemaphoreType.DMA((2, count, 2)),
                pltpu.SemaphoreType.DMA((plan.table // LANES, 2)),
            ],
        ),
        out_shape=[jax.ShapeDtypeStruct(shape, jnp.float32) for shape in shapes],
        compiler_params=pltpu.CompilerParams(vmem_limit_bytes=VMEM),
        cost_estimate=pl.CostEstimate(flops=FORWARD_COST, bytes_accessed=0, transcendentals=0),
        name="partial_spectra",
    )(scal, winds, theta, thick, top, bottom, *tabs)
    return dict(zip(arrays, outs))


def edge_kernel(plan, count, _, *refs):
    ins, outs = refs[:-2], refs[-2:]
    lane = lax.broadcasted_iota(jnp.int32, (plan.levels, LANES), 1)
    some = plan.rows // count
    for side, column in enumerate((0, (plan.width - 1) % LANES)):
        kept = (jnp.zeros((plan.levels, LANES), jnp.float32),) * FIELDS
        for piece in range(count):
            at = (side * count + piece) * FIELDS
            fields = ins[at : at + FIELDS]

            def pick(row, kept, fields=fields, piece=piece, column=column):
                values = (fields[0][0, row], fields[1][0, row], fields[2][row], fields[3][row])
                return tuple(
                    jnp.where(lane == row + piece * some, value[:, column : column + 1], old)
                    for value, old in zip(values, kept)
                )

            kept = lax.fori_loop(0, some, pick, kept, unroll=max(k for k in range(1, 11) if some % k == 0))
        for field in range(FIELDS):
            outs[side][field] = kept[field]


def edges(plan, after, winds, theta, thick):
    count = 3 if plan.rows % 3 == 0 else 1
    some = plan.rows // count
    specs = []
    for at in (0, (plan.width - 1) // LANES):
        for piece in range(count):
            for wind in range(2):
                specs.append(
                    pl.BlockSpec(
                        (1, some, plan.levels, LANES), lambda i, w=wind, p=piece, at=at: (w, p, 0, at)
                    )
                )
            specs += [pl.BlockSpec((some, plan.levels, LANES), lambda i, p=piece, at=at: (p, 0, at))] * 2
    shape = (FIELDS, plan.levels, LANES)
    return pl.pallas_call(
        functools.partial(edge_kernel, plan, count),
        grid=(1,),
        in_specs=[pl.BlockSpec(memory_space=pl.ANY)] + specs,
        out_specs=[pl.BlockSpec(shape, lambda i: (0, 0, 0))] * 2,
        out_shape=[jax.ShapeDtypeStruct(shape, jnp.float32)] * 2,
        compiler_params=pltpu.CompilerParams(vmem_limit_bytes=VMEM),
        cost_estimate=pl.CostEstimate(flops=EDGE_COST, bytes_accessed=0, transcendentals=0),
        name="edge_columns",
    )(after, *[winds, winds, theta, thick] * (2 * count))


def step_kernel(plan, step_rows, scal, coef, west, east, top, bottom, cuts, i_high, i_low, *refs):
    places, heights = plan.places(), plan.heights()
    halves = plan.levels // 8
    raw, refs = refs[: FIELDS * halves], refs[FIELDS * halves :]
    spectra = refs[: FIELDS * len(heights)]
    new_wind, new_theta, new_thick, held, sums, unpacked, table, ready, sems, t_sems, out_sems = refs[FIELDS * len(heights) :]
    step = pl.program_id(0)
    rows, width, wide, levels = plan.rows, plan.width, plan.wide, plan.levels
    last_step = rows // step_rows

    def inverse(at, groups):
        slot_at = np.cumsum([0] + [group.slots for group in groups])
        row_at = np.cumsum([0] + [group.total for group in groups])

        def copies(g):
            number, offset = places[at, g]
            return [
                pltpu.make_async_copy(
                    spectra[number * FIELDS + u].at[pl.ds(offset, groups[g].total)],
                    sums.at[u, pl.ds(int(row_at[g]), groups[g].total)],
                    sems.at[g, u],
                )
                for u in range(FIELDS)
            ]

        have = 0
        for g, group in enumerate(groups):
            for copy in copies(g):
                copy.start()
            for copy in fetch_table(scal[1], (i_high, i_high, i_low), table, t_sems, range(have, group.blocks)):
                copy.start()
            have = max(have, group.blocks)
        have = 0
        for g, group in enumerate(groups):
            for copy in copies(g):
                copy.wait()
            for copy in fetch_table(scal[1], (i_high, i_high, i_low), table, t_sems, range(have, group.blocks)):
                copy.wait()
            have = max(have, group.blocks)
            lanes = group.blocks * LANES
            first_slot, first_sum = int(slot_at[g]), int(row_at[g])

            def back_of(spec, size, lanes=lanes, group=group):
                back = three_pass_in(spec, table[: group.blocks].reshape(3 * lanes, wide))
                return back.reshape(size, levels, wide)

            def masked(u, slot, size, group=group, first_slot=first_slot, first_sum=first_sum):
                rows_at = pl.ds(pl.multiple_of((first_slot + slot) * levels, 8), size)
                cut = cuts[rows_at, :]
                lane = lax.broadcasted_iota(jnp.int32, (size, LANES), 1)
                pieces = []
                for b in range(group.blocks):
                    keep = lax.shift_right_logical(lane + (b * LANES + 1), 1) <= cut
                    if group.packed and b == group.blocks - 1:
                        value = unpacked[u, pl.ds(pl.multiple_of(slot * levels, 8), size), :]
                    else:
                        source = pl.multiple_of(first_sum + b * group.height + slot * levels, 8)
                        value = sums[u, pl.ds(source, size), :]
                    pieces.append(jnp.where(keep, value, 0.0))
                return jnp.concatenate(pieces, axis=1)

            def unpack(u, _, group=group, first_sum=first_sum):
                def packed(row, count):
                    at_row = first_sum + group.full + row * levels
                    return sums[u, at_row : at_row + count * levels, :]

                def to(slot, count, value):
                    at_row = pl.multiple_of(slot * levels, 8)
                    unpacked[u, pl.ds(at_row, count * levels), :] = value

                group.unpack(scal[3], packed, to)
                return 0

            if group.packed:
                lax.fori_loop(0, FIELDS, unpack, 0)
            if group.farthest:
                spec = jnp.concatenate([masked(u, 0, levels) for u in range(FIELDS)], axis=0)
                back = back_of(spec, FIELDS)

                @pl.when(scal[4] >= 0)
                def _(back=back):
                    for u in range(FIELDS):
                        held[u ^ scal[0], scal[4]] = back[u]
            else:
                start = group.start(scal[3], rows)

                def part(n, _, group=group, start=start, masked=masked, back_of=back_of):
                    u, slot = n // group.parts, group.chunk_at(lax.rem(n, group.parts))
                    back = back_of(masked(u, slot, group.chunk * levels), group.chunk)
                    held[u ^ scal[0], pl.ds(start + slot, group.chunk)] = back
                    return 0

                lax.fori_loop(0, FIELDS * group.parts, part, 0)

    @pl.when(step == 0)
    def _():
        for at, groups in enumerate(plan.roles):
            pl.when(scal[2] == at)(functools.partial(inverse, at, groups))
        for side, line in enumerate((top, bottom)):

            @pl.when(scal[5 + side] == 0)
            def _(side=side, line=line):
                for field in range(FIELDS):
                    held[field, side * (rows + 1), :, :width] = line[field]

    base = step * step_rows
    tail = width % LANES

    @pl.when(step < last_step)
    def _():
        lane = lax.broadcasted_iota(jnp.int32, (levels, LANES), 1)

        def load(n, _):
            at = n
            row = base + n
            is_raw = (row >= scal[7]) & (row < scal[8])
            for field in range(FIELDS):
                for half in range(halves):
                    piece = raw[field * halves + half]
                    some = slice(half * 8, half * 8 + 8)
                    value = piece[0, at] if field < 2 else piece[at]
                    held[field, row + 1, some, :width] = jnp.where(
                        is_raw, value, held[field, row + 1, some, :width]
                    )
                beyond = jnp.where(
                    lane == tail,
                    pltpu.roll(east[field], (tail + LANES - row) & (LANES - 1), 1),
                    pltpu.roll(west[field], (2 * LANES - 1 - row) & (LANES - 1), 1),
                )
                held[field, row + 1, :, width:] = jnp.where(
                    is_raw, beyond[:, tail:], held[field, row + 1, :, width:]
                )
            return 0

        @pl.when((base < scal[8]) & (base + step_rows > scal[7]))
        def _():
            lax.fori_loop(0, step_rows, load, 0, unroll=3 if step_rows % 3 == 0 else 1)

    slot = step % 2
    count = wide // LANES
    lane = lax.broadcasted_iota(jnp.int32, (8, LANES), 1)
    is_first, is_last = lane == 0, lane == LANES - 1

    def stencil(row, _):
        at = base - step_rows + row
        along, across, push, turn, cos_north, cos_south = [coef[k * rows + at] for k in range(6)]
        across_north, across_south = across * cos_north, across * cos_south
        for part in range(levels // 8):
            some = pl.ds(part * 8, 8)

            def load(field, shift, k):
                return held[field, at + shift, some, k * LANES : (k + 1) * LANES]

            here = [
                functools.lru_cache(maxsize=None)(lambda k, field=field: load(field, 1, k))
                for field in range(FIELDS)
            ]
            up = [functools.lru_cache(maxsize=None)(lambda k, f=f: pltpu.roll(f(k), LANES - 1, 1)) for f in here]
            down = [functools.lru_cache(maxsize=None)(lambda k, f=f: pltpu.roll(f(k), 1, 1)) for f in here]

            def shifted(which, k):
                return (
                    jnp.where(is_last, up[which]((k + 1) % count), up[which](k)),
                    jnp.where(is_first, down[which]((k - 1) % count), down[which](k)),
                )

            for k in range(count):
                stop = min(width, (k + 1) * LANES)

                def put(field, piece, k=k, stop=stop):
                    ready[slot, field, row, some, k * LANES : stop] = piece[:, : stop - k * LANES]

                u, v, t, h = [here[field](k) for field in range(FIELDS)]
                advect, carry = along * u, 0.1 * v
                (u_e, u_w), (v_e, v_w), (t_e, t_w), (h_e, h_w) = [shifted(field, k) for field in range(FIELDS)]
                v_n, v_s, h_n, h_s = load(1, 0, k), load(1, 2, k), load(3, 0, k), load(3, 2, k)
                put(
                    3,
                    h
                    - along * (u_e * h_e - u_w * h_w)
                    - (across_south * (v_s * h_s) - across_north * (v_n * h_n)),
                )
                put(
                    1,
                    v
                    - advect * (v_e - v_w)
                    - carry * (v_s - v_n)
                    - 0.15 * (h_s - h_n)
                    - turn * u,
                )
                put(
                    0,
                    u
                    - advect * (u_e - u_w)
                    - carry * (load(0, 2, k) - load(0, 0, k))
                    - push * (h_e - h_w)
                    + turn * v,
                )
                put(2, t - advect * (t_e - t_w) - carry * (load(2, 2, k) - load(2, 0, k)))
        return 0

    outs = (new_wind.at[0], new_wind.at[1], new_theta, new_thick)

    def leave(at_step, size, act):
        for field, out in enumerate(outs):
            for k in range(0, step_rows, size):
                act(
                    pltpu.make_async_copy(
                        ready.at[at_step % 2, field, pl.ds(k, size)],
                        out.at[pl.ds((at_step - 1) * step_rows + k, size)],
                        out_sems.at[at_step % 2, field],
                    )
                )

    @pl.when(step > 2)
    def _():
        leave(step - 2, step_rows, lambda copy: copy.wait())

    @pl.when(step > 0)
    def _():
        lax.fori_loop(0, step_rows, stencil, 0, unroll=3 if step_rows % 3 == 0 else 1)
        leave(step, PIECE if step_rows % PIECE == 0 else step_rows, lambda copy: copy.start())

    @pl.when(step == last_step)
    def _():
        if last_step > 1:
            leave(step - 1, step_rows, lambda copy: copy.wait())
        leave(step, step_rows, lambda copy: copy.wait())


def substep(plan, step_rows, scal, coef, winds, theta, thick, west, east, top, bottom, cuts, tabs, spectra):
    rows, width, levels = plan.rows, plan.width, plan.levels
    once = pl.Buffered(1)
    steps = rows // step_rows

    def block(i, s):
        return jnp.clip(i, s[9], s[10])

    def whole(shape):
        return pl.BlockSpec(shape, lambda i, s: (0,) * len(shape), pipeline_mode=once)

    anywhere = pl.BlockSpec(memory_space=pl.ANY)
    halves = range(levels // 8)
    raw_specs = [
        pl.BlockSpec((1, step_rows, 8, width), lambda i, s, w=wind, h=half: (w, block(i, s), h, 0))
        for wind in range(2)
        for half in halves
    ] + [
        pl.BlockSpec((step_rows, 8, width), lambda i, s, h=half: (block(i, s), h, 0))
        for _ in range(2)
        for half in halves
    ]
    raw = [array for array in (winds, winds, theta, thick) for _ in halves]
    edge, halo = (FIELDS, levels, LANES), (FIELDS, levels, width)
    in_specs = [
        pl.BlockSpec(memory_space=pltpu.SMEM),
        whole(edge),
        whole(edge),
        whole(halo),
        whole(halo),
        whole((plan.slots * levels, LANES)),
        anywhere,
        anywhere,
    ] + raw_specs + [anywhere] * len(spectra)
    shapes = [(2, rows, levels, width)] + [(rows, levels, width)] * 2
    most = max(sum(group.total for group in groups) for groups in plan.roles)
    return pl.pallas_call(
        functools.partial(step_kernel, plan, step_rows),
        grid_spec=pltpu.PrefetchScalarGridSpec(
            num_scalar_prefetch=1,
            grid=(steps + 1,),
            in_specs=in_specs,
            out_specs=[anywhere] * 3,
            scratch_shapes=[
                pltpu.VMEM((FIELDS, rows + 2, levels, plan.wide), jnp.float32),
                pltpu.VMEM((FIELDS, most, LANES), jnp.float32),
                pltpu.VMEM((FIELDS, max(group.height for groups in plan.roles for group in groups), LANES), jnp.float32),
                pltpu.VMEM((plan.table // LANES, 3, LANES, plan.wide), jnp.bfloat16),
                pltpu.VMEM((2, FIELDS, step_rows, levels, width), jnp.float32),
                pltpu.SemaphoreType.DMA((max(len(groups) for groups in plan.roles), FIELDS)),
                pltpu.SemaphoreType.DMA((plan.table // LANES, 3)),
                pltpu.SemaphoreType.DMA((2, FIELDS)),
            ],
        ),
        out_shape=[jax.ShapeDtypeStruct(shape, jnp.float32) for shape in shapes],
        compiler_params=pltpu.CompilerParams(vmem_limit_bytes=VMEM),
        cost_estimate=pl.CostEstimate(
            flops=6 * most * FIELDS * LANES * plan.wide, bytes_accessed=40_000_000, transcendentals=0
        ),
        name="inverse_and_substep",
    )(scal, coef, west, east, top, bottom, cuts, *tabs, *raw, *spectra)


def lon_swap(plan, value, blocks, bit):
    pairs = [
        (block * plan.lon + place, block * plan.lon + (place ^ (1 << bit)))
        for block in blocks
        for place in range(plan.lon)
    ]
    return lax.ppermute(value, ("lat", "lon"), pairs)


def lat_move(plan, value, sources, targets):
    pairs = [
        (source * plan.lon + place, target * plan.lon + place)
        for source, target in zip(sources, targets)
        for place in range(plan.lon)
    ]
    return lax.ppermute(value, ("lat", "lon"), pairs)


def spread(plan, blocks, slots, order):
    for bit in reversed(order):
        for s in sorted(slots):
            slots[s | (1 << bit)] = lon_swap(plan, slots[s], blocks, bit)
    return slots


def gather_sums(plan, blocks, slots, order):
    slots = dict(slots)
    for bit in order:
        sent = [s for s in slots if s >> bit & 1]
        for s in sorted(sent, key=lambda s: -bin(s).count("1")):
            slots[s ^ (1 << bit)] = slots[s ^ (1 << bit)] + lon_swap(plan, slots.pop(s), blocks, bit)
    return spread(plan, blocks, slots, order)


def field_sets(plan):
    sent, kept = [], []
    for at in range(len(plan.roles)):
        bit = at % 2
        sent.append([u for u in range(FIELDS) if u >> bit & 1])
        kept.append([u for u in range(FIELDS) if not u >> bit & 1])
    return sent, kept


def parcel_sums(plan, place, at, blocks, sent, kept):
    first, second = field_sets(plan)
    parts, own = plan.parts, place % plan.parts
    if parts == 1:
        near, far = at % 2, 1 - at % 2
        moved = lon_swap(plan, sent, blocks, near)
        send = kept[1] + moved[1]
        slots = {0: (kept[0] + moved[0]) + lon_swap(plan, send, blocks, far)}
        slots = spread(plan, blocks, slots, [near, far])
        return [slots[u] for u in range(FIELDS)]
    bits = plan.lon.bit_length() - 1
    slots = {}
    for us, array in ((first[at], sent), (second[at], kept)):
        for i, u in enumerate(us):
            pieces = array[i].reshape(parts, -1, LANES)
            for k in range(parts):
                slots[u * parts + k] = pieces[k ^ own]
    order = list(range(bits)) if at % 2 == 0 else list(reversed(range(bits)))
    slots = gather_sums(plan, blocks, slots, order)
    result = []
    for u in range(FIELDS):
        pieces = jnp.stack([slots[u * parts + k] for k in range(parts)])
        result.append(pieces[jnp.arange(parts) ^ own].reshape(-1, LANES))
    return result


def all_sums(plan, place, arrays):
    result = []
    for at in range(len(plan.roles)):
        home = plan.blocks(at)
        for parcel in range(len(plan.parcels(at))):
            first, second = arrays[at, parcel, 0], arrays[at, parcel, 1]
            if parcel == 0:
                result += parcel_sums(plan, place, at, home, first, second)
                continue
            helpers = plan.blocks(at + len(plan.roles))
            first, second = [lat_move(plan, array, home, helpers) for array in (first, second)]
            sums = parcel_sums(plan, place, at, helpers, first, second)
            result += [lat_move(plan, array, helpers, home) for array in sums]
    return result


def body(winds, theta, thick, polar_rows, cutoffs):
    lat, lon = lax.axis_size("lat"), lax.axis_size("lon")
    levels, rows, width = theta.shape
    sizes = (lat, lon, levels, rows, width, polar_rows.shape[0])
    plan = Plan(*sizes)
    t_tabs, i_tabs = [tuple(jnp.asarray(part) for part in pair) for pair in tables(sizes)]
    block, place = lax.axis_index("lat"), lax.axis_index("lon")
    winds = winds.transpose(0, 2, 1, 3)
    theta = theta.transpose(1, 0, 2)
    thick = thick.transpose(1, 0, 2)
    hemi = (block >= lat // 2).astype(jnp.int32)
    role = jnp.where(hemi == 1, lat - 1 - block, block)

    def line(row):
        return jnp.stack([winds[0, row], winds[1, row], theta[row], thick[row]])

    south_pairs = [(b * lon + p, (b + 1) * lon + p) for b in range(lat - 1) for p in range(lon)]
    north_pairs = [(to, at) for at, to in south_pairs]
    top = lax.ppermute(line(rows - 1), ("lat", "lon"), south_pairs)
    bottom = lax.ppermute(line(0), ("lat", "lon"), north_pairs)

    step_rows = max(k for k in range(1, 16) if rows % k == 0)
    listed = polar_rows.shape[0]
    north_run = jnp.sum((polar_rows < plan.total_rows // 2).astype(jnp.int32))
    south_first = plan.total_rows - listed + north_run
    far_row = jnp.where(hemi == 1, south_first, north_run - 1)
    far_at = far_row - block * rows + 1
    far_at = jnp.where((far_at >= 0) & (far_at <= rows + 1), far_at, -1)
    raw_from = jnp.clip(north_run - block * rows, 0, rows)
    raw_to = jnp.clip(south_first - block * rows, 0, rows)
    block_from = jnp.minimum(raw_from, rows - 1) // step_rows
    block_to = jnp.maximum(block_from, jnp.maximum(raw_to - 1, 0) // step_rows)
    above, below = block * rows - 1, (block + 1) * rows

    def is_listed(row):
        return (row >= 0) & (row < plan.total_rows) & ((row < north_run) | (row >= south_first))

    facts = [
        place // plan.parts, place, role, hemi, far_at, is_listed(above), is_listed(below),
        raw_from, raw_to, block_from, block_to,
    ]
    scal = jnp.stack([jnp.asarray(fact).astype(jnp.int32) for fact in facts])

    first_edge, last_edge = edges(plan, scal, winds, theta, thick)
    some = [b for b in range(lat) if (min(b, lat - 1 - b) + 1) * rows > plan.low]
    east_pairs = [(b * lon + i, b * lon + (i + 1) % lon) for b in some for i in range(lon)]
    west = lax.ppermute(last_edge, ("lat", "lon"), east_pairs)
    east = lax.ppermute(first_edge, ("lat", "lon"), [(to, at) for at, to in east_pairs])

    scal, _ = lax.optimization_barrier((scal, first_edge))
    arrays = forward(plan, 0, scal, winds, theta, thick, top, bottom, t_tabs)
    scal, _ = lax.optimization_barrier((scal, arrays[plan.arrays()[0][0]]))
    later = forward(plan, 1, scal, winds, theta, thick, top, bottom, t_tabs)
    added = {key: array for key, array in later.items() if key[1] == 0}
    added, west, east = lax.optimization_barrier((added, west, east))
    arrays = {**arrays, **later, **added}
    sums = all_sums(plan, place, arrays)

    slot_rows = jnp.asarray(plan.slot_rows())[jnp.minimum(role, len(plan.roles) - 1), hemi]
    slot_rows = jnp.where(slot_rows == -2, far_at, slot_rows)
    hits = (polar_rows[None, :] == (slot_rows - 1 + block * rows)[:, None]) & (slot_rows >= 0)[:, None]
    cut = jnp.sum(jnp.where(hits, cutoffs[None, :] + 1, 0), axis=1) - 1
    cuts = jnp.broadcast_to(cut.astype(jnp.int32)[:, None, None], (plan.slots, levels, LANES))
    cuts = cuts.reshape(plan.slots * levels, LANES)

    ring = block * rows - 1 + jnp.arange(rows + 2, dtype=jnp.int32)
    centre = (ring.astype(jnp.float32) + 0.5) * (jnp.pi / plan.total_rows)
    cos, sin = jnp.sin(centre), -jnp.cos(centre)
    mid = cos[1:-1]
    coef = jnp.concatenate([0.025 / mid, 0.1 / mid, 0.05 / mid, 0.3 * sin[1:-1], cos[:-2], cos[2:]])

    out = substep(
        plan, step_rows, scal, coef, winds, theta, thick, west, east, top, bottom, cuts, i_tabs, sums
    )
    return (out[0].transpose(0, 2, 1, 3), out[1].transpose(1, 0, 2), out[2].transpose(1, 0, 2))


def solution(mesh):
    in_specs = (P(None, None, "lat", "lon"), P(None, "lat", "lon"), P(None, "lat", "lon"), P(), P())
    out_specs = (P(None, None, "lat", "lon"), P(None, "lat", "lon"), P(None, "lat", "lon"))
    return jax.shard_map(body, mesh=mesh, in_specs=in_specs, out_specs=out_specs, check_vma=False)
```

```python
import functools

import jax
import jax.numpy as jnp
import ml_dtypes
import numpy as np
from jax import lax
from jax.experimental import pallas as pl
from jax.experimental.pallas import tpu as pltpu
from jax.sharding import PartitionSpec as P

FIELDS = 4
LANES = 128
PIECE = 3
VMEM = 60 * 1024 * 1024
FORWARD_COST, EDGE_COST = 5_000_000_000, 5_000_000_000


def round_up(value, step):
    return -(-value // step) * step


class Group:
    def __init__(self, first, stop, near, far, blocks, levels, quarters):
        self.first, self.stop, self.blocks, self.levels = first, stop, blocks, levels
        self.near, self.far = int(near), int(far)
        self.own = stop - first
        self.farthest = self.own == 0
        self.slots = 1 if self.farthest else self.own + self.near + self.far
        self.height = self.slots * levels
        self.quarters = list(quarters)
        assert sum(self.quarters) == self.slots
        one, two, three, four = self.quarters
        self.beside = max(one, three) if one and three else 0
        self.half = -(-two // 2)
        self.packed = self.beside > 0 or two > 1
        self.pieces = []
        if self.packed:
            if not self.beside:
                for start, count in ((0, one), (one + two, three)):
                    if count:
                        self.pieces.append((0, start, count))
            if four:
                self.pieces.append((0, one + two + three, four))
        self.whole_rows = sum(piece[2] for piece in self.pieces)
        self.full = self.height * (blocks - 1 if self.packed else blocks)
        self.packed_rows = (self.whole_rows + self.beside + self.half) * levels if self.packed else 0
        self.total = self.full + self.packed_rows
        parts = max(1, round(self.slots / 16))
        self.chunk = -(-self.slots // parts)
        self.parts = -(-self.slots // self.chunk)

    def start(self, hemi, rows):
        return jnp.where(hemi == 1, rows - self.stop + 1 - self.far, self.first + 1 - self.near)

    def chunk_at(self, part):
        return jnp.minimum(part * self.chunk, self.slots - self.chunk)

    def slot(self, hemi, first, count):
        first = min(first, self.slots - count)
        return jnp.where(hemi == 1, self.slots - count - first, first)

    def pairs(self):
        one, two, three, _ = self.quarters
        result = []
        if self.beside:
            result.append((one + two, 0, self.beside, 96))
        if two:
            result.append((one, one + two - self.half, self.half, 64))
        return result

    def pack(self, hemi, last, to):
        row = 0
        for _, first, count in self.pieces:
            to(row, count, last(self.slot(hemi, first, count), count))
            row += count
        for left, right, count, lanes in self.pairs():
            lane = lax.broadcasted_iota(jnp.int32, (count * self.levels, LANES), 1)
            beside = pltpu.roll(last(self.slot(hemi, right, count), count), lanes, 1)
            to(row, count, jnp.where(lane < lanes, last(self.slot(hemi, left, count), count), beside))
            row += count

    def unpack(self, hemi, packed, to):
        row = self.whole_rows
        for left, right, count, lanes in self.pairs():
            value = packed(row, count)
            to(self.slot(hemi, left, count), count, value)
            to(self.slot(hemi, right, count), count, pltpu.roll(value, LANES - lanes, 1))
            row += count
        row = 0
        for _, first, count in self.pieces:
            to(self.slot(hemi, first, count), count, packed(row, count))
            row += count


class Plan:
    def __init__(self, lat, lon, levels, rows, width, listed):
        self.lat, self.lon, self.levels, self.rows, self.width = lat, lon, levels, rows, width
        self.total_rows, self.length = lat * rows, lon * width
        self.parts = lon // FIELDS
        self.wide = round_up(width + 2, LANES)
        pole = listed // 2
        self.low, self.high = pole - pole // 4, pole + pole // 4
        top = self.length // 4 - 1

        def blocks_of(depth):
            return -(-(2 * min(2 * (depth + 1), top) + 1) // LANES)

        self.roles = []
        last = self.high - 2
        for role in range(lat // 2):
            start = role * rows
            if start > last:
                break
            need = {}
            for depth in range(start, min(start + rows - 1, last) + 1):
                need.setdefault(blocks_of(depth), []).append(depth - start)
            spans = [[need[k][0], need[k][-1] + 1, False, False, k] for k in sorted(need)]
            if role > 0:
                spans[0][2], spans[0][4] = True, max(spans[0][4], blocks_of(start - 1))
            if start + rows <= last:
                spans[-1][3], spans[-1][4] = True, max(spans[-1][4], blocks_of(start + rows))
            groups = []
            for first, stop, near, far, blocks in spans:
                depths = range(start + first - int(near), start + stop + int(far))
                quarters = [0] * 4
                for depth in depths:
                    lanes = 2 * min(2 * (depth + 1), top) + 1 - (blocks - 1) * LANES
                    quarters[max(0, -(-lanes // (LANES // 4)) - 1)] += 1
                groups.append(Group(first, stop, near, far, blocks, levels, quarters))
            groups.append(Group(0, 0, False, False, -(-(2 * top + 1) // LANES), levels, (0, 0, 0, 1)))
            self.roles.append(groups)
        self.slots = max(sum(group.slots for group in groups) for groups in self.roles)
        self.table = LANES * max(group.blocks for groups in self.roles for group in groups)
        count = len(self.roles)
        self.lent = {}
        if self.parts == 1 and 2 * count <= lat // 2:
            self.lent = {count - 1: len(self.roles[-1]) - 2}

    def blocks(self, role):
        return (role, self.lat - 1 - role)

    def parcels(self, at):
        indices = range(len(self.roles[at]))
        away = self.lent.get(at)
        home = [g for g in indices if g != away]
        return [home] if away is None else [home, [away]]

    def stores(self):
        result = []
        for at in range(len(self.roles)):
            size = self.height_of(at, 0)
            for store in result:
                sizes = [self.height_of(*member) for member in store]
                if self.parts == 1 and max(sizes + [size]) <= 1.1 * min(sizes + [size]):
                    store.append((at, 0))
                    break
            else:
                result.append([(at, 0)])
        return result + [[(at, 1)] for at in self.lent]

    def arrays(self):
        return [[(store, which) for store in range(len(self.stores()))] for which in range(2)]

    def places(self):
        result = {}
        for number, store in enumerate(self.stores()):
            for at, parcel in store:
                offset = 0
                for g in self.parcels(at)[parcel]:
                    result[at, g] = (number, offset)
                    offset += self.roles[at][g].total
        return result

    def height_of(self, at, parcel):
        return sum(self.roles[at][g].total for g in self.parcels(at)[parcel])

    def heights(self):
        return [max(self.height_of(*member) for member in store) for store in self.stores()]

    def slot_rows(self):
        table = np.full((len(self.roles), 2, self.slots), -1, np.int32)
        for at, groups in enumerate(self.roles):
            for hemi in range(2):
                rows = []
                for group in groups:
                    first = group.first + 1 - group.near if hemi == 0 else self.rows - group.stop + 1 - group.far
                    rows += [-2] if group.farthest else [first + k for k in range(group.slots)]
                table[at, hemi, : len(rows)] = rows
        return table


def split_table(table):
    high = table.astype(ml_dtypes.bfloat16)
    low = (table - high.astype(np.float64)).astype(ml_dtypes.bfloat16)
    return high, low


@functools.lru_cache(maxsize=None)
def tables(sizes):
    plan = Plan(*sizes)
    index = np.arange(plan.table)
    wave, odd = (index + 1) // 2, (index % 2 == 0) & (index > 0)
    used = wave < plan.length // 4
    points = np.zeros(plan.wide, np.int64)
    points[: plan.width + 1] = np.arange(plan.width + 1)
    points[-1] = -1
    shown = np.zeros(plan.wide, bool)
    shown[: plan.width + 1] = True
    shown[-1] = True

    def trig(at):
        angle = (wave[:, None] * at[None, :]) % plan.length * (2.0 * np.pi / plan.length)
        return np.where(odd[:, None], np.sin(angle), np.cos(angle)) * used[:, None]

    weight = np.where(wave == 0, 1.0, 2.0) / plan.length
    forward, inverse = [], []
    for place in range(plan.lon):
        forward.append(trig(place * plan.width + np.arange(plan.width)).T)
        inverse.append(trig(place * plan.width + points) * weight[:, None] * shown[None, :])
    shape = (plan.lon, plan.width, plan.table // LANES, LANES)
    forward = np.stack(forward).reshape(shape).transpose(0, 2, 1, 3)
    inverse = np.stack(inverse).reshape(plan.lon, plan.table // LANES, LANES, plan.wide)
    return split_table(forward), split_table(inverse)


def fetch_table(place, tabs, held, sems, blocks):
    return [
        pltpu.make_async_copy(tab.at[place, b], held.at[b, k], sems.at[b, k])
        for b in blocks
        for k, tab in enumerate(tabs)
    ]


def split(value):
    high = value.astype(jnp.bfloat16)
    low = (value - high.astype(jnp.float32)).astype(jnp.bfloat16)
    return high, low


def dot(left, right):
    return jnp.dot(left, right, preferred_element_type=jnp.float32)


def three_pass_out(left, right):
    columns = right[0].shape[1]
    both = dot(left[0], jnp.concatenate(right, axis=1))
    return both[:, :columns] + (both[:, columns:] + dot(left[1], right[0]))


def three_pass_in(value, table):
    terms = []
    for at in range(0, value.shape[1], LANES):
        high, low = split(value[:, at : at + LANES])
        terms += [high, low, high]
    return dot(jnp.concatenate(terms, axis=1), table)


def forward_kernel(plan, call, scal, winds, theta, thick, top, bottom, t_high, t_low, *refs):
    places, sets, arrays = plan.places(), field_sets(plan), plan.arrays()[call]
    outs, (points, spectra, held, in_sems, out_sems, t_sems) = refs[: len(arrays)], refs[len(arrays) :]
    levels, width = plan.levels, plan.width
    hemi = scal[3]
    for at, groups in enumerate(plan.roles):

        @pl.when(scal[2] == at)
        def _(at=at, groups=groups):
            targets = {}
            for g in range(len(groups)):
                number, which = next(
                    (n, array[1]) for n, array in enumerate(arrays) if array[0] == places[at, g][0]
                )
                targets[g] = [(number, i, u) for i, u in enumerate(sets[which][at])]
            order = list(range(len(groups)))
            some_fields = {g: [u ^ scal[0] for _, _, u in targets[g]] for g in order}
            turn_of = {g: n % 2 for n, g in enumerate(order)}
            ready = 0

            def first_row(group):
                if group.farthest:
                    return jnp.clip(scal[4] - 1, 0, plan.rows - 1), 0, 1
                first = jnp.where(hemi == 1, plan.rows - group.stop, group.first)
                return first, jnp.where(hemi == 1, group.far, group.near), group.own

            def fetch(g):
                first, slot, count = first_row(groups[g])
                for i, field in enumerate(some_fields[g]):

                    def pieces(source, i=i):
                        for k in range(0, count, PIECE):
                            size = min(PIECE, count - k)
                            pltpu.make_async_copy(
                                source.at[pl.ds(first + k, size)],
                                points.at[turn_of[g], i, pl.ds(slot + k, size)],
                                in_sems.at[turn_of[g], i],
                            ).start()

                    pl.when(field < 2)(lambda: pieces(winds.at[jnp.minimum(field, 1)]))
                    pl.when(field == 2)(lambda: pieces(theta))
                    pl.when(field == 3)(lambda: pieces(thick))

            def arrive(g):
                first, slot, count = first_row(groups[g])
                for i in range(len(targets[g])):
                    pltpu.make_async_copy(
                        theta.at[pl.ds(first, count)],
                        points.at[turn_of[g], i, pl.ds(slot, count)],
                        in_sems.at[turn_of[g], i],
                    ).wait()

            def leave(g, parts):
                group, turn, copies = groups[g], turn_of[g], []
                _, offset = places[at, g]
                size = group.full // parts
                for i, (number, place, _) in enumerate(targets[g]):
                    for k in range(parts if group.full else 0):
                        copies.append(
                            pltpu.make_async_copy(
                                spectra.at[turn, i, pl.ds(k * size, size)],
                                outs[number].at[place, pl.ds(offset + k * size, size)],
                                out_sems.at[turn, i, 0],
                            )
                        )
                    if group.packed:
                        copies.append(
                            pltpu.make_async_copy(
                                spectra.at[turn, i, pl.ds(group.blocks * group.height, group.packed_rows)],
                                outs[number].at[place, pl.ds(offset + group.full, group.packed_rows)],
                                out_sems.at[turn, i, 1],
                            )
                        )
                return copies

            def pack(g, i):
                group, turn = groups[g], turn_of[g]

                def last(slot, count):
                    at_row = pl.multiple_of((group.blocks - 1) * group.height + slot * levels, 8)
                    return spectra[turn, i, pl.ds(at_row, count * levels), :]

                def to(row, count, value):
                    at_row = group.blocks * group.height + row * levels
                    spectra[turn, i, at_row : at_row + count * levels, :] = value

                group.pack(hemi, last, to)

            def halo(g, slot, line, wanted):
                @pl.when(wanted)
                def _():
                    for i, field in enumerate(some_fields[g]):
                        points[turn_of[g], i, slot] = line[field]

            fetch(order[0])
            needed = range(max(groups[g].blocks for g in order))
            for copy in fetch_table(scal[1], (t_high, t_low), held, t_sems, needed):
                copy.start()
            for n, g in enumerate(order):
                group = groups[g]
                if n + 1 < len(order):
                    fetch(order[n + 1])
                arrive(g)
                for copy in fetch_table(scal[1], (t_high, t_low), held, t_sems, range(ready, group.blocks)):
                    copy.wait()
                ready = max(ready, group.blocks)
                if group.farthest:
                    halo(g, 0, top, scal[4] == 0)
                    halo(g, 0, bottom, scal[4] == plan.rows + 1)
                if group.near:
                    halo(g, 0, top, hemi == 0)
                    halo(g, group.slots - 1, bottom, hemi == 1)
                if group.far:
                    halo(g, group.slots - 1, bottom, hemi == 0)
                    halo(g, 0, top, hemi == 1)
                if n >= 2:
                    for copy in leave(order[n - 2], 1):
                        copy.wait()

                def transform(value, group=group):
                    return three_pass_out(
                        split(value),
                        [
                            jnp.concatenate([held[b, half] for b in range(group.blocks)], axis=1)
                            for half in range(2)
                        ],
                    )

                if group.farthest:
                    spec = transform(points[turn_of[g], : len(targets[g]), 0].reshape(len(targets[g]) * levels, width))
                    for i in range(len(targets[g])):
                        for b in range(group.blocks):
                            spectra[turn_of[g], i, b * levels : (b + 1) * levels, :] = spec[
                                i * levels : (i + 1) * levels, b * LANES : (b + 1) * LANES
                            ]
                else:

                    def part(n, _, g=g, group=group, transform=transform):
                        i, slot = n // group.parts, group.chunk_at(lax.rem(n, group.parts))
                        size = group.chunk * levels
                        spec = transform(points[turn_of[g], i, pl.ds(slot, group.chunk)].reshape(size, width))
                        for b in range(group.blocks):
                            target = pl.multiple_of(b * group.height + slot * levels, 8)
                            spectra[turn_of[g], i, pl.ds(target, size), :] = spec[:, b * LANES : (b + 1) * LANES]
                        return 0

                    lax.fori_loop(0, len(targets[g]) * group.parts, part, 0)
                if group.packed:
                    lax.fori_loop(0, len(targets[g]), lambda i, _, g=g: (pack(g, i), 0)[1], 0)
                for copy in leave(g, max(1, group.full // group.height)):
                    copy.start()
            for g in order[-2:]:
                for copy in leave(g, 1):
                    copy.wait()


def forward(plan, call, scal, winds, theta, thick, top, bottom, tabs):
    arrays = plan.arrays()[call]
    count = FIELDS // 2
    shapes = [(FIELDS // 2, plan.heights()[store], LANES) for store, _ in arrays]
    anywhere = pl.BlockSpec(memory_space=pl.ANY)
    halo = pl.BlockSpec((FIELDS, plan.levels, plan.width), lambda i, s: (0, 0, 0))
    slots = max(group.slots for groups in plan.roles for group in groups)
    total = max(group.height * group.blocks + group.packed_rows for groups in plan.roles for group in groups)
    outs = pl.pallas_call(
        functools.partial(forward_kernel, plan, call),
        grid_spec=pltpu.PrefetchScalarGridSpec(
            num_scalar_prefetch=1,
            grid=(1,),
            in_specs=[anywhere] * 3 + [halo, halo, anywhere, anywhere],
            out_specs=[anywhere] * len(arrays),
            scratch_shapes=[
                pltpu.VMEM((2, count, slots, plan.levels, plan.width), jnp.float32),
                pltpu.VMEM((2, count, total, LANES), jnp.float32),
                pltpu.VMEM((plan.table // LANES, 2, plan.width, LANES), jnp.bfloat16),
                pltpu.SemaphoreType.DMA((2, count)),
                pltpu.SemaphoreType.DMA((2, count, 2)),
                pltpu.SemaphoreType.DMA((plan.table // LANES, 2)),
            ],
        ),
        out_shape=[jax.ShapeDtypeStruct(shape, jnp.float32) for shape in shapes],
        compiler_params=pltpu.CompilerParams(vmem_limit_bytes=VMEM),
        cost_estimate=pl.CostEstimate(flops=FORWARD_COST, bytes_accessed=0, transcendentals=0),
        name="partial_spectra",
    )(scal, winds, theta, thick, top, bottom, *tabs)
    return dict(zip(arrays, outs))


def edge_kernel(plan, count, _, *refs):
    ins, outs = refs[:-2], refs[-2:]
    lane = lax.broadcasted_iota(jnp.int32, (plan.levels, LANES), 1)
    some = plan.rows // count
    for side, column in enumerate((0, (plan.width - 1) % LANES)):
        kept = (jnp.zeros((plan.levels, LANES), jnp.float32),) * FIELDS
        for piece in range(count):
            at = (side * count + piece) * FIELDS
            fields = ins[at : at + FIELDS]

            def pick(row, kept, fields=fields, piece=piece, column=column):
                values = (fields[0][0, row], fields[1][0, row], fields[2][row], fields[3][row])
                return tuple(
                    jnp.where(lane == row + piece * some, value[:, column : column + 1], old)
                    for value, old in zip(values, kept)
                )

            kept = lax.fori_loop(0, some, pick, kept, unroll=max(k for k in range(1, 11) if some % k == 0))
        for field in range(FIELDS):
            outs[side][field] = kept[field]


def edges(plan, after, winds, theta, thick):
    count = 3 if plan.rows % 3 == 0 else 1
    some = plan.rows // count
    specs = []
    for at in (0, (plan.width - 1) // LANES):
        for piece in range(count):
            for wind in range(2):
                specs.append(
                    pl.BlockSpec(
                        (1, some, plan.levels, LANES), lambda i, w=wind, p=piece, at=at: (w, p, 0, at)
                    )
                )
            specs += [pl.BlockSpec((some, plan.levels, LANES), lambda i, p=piece, at=at: (p, 0, at))] * 2
    shape = (FIELDS, plan.levels, LANES)
    return pl.pallas_call(
        functools.partial(edge_kernel, plan, count),
        grid=(1,),
        in_specs=[pl.BlockSpec(memory_space=pl.ANY)] + specs,
        out_specs=[pl.BlockSpec(shape, lambda i: (0, 0, 0))] * 2,
        out_shape=[jax.ShapeDtypeStruct(shape, jnp.float32)] * 2,
        compiler_params=pltpu.CompilerParams(vmem_limit_bytes=VMEM),
        cost_estimate=pl.CostEstimate(flops=EDGE_COST, bytes_accessed=0, transcendentals=0),
        name="edge_columns",
    )(after, *[winds, winds, theta, thick] * (2 * count))


def step_kernel(plan, step_rows, scal, coef, west, east, top, bottom, cuts, i_high, i_low, *refs):
    places, heights = plan.places(), plan.heights()
    halves = plan.levels // 8
    raw, refs = refs[: FIELDS * halves], refs[FIELDS * halves :]
    spectra = refs[: FIELDS * len(heights)]
    new_wind, new_theta, new_thick, held, sums, unpacked, table, ready, sems, t_sems, out_sems = refs[FIELDS * len(heights) :]
    step = pl.program_id(0)
    rows, width, wide, levels = plan.rows, plan.width, plan.wide, plan.levels
    last_step = rows // step_rows

    def inverse(at, groups):
        source = [0, 1, 2, 3] if plan.parts > 1 or at % 2 == 0 else [0, 2, 1, 3]
        slot_at = np.cumsum([0] + [group.slots for group in groups])
        row_at = np.cumsum([0] + [group.total for group in groups])

        def copies(g):
            number, offset = places[at, g]
            return [
                pltpu.make_async_copy(
                    spectra[number * FIELDS + source[u]].at[pl.ds(offset, groups[g].total)],
                    sums.at[u, pl.ds(int(row_at[g]), groups[g].total)],
                    sems.at[g, u],
                )
                for u in range(FIELDS)
            ]

        have = 0
        for g, group in enumerate(groups):
            for copy in copies(g):
                copy.start()
            for copy in fetch_table(scal[1], (i_high, i_high, i_low), table, t_sems, range(have, group.blocks)):
                copy.start()
            have = max(have, group.blocks)
        have = 0
        for g, group in enumerate(groups):
            for copy in copies(g):
                copy.wait()
            for copy in fetch_table(scal[1], (i_high, i_high, i_low), table, t_sems, range(have, group.blocks)):
                copy.wait()
            have = max(have, group.blocks)
            lanes = group.blocks * LANES
            first_slot, first_sum = int(slot_at[g]), int(row_at[g])

            def back_of(spec, size, lanes=lanes, group=group):
                back = three_pass_in(spec, table[: group.blocks].reshape(3 * lanes, wide))
                return back.reshape(size, levels, wide)

            def masked(u, slot, size, group=group, first_slot=first_slot, first_sum=first_sum):
                rows_at = pl.ds(pl.multiple_of((first_slot + slot) * levels, 8), size)
                cut = cuts[rows_at, :]
                lane = lax.broadcasted_iota(jnp.int32, (size, LANES), 1)
                pieces = []
                for b in range(group.blocks):
                    keep = lax.shift_right_logical(lane + (b * LANES + 1), 1) <= cut
                    if group.packed and b == group.blocks - 1:
                        value = unpacked[u, pl.ds(pl.multiple_of(slot * levels, 8), size), :]
                    else:
                        source = pl.multiple_of(first_sum + b * group.height + slot * levels, 8)
                        value = sums[u, pl.ds(source, size), :]
                    pieces.append(jnp.where(keep, value, 0.0))
                return jnp.concatenate(pieces, axis=1)

            def unpack(u, _, group=group, first_sum=first_sum):
                def packed(row, count):
                    at_row = first_sum + group.full + row * levels
                    return sums[u, at_row : at_row + count * levels, :]

                def to(slot, count, value):
                    at_row = pl.multiple_of(slot * levels, 8)
                    unpacked[u, pl.ds(at_row, count * levels), :] = value

                group.unpack(scal[3], packed, to)
                return 0

            if group.packed:
                lax.fori_loop(0, FIELDS, unpack, 0)
            if group.farthest:
                spec = jnp.concatenate([masked(u, 0, levels) for u in range(FIELDS)], axis=0)
                back = back_of(spec, FIELDS)

                @pl.when(scal[4] >= 0)
                def _(back=back):
                    for u in range(FIELDS):
                        held[u ^ scal[0], scal[4]] = back[u]
            else:
                start = group.start(scal[3], rows)

                def part(n, _, group=group, start=start, masked=masked, back_of=back_of):
                    u, slot = n // group.parts, group.chunk_at(lax.rem(n, group.parts))
                    back = back_of(masked(u, slot, group.chunk * levels), group.chunk)
                    held[u ^ scal[0], pl.ds(start + slot, group.chunk)] = back
                    return 0

                lax.fori_loop(0, FIELDS * group.parts, part, 0)

    @pl.when(step == 0)
    def _():
        for at, groups in enumerate(plan.roles):
            pl.when(scal[2] == at)(functools.partial(inverse, at, groups))
        for side, line in enumerate((top, bottom)):

            @pl.when(scal[5 + side] == 0)
            def _(side=side, line=line):
                for field in range(FIELDS):
                    held[field, side * (rows + 1), :, :width] = line[field]

    base = step * step_rows
    tail = width % LANES

    @pl.when(step < last_step)
    def _():
        lane = lax.broadcasted_iota(jnp.int32, (levels, LANES), 1)

        def load(n, _):
            at = n
            row = base + n
            is_raw = (row >= scal[7]) & (row < scal[8])
            for field in range(FIELDS):
                for half in range(halves):
                    piece = raw[field * halves + half]
                    some = slice(half * 8, half * 8 + 8)
                    value = piece[0, at] if field < 2 else piece[at]
                    held[field, row + 1, some, :width] = jnp.where(
                        is_raw, value, held[field, row + 1, some, :width]
                    )
                beyond = jnp.where(
                    lane == tail,
                    pltpu.roll(east[field], (tail + LANES - row) & (LANES - 1), 1),
                    pltpu.roll(west[field], (2 * LANES - 1 - row) & (LANES - 1), 1),
                )
                held[field, row + 1, :, width:] = jnp.where(
                    is_raw, beyond[:, tail:], held[field, row + 1, :, width:]
                )
            return 0

        @pl.when((base < scal[8]) & (base + step_rows > scal[7]))
        def _():
            lax.fori_loop(0, step_rows, load, 0, unroll=3 if step_rows % 3 == 0 else 1)

    slot = step % 2
    count = wide // LANES
    lane = lax.broadcasted_iota(jnp.int32, (8, LANES), 1)
    is_first, is_last = lane == 0, lane == LANES - 1

    def stencil(row, _):
        at = base - step_rows + row
        along, across, push, turn, cos_north, cos_south = [coef[k * rows + at] for k in range(6)]
        across_north, across_south = across * cos_north, across * cos_south
        for part in range(levels // 8):
            some = pl.ds(part * 8, 8)

            def load(field, shift, k):
                return held[field, at + shift, some, k * LANES : (k + 1) * LANES]

            here = [
                functools.lru_cache(maxsize=None)(lambda k, field=field: load(field, 1, k))
                for field in range(FIELDS)
            ]
            up = [functools.lru_cache(maxsize=None)(lambda k, f=f: pltpu.roll(f(k), LANES - 1, 1)) for f in here]
            down = [functools.lru_cache(maxsize=None)(lambda k, f=f: pltpu.roll(f(k), 1, 1)) for f in here]

            def shifted(which, k):
                return (
                    jnp.where(is_last, up[which]((k + 1) % count), up[which](k)),
                    jnp.where(is_first, down[which]((k - 1) % count), down[which](k)),
                )

            for k in range(count):
                stop = min(width, (k + 1) * LANES)

                def put(field, piece, k=k, stop=stop):
                    ready[slot, field, row, some, k * LANES : stop] = piece[:, : stop - k * LANES]

                u, v, t, h = [here[field](k) for field in range(FIELDS)]
                advect, carry = along * u, 0.1 * v
                (u_e, u_w), (v_e, v_w), (t_e, t_w), (h_e, h_w) = [shifted(field, k) for field in range(FIELDS)]
                v_n, v_s, h_n, h_s = load(1, 0, k), load(1, 2, k), load(3, 0, k), load(3, 2, k)
                put(
                    3,
                    h
                    - along * (u_e * h_e - u_w * h_w)
                    - (across_south * (v_s * h_s) - across_north * (v_n * h_n)),
                )
                put(
                    1,
                    v
                    - advect * (v_e - v_w)
                    - carry * (v_s - v_n)
                    - 0.15 * (h_s - h_n)
                    - turn * u,
                )
                put(
                    0,
                    u
                    - advect * (u_e - u_w)
                    - carry * (load(0, 2, k) - load(0, 0, k))
                    - push * (h_e - h_w)
                    + turn * v,
                )
                put(2, t - advect * (t_e - t_w) - carry * (load(2, 2, k) - load(2, 0, k)))
        return 0

    outs = (new_wind.at[0], new_wind.at[1], new_theta, new_thick)

    def leave(at_step, size, act):
        for field, out in enumerate(outs):
            for k in range(0, step_rows, size):
                act(
                    pltpu.make_async_copy(
                        ready.at[at_step % 2, field, pl.ds(k, size)],
                        out.at[pl.ds((at_step - 1) * step_rows + k, size)],
                        out_sems.at[at_step % 2, field],
                    )
                )

    @pl.when(step > 2)
    def _():
        leave(step - 2, step_rows, lambda copy: copy.wait())

    @pl.when(step > 0)
    def _():
        lax.fori_loop(0, step_rows, stencil, 0, unroll=5 if step_rows % 5 == 0 else 1)
        leave(step, PIECE if step_rows % PIECE == 0 else step_rows, lambda copy: copy.start())

    @pl.when(step == last_step)
    def _():
        if last_step > 1:
            leave(step - 1, step_rows, lambda copy: copy.wait())
        leave(step, step_rows, lambda copy: copy.wait())


def substep(plan, step_rows, scal, coef, winds, theta, thick, west, east, top, bottom, cuts, tabs, spectra):
    rows, width, levels = plan.rows, plan.width, plan.levels
    once = pl.Buffered(1)
    steps = rows // step_rows

    def block(i, s):
        return jnp.clip(i, s[9], s[10])

    def whole(shape):
        return pl.BlockSpec(shape, lambda i, s: (0,) * len(shape), pipeline_mode=once)

    anywhere = pl.BlockSpec(memory_space=pl.ANY)
    halves = range(levels // 8)
    raw_specs = [
        pl.BlockSpec((1, step_rows, 8, width), lambda i, s, w=wind, h=half: (w, block(i, s), h, 0))
        for wind in range(2)
        for half in halves
    ] + [
        pl.BlockSpec((step_rows, 8, width), lambda i, s, h=half: (block(i, s), h, 0))
        for _ in range(2)
        for half in halves
    ]
    raw = [array for array in (winds, winds, theta, thick) for _ in halves]
    edge, halo = (FIELDS, levels, LANES), (FIELDS, levels, width)
    in_specs = [
        pl.BlockSpec(memory_space=pltpu.SMEM),
        whole(edge),
        whole(edge),
        whole(halo),
        whole(halo),
        whole((plan.slots * levels, LANES)),
        anywhere,
        anywhere,
    ] + raw_specs + [anywhere] * len(spectra)
    shapes = [(2, rows, levels, width)] + [(rows, levels, width)] * 2
    most = max(sum(group.total for group in groups) for groups in plan.roles)
    return pl.pallas_call(
        functools.partial(step_kernel, plan, step_rows),
        grid_spec=pltpu.PrefetchScalarGridSpec(
            num_scalar_prefetch=1,
            grid=(steps + 1,),
            in_specs=in_specs,
            out_specs=[anywhere] * 3,
            scratch_shapes=[
                pltpu.VMEM((FIELDS, rows + 2, levels, plan.wide), jnp.float32),
                pltpu.VMEM((FIELDS, most, LANES), jnp.float32),
                pltpu.VMEM((FIELDS, max(group.height for groups in plan.roles for group in groups), LANES), jnp.float32),
                pltpu.VMEM((plan.table // LANES, 3, LANES, plan.wide), jnp.bfloat16),
                pltpu.VMEM((2, FIELDS, step_rows, levels, width), jnp.float32),
                pltpu.SemaphoreType.DMA((max(len(groups) for groups in plan.roles), FIELDS)),
                pltpu.SemaphoreType.DMA((plan.table // LANES, 3)),
                pltpu.SemaphoreType.DMA((2, FIELDS)),
            ],
        ),
        out_shape=[jax.ShapeDtypeStruct(shape, jnp.float32) for shape in shapes],
        compiler_params=pltpu.CompilerParams(vmem_limit_bytes=VMEM),
        cost_estimate=pl.CostEstimate(
            flops=6 * most * FIELDS * LANES * plan.wide, bytes_accessed=40_000_000, transcendentals=0
        ),
        name="inverse_and_substep",
    )(scal, coef, west, east, top, bottom, cuts, *tabs, *raw, *spectra)


def lon_swap(plan, value, moves):
    pairs = [
        (block * plan.lon + place, block * plan.lon + (place ^ (1 << bit)))
        for blocks, bit in moves
        for block in blocks
        for place in range(plan.lon)
    ]
    return lax.ppermute(value, ("lat", "lon"), pairs)


def lat_move(plan, value, sources, targets):
    pairs = [
        (source * plan.lon + place, target * plan.lon + place)
        for source, target in zip(sources, targets)
        for place in range(plan.lon)
    ]
    return lax.ppermute(value, ("lat", "lon"), pairs)


def gather_sums(plan, blocks, slots, order):
    slots = dict(slots)
    for bit in order:
        sent = [s for s in slots if s >> bit & 1]
        for s in sorted(sent, key=lambda s: -bin(s).count("1")):
            moved = lon_swap(plan, slots.pop(s), [(blocks, bit)])
            slots[s ^ (1 << bit)] = slots[s ^ (1 << bit)] + moved
    for bit in reversed(order):
        for s in sorted(slots):
            slots[s | (1 << bit)] = lon_swap(plan, slots[s], [(blocks, bit)])
    return slots


def field_sets(plan):
    sent, kept = [], []
    for at in range(len(plan.roles)):
        bit = at % 2
        sent.append([u for u in range(FIELDS) if u >> bit & 1])
        kept.append([u for u in range(FIELDS) if not u >> bit & 1])
    return sent, kept


def store_sums(plan, members, sent, kept):
    near = [(blocks, bit) for blocks, bit in members]
    far = [(blocks, 1 - bit) for blocks, bit in members]
    moved = lon_swap(plan, sent, near)
    own = (kept[0] + moved[0]) + lon_swap(plan, kept[1] + moved[1], far)
    across = lon_swap(plan, own, far)
    beside = lon_swap(plan, own, near)
    return own, beside, across, lon_swap(plan, across, near)


def split_sums(plan, place, at, sent, kept):
    first, second = field_sets(plan)
    parts, own = plan.parts, place % plan.parts
    bits = plan.lon.bit_length() - 1
    slots = {}
    for us, array in ((first[at], sent), (second[at], kept)):
        for i, u in enumerate(us):
            pieces = array[i].reshape(parts, -1, LANES)
            for k in range(parts):
                slots[u * parts + k] = pieces[k ^ own]
    order = list(range(bits)) if at % 2 == 0 else list(reversed(range(bits)))
    slots = gather_sums(plan, plan.blocks(at), slots, order)
    result = []
    for u in range(FIELDS):
        pieces = jnp.stack([slots[u * parts + k] for k in range(parts)])
        result.append(pieces[jnp.arange(parts) ^ own].reshape(-1, LANES))
    return result


def all_sums(plan, place, arrays):
    result = []
    for number, store in enumerate(plan.stores()):
        first, second = arrays[number, 0], arrays[number, 1]
        if plan.parts > 1:
            result += split_sums(plan, place, store[0][0], first, second)
        elif store[0][1] == 0:
            result += store_sums(plan, [(plan.blocks(at), at % 2) for at, _ in store], first, second)
        else:
            at = store[0][0]
            home, helpers = plan.blocks(at), plan.blocks(at + len(plan.roles))
            first, second = [lat_move(plan, array, home, helpers) for array in (first, second)]
            own, near, far, both = store_sums(plan, [(helpers, at % 2)], first, second)
            own, far = lax.optimization_barrier((own, far))
            result += [lat_move(plan, array, helpers, home) for array in (own, near, far, both)]
    return result


def body(winds, theta, thick, polar_rows, cutoffs):
    lat, lon = lax.axis_size("lat"), lax.axis_size("lon")
    levels, rows, width = theta.shape
    sizes = (lat, lon, levels, rows, width, polar_rows.shape[0])
    plan = Plan(*sizes)
    t_tabs, i_tabs = [tuple(jnp.asarray(part) for part in pair) for pair in tables(sizes)]
    block, place = lax.axis_index("lat"), lax.axis_index("lon")
    winds = winds.transpose(0, 2, 1, 3)
    theta = theta.transpose(1, 0, 2)
    thick = thick.transpose(1, 0, 2)
    hemi = (block >= lat // 2).astype(jnp.int32)
    role = jnp.where(hemi == 1, lat - 1 - block, block)

    def line(row):
        return jnp.stack([winds[0, row], winds[1, row], theta[row], thick[row]])

    south_pairs = [(b * lon + p, (b + 1) * lon + p) for b in range(lat - 1) for p in range(lon)]
    north_pairs = [(to, at) for at, to in south_pairs]
    top = lax.ppermute(line(rows - 1), ("lat", "lon"), south_pairs)
    bottom = lax.ppermute(line(0), ("lat", "lon"), north_pairs)

    step_rows = max(k for k in range(1, 16) if rows % k == 0)
    listed = polar_rows.shape[0]
    north_run = jnp.sum((polar_rows < plan.total_rows // 2).astype(jnp.int32))
    south_first = plan.total_rows - listed + north_run
    far_row = jnp.where(hemi == 1, south_first, north_run - 1)
    far_at = far_row - block * rows + 1
    far_at = jnp.where((far_at >= 0) & (far_at <= rows + 1), far_at, -1)
    raw_from = jnp.clip(north_run - block * rows, 0, rows)
    raw_to = jnp.clip(south_first - block * rows, 0, rows)
    block_from = jnp.minimum(raw_from, rows - 1) // step_rows
    block_to = jnp.maximum(block_from, jnp.maximum(raw_to - 1, 0) // step_rows)
    above, below = block * rows - 1, (block + 1) * rows

    def is_listed(row):
        return (row >= 0) & (row < plan.total_rows) & ((row < north_run) | (row >= south_first))

    facts = [
        place // plan.parts, place, role, hemi, far_at, is_listed(above), is_listed(below),
        raw_from, raw_to, block_from, block_to,
    ]
    scal = jnp.stack([jnp.asarray(fact).astype(jnp.int32) for fact in facts])

    first_edge, last_edge = edges(plan, scal, winds, theta, thick)
    some = [b for b in range(lat) if (min(b, lat - 1 - b) + 1) * rows > plan.low]
    east_pairs = [(b * lon + i, b * lon + (i + 1) % lon) for b in some for i in range(lon)]
    west = lax.ppermute(last_edge, ("lat", "lon"), east_pairs)
    east = lax.ppermute(first_edge, ("lat", "lon"), [(to, at) for at, to in east_pairs])

    scal, _ = lax.optimization_barrier((scal, first_edge))
    arrays = forward(plan, 0, scal, winds, theta, thick, top, bottom, t_tabs)
    scal, _ = lax.optimization_barrier((scal, arrays[plan.arrays()[0][0]]))
    later = forward(plan, 1, scal, winds, theta, thick, top, bottom, t_tabs)
    added = {key: array for key, array in later.items() if plan.stores()[key[0]][0][1] == 0}
    added, west, east = lax.optimization_barrier((added, west, east))
    arrays = {**arrays, **later, **added}
    sums = all_sums(plan, place, arrays)

    slot_rows = jnp.asarray(plan.slot_rows())[jnp.minimum(role, len(plan.roles) - 1), hemi]
    slot_rows = jnp.where(slot_rows == -2, far_at, slot_rows)
    hits = (polar_rows[None, :] == (slot_rows - 1 + block * rows)[:, None]) & (slot_rows >= 0)[:, None]
    cut = jnp.sum(jnp.where(hits, cutoffs[None, :] + 1, 0), axis=1) - 1
    cuts = jnp.broadcast_to(cut.astype(jnp.int32)[:, None, None], (plan.slots, levels, LANES))
    cuts = cuts.reshape(plan.slots * levels, LANES)

    ring = block * rows - 1 + jnp.arange(rows + 2, dtype=jnp.int32)
    centre = (ring.astype(jnp.float32) + 0.5) * (jnp.pi / plan.total_rows)
    cos, sin = jnp.sin(centre), -jnp.cos(centre)
    mid = cos[1:-1]
    coef = jnp.concatenate([0.025 / mid, 0.1 / mid, 0.05 / mid, 0.3 * sin[1:-1], cos[:-2], cos[2:]])

    out = substep(
        plan, step_rows, scal, coef, winds, theta, thick, west, east, top, bottom, cuts, i_tabs, sums
    )
    return (out[0].transpose(0, 2, 1, 3), out[1].transpose(1, 0, 2), out[2].transpose(1, 0, 2))


def solution(mesh):
    in_specs = (P(None, None, "lat", "lon"), P(None, "lat", "lon"), P(None, "lat", "lon"), P(), P())
    out_specs = (P(None, None, "lat", "lon"), P(None, "lat", "lon"), P(None, "lat", "lon"))
    return jax.shard_map(body, mesh=mesh, in_specs=in_specs, out_specs=out_specs, check_vma=False)
```

```python
import functools

import jax
import jax.numpy as jnp
import ml_dtypes
import numpy as np
from jax import lax
from jax.experimental import pallas as pl
from jax.experimental.pallas import tpu as pltpu
from jax.sharding import PartitionSpec as P

FIELDS = 4
LANES = 128
PIECE = 3
VMEM = 60 * 1024 * 1024
FORWARD_COST, EDGE_COST = 5_000_000_000, 5_000_000_000


def round_up(value, step):
    return -(-value // step) * step


class Group:
    def __init__(self, first, stop, near, far, blocks, levels, quarters):
        self.first, self.stop, self.blocks, self.levels = first, stop, blocks, levels
        self.near, self.far = int(near), int(far)
        self.own = stop - first
        self.farthest = self.own == 0
        self.slots = 1 if self.farthest else self.own + self.near + self.far
        self.height = self.slots * levels
        self.quarters = list(quarters)
        assert sum(self.quarters) == self.slots
        one, two, three, four = self.quarters
        self.beside = max(one, three) if one and three else 0
        self.half = -(-two // 2)
        self.packed = self.beside > 0 or two > 1
        self.pieces = []
        if self.packed:
            if not self.beside:
                for start, count in ((0, one), (one + two, three)):
                    if count:
                        self.pieces.append((0, start, count))
            if four:
                self.pieces.append((0, one + two + three, four))
        self.whole_rows = sum(piece[2] for piece in self.pieces)
        self.full = self.height * (blocks - 1 if self.packed else blocks)
        self.packed_rows = (self.whole_rows + self.beside + self.half) * levels if self.packed else 0
        self.total = self.full + self.packed_rows
        parts = max(1, round(self.slots / 16))
        self.chunk = -(-self.slots // parts)
        self.parts = -(-self.slots // self.chunk)

    def start(self, hemi, rows):
        return jnp.where(hemi == 1, rows - self.stop + 1 - self.far, self.first + 1 - self.near)

    def chunk_at(self, part):
        return jnp.minimum(part * self.chunk, self.slots - self.chunk)

    def slot(self, hemi, first, count):
        first = min(first, self.slots - count)
        return jnp.where(hemi == 1, self.slots - count - first, first)

    def pairs(self):
        one, two, three, _ = self.quarters
        result = []
        if self.beside:
            result.append((one + two, 0, self.beside, 96))
        if two:
            result.append((one, one + two - self.half, self.half, 64))
        return result

    def pack(self, hemi, last, to):
        row = 0
        for _, first, count in self.pieces:
            to(row, count, last(self.slot(hemi, first, count), count))
            row += count
        for left, right, count, lanes in self.pairs():
            lane = lax.broadcasted_iota(jnp.int32, (count * self.levels, LANES), 1)
            beside = pltpu.roll(last(self.slot(hemi, right, count), count), lanes, 1)
            to(row, count, jnp.where(lane < lanes, last(self.slot(hemi, left, count), count), beside))
            row += count

    def unpack(self, hemi, packed, to):
        row = self.whole_rows
        for left, right, count, lanes in self.pairs():
            value = packed(row, count)
            to(self.slot(hemi, left, count), count, value)
            to(self.slot(hemi, right, count), count, pltpu.roll(value, LANES - lanes, 1))
            row += count
        row = 0
        for _, first, count in self.pieces:
            to(self.slot(hemi, first, count), count, packed(row, count))
            row += count


class Plan:
    def __init__(self, lat, lon, levels, rows, width, listed):
        self.lat, self.lon, self.levels, self.rows, self.width = lat, lon, levels, rows, width
        self.total_rows, self.length = lat * rows, lon * width
        self.parts = lon // FIELDS
        self.wide = round_up(width + 2, LANES)
        pole = listed // 2
        self.low, self.high = pole - pole // 4, pole + pole // 4
        top = self.length // 4 - 1

        def blocks_of(depth):
            return -(-(2 * min(2 * (depth + 1), top) + 1) // LANES)

        self.roles = []
        last = self.high - 2
        for role in range(lat // 2):
            start = role * rows
            if start > last:
                break
            need = {}
            for depth in range(start, min(start + rows - 1, last) + 1):
                need.setdefault(blocks_of(depth), []).append(depth - start)
            spans = [[need[k][0], need[k][-1] + 1, False, False, k] for k in sorted(need)]
            if role > 0:
                spans[0][2], spans[0][4] = True, max(spans[0][4], blocks_of(start - 1))
            if start + rows <= last:
                spans[-1][3], spans[-1][4] = True, max(spans[-1][4], blocks_of(start + rows))
            groups = []
            for first, stop, near, far, blocks in spans:
                depths = range(start + first - int(near), start + stop + int(far))
                quarters = [0] * 4
                for depth in depths:
                    lanes = 2 * min(2 * (depth + 1), top) + 1 - (blocks - 1) * LANES
                    quarters[max(0, -(-lanes // (LANES // 4)) - 1)] += 1
                groups.append(Group(first, stop, near, far, blocks, levels, quarters))
            groups.append(Group(0, 0, False, False, -(-(2 * top + 1) // LANES), levels, (0, 0, 0, 1)))
            self.roles.append(groups)
        self.slots = max(sum(group.slots for group in groups) for groups in self.roles)
        self.table = LANES * max(group.blocks for groups in self.roles for group in groups)
        count = len(self.roles)
        self.lent = {}
        if self.parts == 1 and 2 * count <= lat // 2:
            self.lent = {count - 1: len(self.roles[-1]) - 2}

    def blocks(self, role):
        return (role, self.lat - 1 - role)

    def parcels(self, at):
        indices = range(len(self.roles[at]))
        away = self.lent.get(at)
        home = [g for g in indices if g != away]
        return [home] if away is None else [home, [away]]

    def stores(self):
        result = []
        for at in range(len(self.roles)):
            size = self.height_of(at, 0)
            for store in result:
                sizes = [self.height_of(*member) for member in store]
                if self.parts == 1 and max(sizes + [size]) <= 1.1 * min(sizes + [size]):
                    store.append((at, 0))
                    break
            else:
                result.append([(at, 0)])
        return result + [[(at, 1)] for at in self.lent]

    def arrays(self):
        return [[(store, which) for store in range(len(self.stores()))] for which in range(2)]

    def places(self):
        result = {}
        for number, store in enumerate(self.stores()):
            for at, parcel in store:
                offset = 0
                for g in self.parcels(at)[parcel]:
                    result[at, g] = (number, offset)
                    offset += self.roles[at][g].total
        return result

    def height_of(self, at, parcel):
        return sum(self.roles[at][g].total for g in self.parcels(at)[parcel])

    def heights(self):
        return [max(self.height_of(*member) for member in store) for store in self.stores()]

    def slot_rows(self):
        table = np.full((len(self.roles), 2, self.slots), -1, np.int32)
        for at, groups in enumerate(self.roles):
            for hemi in range(2):
                rows = []
                for group in groups:
                    first = group.first + 1 - group.near if hemi == 0 else self.rows - group.stop + 1 - group.far
                    rows += [-2] if group.farthest else [first + k for k in range(group.slots)]
                table[at, hemi, : len(rows)] = rows
        return table


def split_table(table):
    high = table.astype(ml_dtypes.bfloat16)
    low = (table - high.astype(np.float64)).astype(ml_dtypes.bfloat16)
    return high, low


@functools.lru_cache(maxsize=None)
def tables(sizes):
    plan = Plan(*sizes)
    index = np.arange(plan.table)
    wave, odd = (index + 1) // 2, (index % 2 == 0) & (index > 0)
    used = wave < plan.length // 4
    points = np.zeros(plan.wide, np.int64)
    points[: plan.width + 1] = np.arange(plan.width + 1)
    points[-1] = -1
    shown = np.zeros(plan.wide, bool)
    shown[: plan.width + 1] = True
    shown[-1] = True

    def trig(at):
        angle = (wave[:, None] * at[None, :]) % plan.length * (2.0 * np.pi / plan.length)
        return np.where(odd[:, None], np.sin(angle), np.cos(angle)) * used[:, None]

    weight = np.where(wave == 0, 1.0, 2.0) / plan.length
    forward, inverse = [], []
    for place in range(plan.lon):
        forward.append(trig(place * plan.width + np.arange(plan.width)).T)
        inverse.append(trig(place * plan.width + points) * weight[:, None] * shown[None, :])
    shape = (plan.lon, plan.width, plan.table // LANES, LANES)
    forward = np.stack(forward).reshape(shape).transpose(0, 2, 1, 3)
    inverse = np.stack(inverse).reshape(plan.lon, plan.table // LANES, LANES, plan.wide)
    return split_table(forward), split_table(inverse)


def fetch_table(place, tabs, held, sems, blocks):
    return [
        pltpu.make_async_copy(tab.at[place, b], held.at[b, k], sems.at[b, k])
        for b in blocks
        for k, tab in enumerate(tabs)
    ]


def split(value):
    high = value.astype(jnp.bfloat16)
    low = (value - high.astype(jnp.float32)).astype(jnp.bfloat16)
    return high, low


def dot(left, right):
    return jnp.dot(left, right, preferred_element_type=jnp.float32)


def three_pass_out(left, right):
    columns = right[0].shape[1]
    both = dot(left[0], jnp.concatenate(right, axis=1))
    return both[:, :columns] + (both[:, columns:] + dot(left[1], right[0]))


def three_pass_in(value, table):
    terms = []
    for at in range(0, value.shape[1], LANES):
        high, low = split(value[:, at : at + LANES])
        terms += [high, low, high]
    return dot(jnp.concatenate(terms, axis=1), table)


def forward_kernel(plan, call, scal, winds, theta, thick, top, bottom, t_high, t_low, *refs):
    places, sets, arrays = plan.places(), field_sets(plan), plan.arrays()[call]
    outs, (points, spectra, held, in_sems, out_sems, t_sems) = refs[: len(arrays)], refs[len(arrays) :]
    levels, width = plan.levels, plan.width
    hemi = scal[3]
    for at, groups in enumerate(plan.roles):

        @pl.when(scal[2] == at)
        def _(at=at, groups=groups):
            targets = {}
            for g in range(len(groups)):
                number, which = next(
                    (n, array[1]) for n, array in enumerate(arrays) if array[0] == places[at, g][0]
                )
                targets[g] = [(number, i, u) for i, u in enumerate(sets[which][at])]
            order = list(range(len(groups)))
            some_fields = {g: [u ^ scal[0] for _, _, u in targets[g]] for g in order}
            turn_of = {g: n % 2 for n, g in enumerate(order)}
            ready = 0

            def first_row(group):
                if group.farthest:
                    return jnp.clip(scal[4] - 1, 0, plan.rows - 1), 0, 1
                first = jnp.where(hemi == 1, plan.rows - group.stop, group.first)
                return first, jnp.where(hemi == 1, group.far, group.near), group.own

            def fetch(g):
                first, slot, count = first_row(groups[g])
                for i, field in enumerate(some_fields[g]):

                    def pieces(source, i=i):
                        for k in range(0, count, PIECE):
                            size = min(PIECE, count - k)
                            pltpu.make_async_copy(
                                source.at[pl.ds(first + k, size)],
                                points.at[turn_of[g], i, pl.ds(slot + k, size)],
                                in_sems.at[turn_of[g], i],
                            ).start()

                    pl.when(field < 2)(lambda: pieces(winds.at[jnp.minimum(field, 1)]))
                    pl.when(field == 2)(lambda: pieces(theta))
                    pl.when(field == 3)(lambda: pieces(thick))

            def arrive(g):
                first, slot, count = first_row(groups[g])
                for i in range(len(targets[g])):
                    pltpu.make_async_copy(
                        theta.at[pl.ds(first, count)],
                        points.at[turn_of[g], i, pl.ds(slot, count)],
                        in_sems.at[turn_of[g], i],
                    ).wait()

            def leave(g, parts):
                group, turn, copies = groups[g], turn_of[g], []
                _, offset = places[at, g]
                size = group.full // parts
                for i, (number, place, _) in enumerate(targets[g]):
                    for k in range(parts if group.full else 0):
                        copies.append(
                            pltpu.make_async_copy(
                                spectra.at[turn, i, pl.ds(k * size, size)],
                                outs[number].at[place, pl.ds(offset + k * size, size)],
                                out_sems.at[turn, i, 0],
                            )
                        )
                    if group.packed:
                        copies.append(
                            pltpu.make_async_copy(
                                spectra.at[turn, i, pl.ds(group.blocks * group.height, group.packed_rows)],
                                outs[number].at[place, pl.ds(offset + group.full, group.packed_rows)],
                                out_sems.at[turn, i, 1],
                            )
                        )
                return copies

            def pack(g, i):
                group, turn = groups[g], turn_of[g]

                def last(slot, count):
                    at_row = pl.multiple_of((group.blocks - 1) * group.height + slot * levels, 8)
                    return spectra[turn, i, pl.ds(at_row, count * levels), :]

                def to(row, count, value):
                    at_row = group.blocks * group.height + row * levels
                    spectra[turn, i, at_row : at_row + count * levels, :] = value

                group.pack(hemi, last, to)

            def halo(g, slot, line, wanted):
                @pl.when(wanted)
                def _():
                    for i, field in enumerate(some_fields[g]):
                        points[turn_of[g], i, slot] = line[field]

            fetch(order[0])
            needed = range(max(groups[g].blocks for g in order))
            for copy in fetch_table(scal[1], (t_high, t_low), held, t_sems, needed):
                copy.start()
            for n, g in enumerate(order):
                group = groups[g]
                if n + 1 < len(order):
                    fetch(order[n + 1])
                arrive(g)
                for copy in fetch_table(scal[1], (t_high, t_low), held, t_sems, range(ready, group.blocks)):
                    copy.wait()
                ready = max(ready, group.blocks)
                if group.farthest:
                    halo(g, 0, top, scal[4] == 0)
                    halo(g, 0, bottom, scal[4] == plan.rows + 1)
                if group.near:
                    halo(g, 0, top, hemi == 0)
                    halo(g, group.slots - 1, bottom, hemi == 1)
                if group.far:
                    halo(g, group.slots - 1, bottom, hemi == 0)
                    halo(g, 0, top, hemi == 1)
                if n >= 2:
                    for copy in leave(order[n - 2], 1):
                        copy.wait()

                def transform(value, group=group):
                    return three_pass_out(
                        split(value),
                        [
                            jnp.concatenate([held[b, half] for b in range(group.blocks)], axis=1)
                            for half in range(2)
                        ],
                    )

                if group.farthest:
                    spec = transform(points[turn_of[g], : len(targets[g]), 0].reshape(len(targets[g]) * levels, width))
                    for i in range(len(targets[g])):
                        for b in range(group.blocks):
                            spectra[turn_of[g], i, b * levels : (b + 1) * levels, :] = spec[
                                i * levels : (i + 1) * levels, b * LANES : (b + 1) * LANES
                            ]
                else:

                    def part(n, _, g=g, group=group, transform=transform):
                        i, slot = n // group.parts, group.chunk_at(lax.rem(n, group.parts))
                        size = group.chunk * levels
                        spec = transform(points[turn_of[g], i, pl.ds(slot, group.chunk)].reshape(size, width))
                        for b in range(group.blocks):
                            target = pl.multiple_of(b * group.height + slot * levels, 8)
                            spectra[turn_of[g], i, pl.ds(target, size), :] = spec[:, b * LANES : (b + 1) * LANES]
                        return 0

                    lax.fori_loop(0, len(targets[g]) * group.parts, part, 0)
                if group.packed:
                    lax.fori_loop(0, len(targets[g]), lambda i, _, g=g: (pack(g, i), 0)[1], 0)
                for copy in leave(g, max(1, group.full // group.height)):
                    copy.start()
            for g in order[-2:]:
                for copy in leave(g, 1):
                    copy.wait()


def forward(plan, call, scal, winds, theta, thick, top, bottom, tabs):
    arrays = plan.arrays()[call]
    count = FIELDS // 2
    shapes = [(FIELDS // 2, plan.heights()[store], LANES) for store, _ in arrays]
    anywhere = pl.BlockSpec(memory_space=pl.ANY)
    halo = pl.BlockSpec((FIELDS, plan.levels, plan.width), lambda i, s: (0, 0, 0))
    slots = max(group.slots for groups in plan.roles for group in groups)
    total = max(group.height * group.blocks + group.packed_rows for groups in plan.roles for group in groups)
    outs = pl.pallas_call(
        functools.partial(forward_kernel, plan, call),
        grid_spec=pltpu.PrefetchScalarGridSpec(
            num_scalar_prefetch=1,
            grid=(1,),
            in_specs=[anywhere] * 3 + [halo, halo, anywhere, anywhere],
            out_specs=[anywhere] * len(arrays),
            scratch_shapes=[
                pltpu.VMEM((2, count, slots, plan.levels, plan.width), jnp.float32),
                pltpu.VMEM((2, count, total, LANES), jnp.float32),
                pltpu.VMEM((plan.table // LANES, 2, plan.width, LANES), jnp.bfloat16),
                pltpu.SemaphoreType.DMA((2, count)),
                pltpu.SemaphoreType.DMA((2, count, 2)),
                pltpu.SemaphoreType.DMA((plan.table // LANES, 2)),
            ],
        ),
        out_shape=[jax.ShapeDtypeStruct(shape, jnp.float32) for shape in shapes],
        compiler_params=pltpu.CompilerParams(vmem_limit_bytes=VMEM),
        cost_estimate=pl.CostEstimate(flops=FORWARD_COST, bytes_accessed=0, transcendentals=0),
        name="partial_spectra",
    )(scal, winds, theta, thick, top, bottom, *tabs)
    return dict(zip(arrays, outs))


def edge_kernel(plan, count, _, *refs):
    ins, outs = refs[:-2], refs[-2:]
    lane = lax.broadcasted_iota(jnp.int32, (plan.levels, LANES), 1)
    some = plan.rows // count
    for side, column in enumerate((0, (plan.width - 1) % LANES)):
        kept = (jnp.zeros((plan.levels, LANES), jnp.float32),) * FIELDS
        for piece in range(count):
            at = (side * count + piece) * FIELDS
            fields = ins[at : at + FIELDS]

            def pick(row, kept, fields=fields, piece=piece, column=column):
                values = (fields[0][0, row], fields[1][0, row], fields[2][row], fields[3][row])
                return tuple(
                    jnp.where(lane == row + piece * some, value[:, column : column + 1], old)
                    for value, old in zip(values, kept)
                )

            kept = lax.fori_loop(0, some, pick, kept, unroll=max(k for k in range(1, 11) if some % k == 0))
        for field in range(FIELDS):
            outs[side][field] = kept[field]


def edges(plan, after, winds, theta, thick):
    count = 3 if plan.rows % 3 == 0 else 1
    some = plan.rows // count
    specs = []
    for at in (0, (plan.width - 1) // LANES):
        for piece in range(count):
            for wind in range(2):
                specs.append(
                    pl.BlockSpec(
                        (1, some, plan.levels, LANES), lambda i, w=wind, p=piece, at=at: (w, p, 0, at)
                    )
                )
            specs += [pl.BlockSpec((some, plan.levels, LANES), lambda i, p=piece, at=at: (p, 0, at))] * 2
    shape = (FIELDS, plan.levels, LANES)
    return pl.pallas_call(
        functools.partial(edge_kernel, plan, count),
        grid=(1,),
        in_specs=[pl.BlockSpec(memory_space=pl.ANY)] + specs,
        out_specs=[pl.BlockSpec(shape, lambda i: (0, 0, 0))] * 2,
        out_shape=[jax.ShapeDtypeStruct(shape, jnp.float32)] * 2,
        compiler_params=pltpu.CompilerParams(vmem_limit_bytes=VMEM),
        cost_estimate=pl.CostEstimate(flops=EDGE_COST, bytes_accessed=0, transcendentals=0),
        name="edge_columns",
    )(after, *[winds, winds, theta, thick] * (2 * count))


def step_kernel(plan, step_rows, scal, coef, west, east, top, bottom, cuts, i_high, i_low, *refs):
    places, heights = plan.places(), plan.heights()
    halves = plan.levels // 8
    raw, refs = refs[: FIELDS * halves], refs[FIELDS * halves :]
    spectra = refs[: FIELDS * len(heights)]
    new_wind, new_theta, new_thick, held, sums, unpacked, table, ready, sems, t_sems, out_sems = refs[FIELDS * len(heights) :]
    step = pl.program_id(0)
    rows, width, wide, levels = plan.rows, plan.width, plan.wide, plan.levels
    last_step = rows // step_rows

    def inverse(at, groups):
        source = [0, 1, 2, 3] if plan.parts > 1 or at % 2 == 0 else [0, 2, 1, 3]
        slot_at = np.cumsum([0] + [group.slots for group in groups])
        row_at = np.cumsum([0] + [group.total for group in groups])

        def copies(g):
            number, offset = places[at, g]
            return [
                pltpu.make_async_copy(
                    spectra[number * FIELDS + source[u]].at[pl.ds(offset, groups[g].total)],
                    sums.at[u, pl.ds(int(row_at[g]), groups[g].total)],
                    sems.at[g, u],
                )
                for u in range(FIELDS)
            ]

        have = 0
        for g, group in enumerate(groups):
            for copy in copies(g):
                copy.start()
            for copy in fetch_table(scal[1], (i_high, i_high, i_low), table, t_sems, range(have, group.blocks)):
                copy.start()
            have = max(have, group.blocks)
        have = 0
        for g, group in enumerate(groups):
            for copy in copies(g):
                copy.wait()
            for copy in fetch_table(scal[1], (i_high, i_high, i_low), table, t_sems, range(have, group.blocks)):
                copy.wait()
            have = max(have, group.blocks)
            lanes = group.blocks * LANES
            first_slot, first_sum = int(slot_at[g]), int(row_at[g])

            def back_of(spec, size, lanes=lanes, group=group):
                back = three_pass_in(spec, table[: group.blocks].reshape(3 * lanes, wide))
                return back.reshape(size, levels, wide)

            def masked(u, slot, size, group=group, first_slot=first_slot, first_sum=first_sum):
                rows_at = pl.ds(pl.multiple_of((first_slot + slot) * levels, 8), size)
                cut = cuts[rows_at, :]
                lane = lax.broadcasted_iota(jnp.int32, (size, LANES), 1)
                pieces = []
                for b in range(group.blocks):
                    keep = lax.shift_right_logical(lane + (b * LANES + 1), 1) <= cut
                    if group.packed and b == group.blocks - 1:
                        value = unpacked[u, pl.ds(pl.multiple_of(slot * levels, 8), size), :]
                    else:
                        source = pl.multiple_of(first_sum + b * group.height + slot * levels, 8)
                        value = sums[u, pl.ds(source, size), :]
                    pieces.append(jnp.where(keep, value, 0.0))
                return jnp.concatenate(pieces, axis=1)

            def unpack(u, _, group=group, first_sum=first_sum):
                def packed(row, count):
                    at_row = first_sum + group.full + row * levels
                    return sums[u, at_row : at_row + count * levels, :]

                def to(slot, count, value):
                    at_row = pl.multiple_of(slot * levels, 8)
                    unpacked[u, pl.ds(at_row, count * levels), :] = value

                group.unpack(scal[3], packed, to)
                return 0

            if group.packed:
                lax.fori_loop(0, FIELDS, unpack, 0)
            if group.farthest:
                spec = jnp.concatenate([masked(u, 0, levels) for u in range(FIELDS)], axis=0)
                back = back_of(spec, FIELDS)

                @pl.when(scal[4] >= 0)
                def _(back=back):
                    for u in range(FIELDS):
                        held[u ^ scal[0], scal[4]] = back[u]
            else:
                start = group.start(scal[3], rows)

                def part(n, _, group=group, start=start, masked=masked, back_of=back_of):
                    u, slot = n // group.parts, group.chunk_at(lax.rem(n, group.parts))
                    back = back_of(masked(u, slot, group.chunk * levels), group.chunk)
                    held[u ^ scal[0], pl.ds(start + slot, group.chunk)] = back
                    return 0

                lax.fori_loop(0, FIELDS * group.parts, part, 0)

    @pl.when(step == 0)
    def _():
        for at, groups in enumerate(plan.roles):
            pl.when(scal[2] == at)(functools.partial(inverse, at, groups))
        for side, line in enumerate((top, bottom)):

            @pl.when(scal[5 + side] == 0)
            def _(side=side, line=line):
                for field in range(FIELDS):
                    held[field, side * (rows + 1), :, :width] = line[field]

    base = step * step_rows
    tail = width % LANES

    @pl.when(step < last_step)
    def _():
        lane = lax.broadcasted_iota(jnp.int32, (levels, LANES), 1)

        def load(n, _):
            at = n
            row = base + n
            is_raw = (row >= scal[7]) & (row < scal[8])
            for field in range(FIELDS):
                for half in range(halves):
                    piece = raw[field * halves + half]
                    some = slice(half * 8, half * 8 + 8)
                    value = piece[0, at] if field < 2 else piece[at]
                    held[field, row + 1, some, :width] = jnp.where(
                        is_raw, value, held[field, row + 1, some, :width]
                    )
                beyond = jnp.where(
                    lane == tail,
                    pltpu.roll(east[field], (tail + LANES - row) & (LANES - 1), 1),
                    pltpu.roll(west[field], (2 * LANES - 1 - row) & (LANES - 1), 1),
                )
                held[field, row + 1, :, width:] = jnp.where(
                    is_raw, beyond[:, tail:], held[field, row + 1, :, width:]
                )
            return 0

        @pl.when((base < scal[8]) & (base + step_rows > scal[7]))
        def _():
            lax.fori_loop(0, step_rows, load, 0, unroll=3 if step_rows % 3 == 0 else 1)

    slot = step % 2
    count = wide // LANES
    lane = lax.broadcasted_iota(jnp.int32, (8, LANES), 1)
    is_first, is_last = lane == 0, lane == LANES - 1

    def stencil(row, _):
        at = base - step_rows + row
        along, across, push, turn, cos_north, cos_south = [coef[k * rows + at] for k in range(6)]
        across_north, across_south = across * cos_north, across * cos_south
        for part in range(levels // 8):
            some = pl.ds(part * 8, 8)

            def load(field, shift, k):
                return held[field, at + shift, some, k * LANES : (k + 1) * LANES]

            here = [
                functools.lru_cache(maxsize=None)(lambda k, field=field: load(field, 1, k))
                for field in range(FIELDS)
            ]
            up = [functools.lru_cache(maxsize=None)(lambda k, f=f: pltpu.roll(f(k), LANES - 1, 1)) for f in here]
            down = [functools.lru_cache(maxsize=None)(lambda k, f=f: pltpu.roll(f(k), 1, 1)) for f in here]

            def shifted(which, k):
                return (
                    jnp.where(is_last, up[which]((k + 1) % count), up[which](k)),
                    jnp.where(is_first, down[which]((k - 1) % count), down[which](k)),
                )

            for k in range(count):
                stop = min(width, (k + 1) * LANES)

                def put(field, piece, k=k, stop=stop):
                    ready[slot, field, row, some, k * LANES : stop] = piece[:, : stop - k * LANES]

                u, v, t, h = [here[field](k) for field in range(FIELDS)]
                advect, carry = along * u, 0.1 * v
                (u_e, u_w), (v_e, v_w), (t_e, t_w), (h_e, h_w) = [shifted(field, k) for field in range(FIELDS)]
                v_n, v_s, h_n, h_s = load(1, 0, k), load(1, 2, k), load(3, 0, k), load(3, 2, k)
                put(
                    3,
                    h
                    - along * (u_e * h_e - u_w * h_w)
                    - (across_south * (v_s * h_s) - across_north * (v_n * h_n)),
                )
                put(
                    1,
                    v
                    - advect * (v_e - v_w)
                    - carry * (v_s - v_n)
                    - 0.15 * (h_s - h_n)
                    - turn * u,
                )
                put(
                    0,
                    u
                    - advect * (u_e - u_w)
                    - carry * (load(0, 2, k) - load(0, 0, k))
                    - push * (h_e - h_w)
                    + turn * v,
                )
                put(2, t - advect * (t_e - t_w) - carry * (load(2, 2, k) - load(2, 0, k)))
        return 0

    outs = (new_wind.at[0], new_wind.at[1], new_theta, new_thick)

    def leave(at_step, size, act):
        for field, out in enumerate(outs):
            for k in range(0, step_rows, size):
                act(
                    pltpu.make_async_copy(
                        ready.at[at_step % 2, field, pl.ds(k, size)],
                        out.at[pl.ds((at_step - 1) * step_rows + k, size)],
                        out_sems.at[at_step % 2, field],
                    )
                )

    @pl.when(step > 2)
    def _():
        leave(step - 2, step_rows, lambda copy: copy.wait())

    @pl.when(step > 0)
    def _():
        lax.fori_loop(0, step_rows, stencil, 0, unroll=5 if step_rows % 5 == 0 else 1)
        leave(step, PIECE if step_rows % PIECE == 0 else step_rows, lambda copy: copy.start())

    @pl.when(step == last_step)
    def _():
        if last_step > 1:
            leave(step - 1, step_rows, lambda copy: copy.wait())
        leave(step, step_rows, lambda copy: copy.wait())


def substep(plan, step_rows, scal, coef, winds, theta, thick, west, east, top, bottom, cuts, tabs, spectra):
    rows, width, levels = plan.rows, plan.width, plan.levels
    once = pl.Buffered(1)
    steps = rows // step_rows

    def block(i, s):
        return jnp.clip(i, s[9], s[10])

    def whole(shape):
        return pl.BlockSpec(shape, lambda i, s: (0,) * len(shape), pipeline_mode=once)

    anywhere = pl.BlockSpec(memory_space=pl.ANY)
    halves = range(levels // 8)
    raw_specs = [
        pl.BlockSpec((1, step_rows, 8, width), lambda i, s, w=wind, h=half: (w, block(i, s), h, 0))
        for wind in range(2)
        for half in halves
    ] + [
        pl.BlockSpec((step_rows, 8, width), lambda i, s, h=half: (block(i, s), h, 0))
        for _ in range(2)
        for half in halves
    ]
    raw = [array for array in (winds, winds, theta, thick) for _ in halves]
    edge, halo = (FIELDS, levels, LANES), (FIELDS, levels, width)
    in_specs = [
        pl.BlockSpec(memory_space=pltpu.SMEM),
        whole(edge),
        whole(edge),
        whole(halo),
        whole(halo),
        whole((plan.slots * levels, LANES)),
        anywhere,
        anywhere,
    ] + raw_specs + [anywhere] * len(spectra)
    shapes = [(2, rows, levels, width)] + [(rows, levels, width)] * 2
    most = max(sum(group.total for group in groups) for groups in plan.roles)
    return pl.pallas_call(
        functools.partial(step_kernel, plan, step_rows),
        grid_spec=pltpu.PrefetchScalarGridSpec(
            num_scalar_prefetch=1,
            grid=(steps + 1,),
            in_specs=in_specs,
            out_specs=[anywhere] * 3,
            scratch_shapes=[
                pltpu.VMEM((FIELDS, rows + 2, levels, plan.wide), jnp.float32),
                pltpu.VMEM((FIELDS, most, LANES), jnp.float32),
                pltpu.VMEM((FIELDS, max(group.height for groups in plan.roles for group in groups), LANES), jnp.float32),
                pltpu.VMEM((plan.table // LANES, 3, LANES, plan.wide), jnp.bfloat16),
                pltpu.VMEM((2, FIELDS, step_rows, levels, width), jnp.float32),
                pltpu.SemaphoreType.DMA((max(len(groups) for groups in plan.roles), FIELDS)),
                pltpu.SemaphoreType.DMA((plan.table // LANES, 3)),
                pltpu.SemaphoreType.DMA((2, FIELDS)),
            ],
        ),
        out_shape=[jax.ShapeDtypeStruct(shape, jnp.float32) for shape in shapes],
        compiler_params=pltpu.CompilerParams(vmem_limit_bytes=VMEM),
        cost_estimate=pl.CostEstimate(
            flops=6 * most * FIELDS * LANES * plan.wide, bytes_accessed=40_000_000, transcendentals=0
        ),
        name="inverse_and_substep",
    )(scal, coef, west, east, top, bottom, cuts, *tabs, *raw, *spectra)


def lon_swap(plan, value, moves):
    pairs = [
        (block * plan.lon + place, block * plan.lon + (place ^ (1 << bit)))
        for blocks, bit in moves
        for block in blocks
        for place in range(plan.lon)
    ]
    return lax.ppermute(value, ("lat", "lon"), pairs)


def lat_move(plan, value, sources, targets):
    pairs = [
        (source * plan.lon + place, target * plan.lon + place)
        for source, target in zip(sources, targets)
        for place in range(plan.lon)
    ]
    return lax.ppermute(value, ("lat", "lon"), pairs)


def gather_sums(plan, blocks, slots, order):
    slots = dict(slots)
    for bit in order:
        sent = [s for s in slots if s >> bit & 1]
        for s in sorted(sent, key=lambda s: -bin(s).count("1")):
            moved = lon_swap(plan, slots.pop(s), [(blocks, bit)])
            slots[s ^ (1 << bit)] = slots[s ^ (1 << bit)] + moved
    for bit in reversed(order):
        for s in sorted(slots):
            slots[s | (1 << bit)] = lon_swap(plan, slots[s], [(blocks, bit)])
    return slots


def field_sets(plan):
    sent, kept = [], []
    for at in range(len(plan.roles)):
        bit = at % 2
        sent.append([u for u in range(FIELDS) if u >> bit & 1])
        kept.append([u for u in range(FIELDS) if not u >> bit & 1])
    return sent, kept


def store_sums(plan, members, sent, kept, before=None):
    near = [(blocks, bit) for blocks, bit in members]
    far = [(blocks, 1 - bit) for blocks, bit in members]
    moved = lon_swap(plan, sent, near)
    own = (kept[0] + moved[0]) + lon_swap(plan, kept[1] + moved[1], far)
    across = lon_swap(plan, own, far)
    beside = lon_swap(plan, own, near)
    onward = across if before is None else lax.optimization_barrier((across, before))[0]
    return own, beside, across, lon_swap(plan, onward, near)


def split_sums(plan, place, at, sent, kept):
    first, second = field_sets(plan)
    parts, own = plan.parts, place % plan.parts
    bits = plan.lon.bit_length() - 1
    slots = {}
    for us, array in ((first[at], sent), (second[at], kept)):
        for i, u in enumerate(us):
            pieces = array[i].reshape(parts, -1, LANES)
            for k in range(parts):
                slots[u * parts + k] = pieces[k ^ own]
    order = list(range(bits)) if at % 2 == 0 else list(reversed(range(bits)))
    slots = gather_sums(plan, plan.blocks(at), slots, order)
    result = []
    for u in range(FIELDS):
        pieces = jnp.stack([slots[u * parts + k] for k in range(parts)])
        result.append(pieces[jnp.arange(parts) ^ own].reshape(-1, LANES))
    return result


def all_sums(plan, place, arrays):
    stores = plan.stores()
    if plan.parts > 1:
        return sum(
            [
                split_sums(plan, place, store[0][0], arrays[number, 0], arrays[number, 1])
                for number, store in enumerate(stores)
            ],
            [],
        )
    back, results = None, {}
    for number in reversed(range(len(stores))):
        store, first, second = stores[number], arrays[number, 0], arrays[number, 1]
        if store[0][1] == 0:
            members = [(plan.blocks(at), at % 2) for at, _ in store]
            results[number] = store_sums(plan, members, first, second, back)
        else:
            at = store[0][0]
            home, helpers = plan.blocks(at), plan.blocks(at + len(plan.roles))
            first, second = [lat_move(plan, array, home, helpers) for array in (first, second)]
            sums = store_sums(plan, [(helpers, at % 2)], first, second)
            results[number] = [lat_move(plan, array, helpers, home) for array in sums]
            back = results[number][0]
    return [array for number in range(len(stores)) for array in results[number]]


def body(winds, theta, thick, polar_rows, cutoffs):
    lat, lon = lax.axis_size("lat"), lax.axis_size("lon")
    levels, rows, width = theta.shape
    sizes = (lat, lon, levels, rows, width, polar_rows.shape[0])
    plan = Plan(*sizes)
    t_tabs, i_tabs = [tuple(jnp.asarray(part) for part in pair) for pair in tables(sizes)]
    block, place = lax.axis_index("lat"), lax.axis_index("lon")
    winds = winds.transpose(0, 2, 1, 3)
    theta = theta.transpose(1, 0, 2)
    thick = thick.transpose(1, 0, 2)
    hemi = (block >= lat // 2).astype(jnp.int32)
    role = jnp.where(hemi == 1, lat - 1 - block, block)

    def line(row):
        return jnp.stack([winds[0, row], winds[1, row], theta[row], thick[row]])

    south_pairs = [(b * lon + p, (b + 1) * lon + p) for b in range(lat - 1) for p in range(lon)]
    north_pairs = [(to, at) for at, to in south_pairs]
    top = lax.ppermute(line(rows - 1), ("lat", "lon"), south_pairs)
    bottom = lax.ppermute(line(0), ("lat", "lon"), north_pairs)

    step_rows = max(k for k in range(1, 16) if rows % k == 0)
    listed = polar_rows.shape[0]
    north_run = jnp.sum((polar_rows < plan.total_rows // 2).astype(jnp.int32))
    south_first = plan.total_rows - listed + north_run
    far_row = jnp.where(hemi == 1, south_first, north_run - 1)
    far_at = far_row - block * rows + 1
    far_at = jnp.where((far_at >= 0) & (far_at <= rows + 1), far_at, -1)
    raw_from = jnp.clip(north_run - block * rows, 0, rows)
    raw_to = jnp.clip(south_first - block * rows, 0, rows)
    block_from = jnp.minimum(raw_from, rows - 1) // step_rows
    block_to = jnp.maximum(block_from, jnp.maximum(raw_to - 1, 0) // step_rows)
    above, below = block * rows - 1, (block + 1) * rows

    def is_listed(row):
        return (row >= 0) & (row < plan.total_rows) & ((row < north_run) | (row >= south_first))

    facts = [
        place // plan.parts, place, role, hemi, far_at, is_listed(above), is_listed(below),
        raw_from, raw_to, block_from, block_to,
    ]
    scal = jnp.stack([jnp.asarray(fact).astype(jnp.int32) for fact in facts])

    arrays = forward(plan, 0, scal, winds, theta, thick, top, bottom, t_tabs)

    first_edge, last_edge = edges(plan, arrays[plan.arrays()[0][0]], winds, theta, thick)
    some = [b for b in range(lat) if (min(b, lat - 1 - b) + 1) * rows > plan.low]
    east_pairs = [(b * lon + i, b * lon + (i + 1) % lon) for b in some for i in range(lon)]
    west = lax.ppermute(last_edge, ("lat", "lon"), east_pairs)
    east = lax.ppermute(first_edge, ("lat", "lon"), [(to, at) for at, to in east_pairs])

    scal, _ = lax.optimization_barrier((scal, first_edge))
    later = forward(plan, 1, scal, winds, theta, thick, top, bottom, t_tabs)
    added = {key: array for key, array in later.items() if plan.stores()[key[0]][0][1] == 0}
    added, west, east = lax.optimization_barrier((added, west, east))
    arrays = {**arrays, **later, **added}
    sums = all_sums(plan, place, arrays)

    slot_rows = jnp.asarray(plan.slot_rows())[jnp.minimum(role, len(plan.roles) - 1), hemi]
    slot_rows = jnp.where(slot_rows == -2, far_at, slot_rows)
    hits = (polar_rows[None, :] == (slot_rows - 1 + block * rows)[:, None]) & (slot_rows >= 0)[:, None]
    cut = jnp.sum(jnp.where(hits, cutoffs[None, :] + 1, 0), axis=1) - 1
    cuts = jnp.broadcast_to(cut.astype(jnp.int32)[:, None, None], (plan.slots, levels, LANES))
    cuts = cuts.reshape(plan.slots * levels, LANES)

    ring = block * rows - 1 + jnp.arange(rows + 2, dtype=jnp.int32)
    centre = (ring.astype(jnp.float32) + 0.5) * (jnp.pi / plan.total_rows)
    cos, sin = jnp.sin(centre), -jnp.cos(centre)
    mid = cos[1:-1]
    coef = jnp.concatenate([0.025 / mid, 0.1 / mid, 0.05 / mid, 0.3 * sin[1:-1], cos[:-2], cos[2:]])

    out = substep(
        plan, step_rows, scal, coef, winds, theta, thick, west, east, top, bottom, cuts, i_tabs, sums
    )
    return (out[0].transpose(0, 2, 1, 3), out[1].transpose(1, 0, 2), out[2].transpose(1, 0, 2))


def solution(mesh):
    in_specs = (P(None, None, "lat", "lon"), P(None, "lat", "lon"), P(None, "lat", "lon"), P(), P())
    out_specs = (P(None, None, "lat", "lon"), P(None, "lat", "lon"), P(None, "lat", "lon"))
    return jax.shard_map(body, mesh=mesh, in_specs=in_specs, out_specs=out_specs, check_vma=False)
```

```python
import functools

import jax
import jax.numpy as jnp
import ml_dtypes
import numpy as np
from jax import lax
from jax.experimental import pallas as pl
from jax.experimental.pallas import tpu as pltpu
from jax.sharding import PartitionSpec as P

FIELDS = 4
LANES = 128
PIECE = 3
VMEM = 60 * 1024 * 1024
FORWARD_COST, EDGE_COST = 5_000_000_000, 5_000_000_000


def round_up(value, step):
    return -(-value // step) * step


class Group:
    def __init__(self, first, stop, near, far, blocks, levels, quarters):
        self.first, self.stop, self.blocks, self.levels = first, stop, blocks, levels
        self.near, self.far = int(near), int(far)
        self.own = stop - first
        self.farthest = self.own == 0
        self.slots = 1 if self.farthest else self.own + self.near + self.far
        self.height = self.slots * levels
        self.quarters = list(quarters)
        assert sum(self.quarters) == self.slots
        one, two, three, four = self.quarters
        self.beside = max(one, three) if one and three else 0
        self.half = -(-two // 2)
        self.packed = self.beside > 0 or two > 1
        self.pieces = []
        if self.packed:
            if not self.beside:
                for start, count in ((0, one), (one + two, three)):
                    if count:
                        self.pieces.append((0, start, count))
            if four:
                self.pieces.append((0, one + two + three, four))
        self.whole_rows = sum(piece[2] for piece in self.pieces)
        self.full = self.height * (blocks - 1 if self.packed else blocks)
        self.packed_rows = (self.whole_rows + self.beside + self.half) * levels if self.packed else 0
        self.total = self.full + self.packed_rows
        parts = max(1, round(self.slots / 16))
        self.chunk = -(-self.slots // parts)
        self.parts = -(-self.slots // self.chunk)

    def start(self, hemi, rows):
        return jnp.where(hemi == 1, rows - self.stop + 1 - self.far, self.first + 1 - self.near)

    def chunk_at(self, part):
        return jnp.minimum(part * self.chunk, self.slots - self.chunk)

    def slot(self, hemi, first, count):
        first = min(first, self.slots - count)
        return jnp.where(hemi == 1, self.slots - count - first, first)

    def pairs(self):
        one, two, three, _ = self.quarters
        result = []
        if self.beside:
            result.append((one + two, 0, self.beside, 96))
        if two:
            result.append((one, one + two - self.half, self.half, 64))
        return result

    def pack(self, hemi, last, to):
        row = 0
        for _, first, count in self.pieces:
            to(row, count, last(self.slot(hemi, first, count), count))
            row += count
        for left, right, count, lanes in self.pairs():
            lane = lax.broadcasted_iota(jnp.int32, (count * self.levels, LANES), 1)
            beside = pltpu.roll(last(self.slot(hemi, right, count), count), lanes, 1)
            to(row, count, jnp.where(lane < lanes, last(self.slot(hemi, left, count), count), beside))
            row += count

    def unpack(self, hemi, packed, to):
        row = self.whole_rows
        for left, right, count, lanes in self.pairs():
            value = packed(row, count)
            to(self.slot(hemi, left, count), count, value)
            to(self.slot(hemi, right, count), count, pltpu.roll(value, LANES - lanes, 1))
            row += count
        row = 0
        for _, first, count in self.pieces:
            to(self.slot(hemi, first, count), count, packed(row, count))
            row += count


class Plan:
    def __init__(self, lat, lon, levels, rows, width, listed):
        self.lat, self.lon, self.levels, self.rows, self.width = lat, lon, levels, rows, width
        self.total_rows, self.length = lat * rows, lon * width
        self.parts = lon // FIELDS
        self.wide = round_up(width + 2, LANES)
        pole = listed // 2
        self.low, self.high = pole - pole // 4, pole + pole // 4
        top = self.length // 4 - 1

        def blocks_of(depth):
            return -(-(2 * min(2 * (depth + 1), top) + 1) // LANES)

        self.roles = []
        last = self.high - 2
        for role in range(lat // 2):
            start = role * rows
            if start > last:
                break
            need = {}
            for depth in range(start, min(start + rows - 1, last) + 1):
                need.setdefault(blocks_of(depth), []).append(depth - start)
            spans = [[need[k][0], need[k][-1] + 1, False, False, k] for k in sorted(need)]
            if role > 0:
                spans[0][2], spans[0][4] = True, max(spans[0][4], blocks_of(start - 1))
            if start + rows <= last:
                spans[-1][3], spans[-1][4] = True, max(spans[-1][4], blocks_of(start + rows))
            groups = []
            for first, stop, near, far, blocks in spans:
                depths = range(start + first - int(near), start + stop + int(far))
                quarters = [0] * 4
                for depth in depths:
                    lanes = 2 * min(2 * (depth + 1), top) + 1 - (blocks - 1) * LANES
                    quarters[max(0, -(-lanes // (LANES // 4)) - 1)] += 1
                groups.append(Group(first, stop, near, far, blocks, levels, quarters))
            groups.append(Group(0, 0, False, False, -(-(2 * top + 1) // LANES), levels, (0, 0, 0, 1)))
            self.roles.append(groups)
        self.slots = max(sum(group.slots for group in groups) for groups in self.roles)
        self.table = LANES * max(group.blocks for groups in self.roles for group in groups)
        count = len(self.roles)
        self.lent = {}
        if self.parts == 1 and 2 * count <= lat // 2:
            self.lent = {count - 1: len(self.roles[-1]) - 2}

    def blocks(self, role):
        return (role, self.lat - 1 - role)

    def parcels(self, at):
        indices = range(len(self.roles[at]))
        away = self.lent.get(at)
        home = [g for g in indices if g != away]
        return [home] if away is None else [home, [away]]

    def stores(self):
        result = []
        for at in range(len(self.roles)):
            size = self.height_of(at, 0)
            for store in result:
                sizes = [self.height_of(*member) for member in store]
                if self.parts == 1 and max(sizes + [size]) <= 1.1 * min(sizes + [size]):
                    store.append((at, 0))
                    break
            else:
                result.append([(at, 0)])
        return result + [[(at, 1)] for at in self.lent]

    def arrays(self):
        return [[(store, which) for store in range(len(self.stores()))] for which in range(2)]

    def places(self):
        result = {}
        for number, store in enumerate(self.stores()):
            for at, parcel in store:
                offset = 0
                for g in self.parcels(at)[parcel]:
                    result[at, g] = (number, offset)
                    offset += self.roles[at][g].total
        return result

    def height_of(self, at, parcel):
        return sum(self.roles[at][g].total for g in self.parcels(at)[parcel])

    def heights(self):
        return [max(self.height_of(*member) for member in store) for store in self.stores()]

    def slot_rows(self):
        table = np.full((len(self.roles), 2, self.slots), -1, np.int32)
        for at, groups in enumerate(self.roles):
            for hemi in range(2):
                rows = []
                for group in groups:
                    first = group.first + 1 - group.near if hemi == 0 else self.rows - group.stop + 1 - group.far
                    rows += [-2] if group.farthest else [first + k for k in range(group.slots)]
                table[at, hemi, : len(rows)] = rows
        return table


def split_table(table):
    high = table.astype(ml_dtypes.bfloat16)
    low = (table - high.astype(np.float64)).astype(ml_dtypes.bfloat16)
    return high, low


@functools.lru_cache(maxsize=None)
def tables(sizes):
    plan = Plan(*sizes)
    index = np.arange(plan.table)
    wave, odd = (index + 1) // 2, (index % 2 == 0) & (index > 0)
    used = wave < plan.length // 4
    points = np.zeros(plan.wide, np.int64)
    points[: plan.width + 1] = np.arange(plan.width + 1)
    points[-1] = -1
    shown = np.zeros(plan.wide, bool)
    shown[: plan.width + 1] = True
    shown[-1] = True

    def trig(at):
        angle = (wave[:, None] * at[None, :]) % plan.length * (2.0 * np.pi / plan.length)
        return np.where(odd[:, None], np.sin(angle), np.cos(angle)) * used[:, None]

    weight = np.where(wave == 0, 1.0, 2.0) / plan.length
    forward, inverse = [], []
    for place in range(plan.lon):
        forward.append(trig(place * plan.width + np.arange(plan.width)).T)
        inverse.append(trig(place * plan.width + points) * weight[:, None] * shown[None, :])
    shape = (plan.lon, plan.width, plan.table // LANES, LANES)
    forward = np.stack(forward).reshape(shape).transpose(0, 2, 1, 3)
    inverse = np.stack(inverse).reshape(plan.lon, plan.table // LANES, LANES, plan.wide)
    return split_table(forward), split_table(inverse)


def fetch_table(place, tabs, held, sems, blocks):
    return [
        pltpu.make_async_copy(tab.at[place, b], held.at[b, k], sems.at[b, k])
        for b in blocks
        for k, tab in enumerate(tabs)
    ]


def split(value):
    high = value.astype(jnp.bfloat16)
    low = (value - high.astype(jnp.float32)).astype(jnp.bfloat16)
    return high, low


def dot(left, right):
    return jnp.dot(left, right, preferred_element_type=jnp.float32)


def three_pass_out(left, right):
    columns = right[0].shape[1]
    both = dot(left[0], jnp.concatenate(right, axis=1))
    return both[:, :columns] + (both[:, columns:] + dot(left[1], right[0]))


def three_pass_in(value, table):
    terms = []
    for at in range(0, value.shape[1], LANES):
        high, low = split(value[:, at : at + LANES])
        terms += [high, low, high]
    return dot(jnp.concatenate(terms, axis=1), table)


def forward_kernel(plan, call, scal, winds, theta, thick, top, bottom, t_high, t_low, *refs):
    places, sets, arrays = plan.places(), field_sets(plan), plan.arrays()[call]
    outs, (points, spectra, held, in_sems, out_sems, t_sems) = refs[: len(arrays)], refs[len(arrays) :]
    levels, width = plan.levels, plan.width
    hemi = scal[3]
    for at, groups in enumerate(plan.roles):

        @pl.when(scal[2] == at)
        def _(at=at, groups=groups):
            targets = {}
            for g in range(len(groups)):
                number, which = next(
                    (n, array[1]) for n, array in enumerate(arrays) if array[0] == places[at, g][0]
                )
                targets[g] = [(number, i, u) for i, u in enumerate(sets[which][at])]
            order = list(range(len(groups)))
            some_fields = {g: [u ^ scal[0] for _, _, u in targets[g]] for g in order}
            turn_of = {g: n % 2 for n, g in enumerate(order)}
            ready = 0

            def first_row(group):
                if group.farthest:
                    return jnp.clip(scal[4] - 1, 0, plan.rows - 1), 0, 1
                first = jnp.where(hemi == 1, plan.rows - group.stop, group.first)
                return first, jnp.where(hemi == 1, group.far, group.near), group.own

            def fetch(g):
                first, slot, count = first_row(groups[g])
                for i, field in enumerate(some_fields[g]):

                    def pieces(source, i=i):
                        for k in range(0, count, PIECE):
                            size = min(PIECE, count - k)
                            pltpu.make_async_copy(
                                source.at[pl.ds(first + k, size)],
                                points.at[turn_of[g], i, pl.ds(slot + k, size)],
                                in_sems.at[turn_of[g], i],
                            ).start()

                    pl.when(field < 2)(lambda: pieces(winds.at[jnp.minimum(field, 1)]))
                    pl.when(field == 2)(lambda: pieces(theta))
                    pl.when(field == 3)(lambda: pieces(thick))

            def arrive(g):
                first, slot, count = first_row(groups[g])
                for i in range(len(targets[g])):
                    pltpu.make_async_copy(
                        theta.at[pl.ds(first, count)],
                        points.at[turn_of[g], i, pl.ds(slot, count)],
                        in_sems.at[turn_of[g], i],
                    ).wait()

            def leave(g, parts):
                group, turn, copies = groups[g], turn_of[g], []
                _, offset = places[at, g]
                size = group.full // parts
                for i, (number, place, _) in enumerate(targets[g]):
                    for k in range(parts if group.full else 0):
                        copies.append(
                            pltpu.make_async_copy(
                                spectra.at[turn, i, pl.ds(k * size, size)],
                                outs[number].at[place, pl.ds(offset + k * size, size)],
                                out_sems.at[turn, i, 0],
                            )
                        )
                    if group.packed:
                        copies.append(
                            pltpu.make_async_copy(
                                spectra.at[turn, i, pl.ds(group.blocks * group.height, group.packed_rows)],
                                outs[number].at[place, pl.ds(offset + group.full, group.packed_rows)],
                                out_sems.at[turn, i, 1],
                            )
                        )
                return copies

            def pack(g, i):
                group, turn = groups[g], turn_of[g]

                def last(slot, count):
                    at_row = pl.multiple_of((group.blocks - 1) * group.height + slot * levels, 8)
                    return spectra[turn, i, pl.ds(at_row, count * levels), :]

                def to(row, count, value):
                    at_row = group.blocks * group.height + row * levels
                    spectra[turn, i, at_row : at_row + count * levels, :] = value

                group.pack(hemi, last, to)

            def halo(g, slot, line, wanted):
                @pl.when(wanted)
                def _():
                    for i, field in enumerate(some_fields[g]):
                        points[turn_of[g], i, slot] = line[field]

            fetch(order[0])
            needed = range(max(groups[g].blocks for g in order))
            for copy in fetch_table(scal[1], (t_high, t_low), held, t_sems, needed):
                copy.start()
            for n, g in enumerate(order):
                group = groups[g]
                if n + 1 < len(order):
                    fetch(order[n + 1])
                arrive(g)
                for copy in fetch_table(scal[1], (t_high, t_low), held, t_sems, range(ready, group.blocks)):
                    copy.wait()
                ready = max(ready, group.blocks)
                if group.farthest:
                    halo(g, 0, top, scal[4] == 0)
                    halo(g, 0, bottom, scal[4] == plan.rows + 1)
                if group.near:
                    halo(g, 0, top, hemi == 0)
                    halo(g, group.slots - 1, bottom, hemi == 1)
                if group.far:
                    halo(g, group.slots - 1, bottom, hemi == 0)
                    halo(g, 0, top, hemi == 1)
                if n >= 2:
                    for copy in leave(order[n - 2], 1):
                        copy.wait()

                def transform(value, group=group):
                    return three_pass_out(
                        split(value),
                        [
                            jnp.concatenate([held[b, half] for b in range(group.blocks)], axis=1)
                            for half in range(2)
                        ],
                    )

                if group.farthest:
                    spec = transform(points[turn_of[g], : len(targets[g]), 0].reshape(len(targets[g]) * levels, width))
                    for i in range(len(targets[g])):
                        for b in range(group.blocks):
                            spectra[turn_of[g], i, b * levels : (b + 1) * levels, :] = spec[
                                i * levels : (i + 1) * levels, b * LANES : (b + 1) * LANES
                            ]
                else:

                    def part(n, _, g=g, group=group, transform=transform):
                        i, slot = n // group.parts, group.chunk_at(lax.rem(n, group.parts))
                        size = group.chunk * levels
                        spec = transform(points[turn_of[g], i, pl.ds(slot, group.chunk)].reshape(size, width))
                        for b in range(group.blocks):
                            target = pl.multiple_of(b * group.height + slot * levels, 8)
                            spectra[turn_of[g], i, pl.ds(target, size), :] = spec[:, b * LANES : (b + 1) * LANES]
                        return 0

                    lax.fori_loop(0, len(targets[g]) * group.parts, part, 0)
                if group.packed:
                    lax.fori_loop(0, len(targets[g]), lambda i, _, g=g: (pack(g, i), 0)[1], 0)
                for copy in leave(g, max(1, group.full // group.height)):
                    copy.start()
            for g in order[-2:]:
                for copy in leave(g, 1):
                    copy.wait()


def forward(plan, call, scal, winds, theta, thick, top, bottom, tabs):
    arrays = plan.arrays()[call]
    count = FIELDS // 2
    shapes = [(FIELDS // 2, plan.heights()[store], LANES) for store, _ in arrays]
    anywhere = pl.BlockSpec(memory_space=pl.ANY)
    halo = pl.BlockSpec((FIELDS, plan.levels, plan.width), lambda i, s: (0, 0, 0))
    slots = max(group.slots for groups in plan.roles for group in groups)
    total = max(group.height * group.blocks + group.packed_rows for groups in plan.roles for group in groups)
    outs = pl.pallas_call(
        functools.partial(forward_kernel, plan, call),
        grid_spec=pltpu.PrefetchScalarGridSpec(
            num_scalar_prefetch=1,
            grid=(1,),
            in_specs=[anywhere] * 3 + [halo, halo, anywhere, anywhere],
            out_specs=[anywhere] * len(arrays),
            scratch_shapes=[
                pltpu.VMEM((2, count, slots, plan.levels, plan.width), jnp.float32),
                pltpu.VMEM((2, count, total, LANES), jnp.float32),
                pltpu.VMEM((plan.table // LANES, 2, plan.width, LANES), jnp.bfloat16),
                pltpu.SemaphoreType.DMA((2, count)),
                pltpu.SemaphoreType.DMA((2, count, 2)),
                pltpu.SemaphoreType.DMA((plan.table // LANES, 2)),
            ],
        ),
        out_shape=[jax.ShapeDtypeStruct(shape, jnp.float32) for shape in shapes],
        compiler_params=pltpu.CompilerParams(vmem_limit_bytes=VMEM),
        cost_estimate=pl.CostEstimate(flops=FORWARD_COST, bytes_accessed=0, transcendentals=0),
        name="partial_spectra",
    )(scal, winds, theta, thick, top, bottom, *tabs)
    return dict(zip(arrays, outs))


def edge_kernel(plan, count, _, *refs):
    ins, outs = refs[:-2], refs[-2:]
    lane = lax.broadcasted_iota(jnp.int32, (plan.levels, LANES), 1)
    some = plan.rows // count
    for side, column in enumerate((0, (plan.width - 1) % LANES)):
        kept = (jnp.zeros((plan.levels, LANES), jnp.float32),) * FIELDS
        for piece in range(count):
            at = (side * count + piece) * FIELDS
            fields = ins[at : at + FIELDS]

            def pick(row, kept, fields=fields, piece=piece, column=column):
                values = (fields[0][0, row], fields[1][0, row], fields[2][row], fields[3][row])
                return tuple(
                    jnp.where(lane == row + piece * some, value[:, column : column + 1], old)
                    for value, old in zip(values, kept)
                )

            kept = lax.fori_loop(0, some, pick, kept, unroll=max(k for k in range(1, 11) if some % k == 0))
        for field in range(FIELDS):
            outs[side][field] = kept[field]


def edges(plan, after, winds, theta, thick):
    count = 3 if plan.rows % 3 == 0 else 1
    some = plan.rows // count
    specs = []
    for at in (0, (plan.width - 1) // LANES):
        for piece in range(count):
            for wind in range(2):
                specs.append(
                    pl.BlockSpec(
                        (1, some, plan.levels, LANES), lambda i, w=wind, p=piece, at=at: (w, p, 0, at)
                    )
                )
            specs += [pl.BlockSpec((some, plan.levels, LANES), lambda i, p=piece, at=at: (p, 0, at))] * 2
    shape = (FIELDS, plan.levels, LANES)
    return pl.pallas_call(
        functools.partial(edge_kernel, plan, count),
        grid=(1,),
        in_specs=[pl.BlockSpec(memory_space=pl.ANY)] + specs,
        out_specs=[pl.BlockSpec(shape, lambda i: (0, 0, 0))] * 2,
        out_shape=[jax.ShapeDtypeStruct(shape, jnp.float32)] * 2,
        compiler_params=pltpu.CompilerParams(vmem_limit_bytes=VMEM),
        cost_estimate=pl.CostEstimate(flops=EDGE_COST, bytes_accessed=0, transcendentals=0),
        name="edge_columns",
    )(after, *[winds, winds, theta, thick] * (2 * count))


def step_kernel(plan, step_rows, scal, coef, west, east, top, bottom, cuts, i_high, i_low, *refs):
    places, heights = plan.places(), plan.heights()
    halves = plan.levels // 8
    raw, refs = refs[: FIELDS * halves], refs[FIELDS * halves :]
    spectra = refs[: FIELDS * len(heights)]
    new_wind, new_theta, new_thick, held, sums, unpacked, table, ready, sems, t_sems, out_sems = refs[FIELDS * len(heights) :]
    step = pl.program_id(0)
    rows, width, wide, levels = plan.rows, plan.width, plan.wide, plan.levels
    last_step = rows // step_rows

    def inverse(at, groups):
        source = [0, 1, 2, 3] if plan.parts > 1 or at % 2 == 0 else [0, 2, 1, 3]
        slot_at = np.cumsum([0] + [group.slots for group in groups])
        row_at = np.cumsum([0] + [group.total for group in groups])

        def copies(g):
            number, offset = places[at, g]
            return [
                pltpu.make_async_copy(
                    spectra[number * FIELDS + source[u]].at[pl.ds(offset, groups[g].total)],
                    sums.at[u, pl.ds(int(row_at[g]), groups[g].total)],
                    sems.at[g, u],
                )
                for u in range(FIELDS)
            ]

        have = 0
        for g, group in enumerate(groups):
            for copy in copies(g):
                copy.start()
            for copy in fetch_table(scal[1], (i_high, i_high, i_low), table, t_sems, range(have, group.blocks)):
                copy.start()
            have = max(have, group.blocks)
        have = 0
        for g, group in enumerate(groups):
            for copy in copies(g):
                copy.wait()
            for copy in fetch_table(scal[1], (i_high, i_high, i_low), table, t_sems, range(have, group.blocks)):
                copy.wait()
            have = max(have, group.blocks)
            lanes = group.blocks * LANES
            first_slot, first_sum = int(slot_at[g]), int(row_at[g])

            def back_of(spec, size, lanes=lanes, group=group):
                back = three_pass_in(spec, table[: group.blocks].reshape(3 * lanes, wide))
                return back.reshape(size, levels, wide)

            def masked(u, slot, size, group=group, first_slot=first_slot, first_sum=first_sum):
                rows_at = pl.ds(pl.multiple_of((first_slot + slot) * levels, 8), size)
                cut = cuts[rows_at, :]
                lane = lax.broadcasted_iota(jnp.int32, (size, LANES), 1)
                pieces = []
                for b in range(group.blocks):
                    keep = lax.shift_right_logical(lane + (b * LANES + 1), 1) <= cut
                    if group.packed and b == group.blocks - 1:
                        value = unpacked[u, pl.ds(pl.multiple_of(slot * levels, 8), size), :]
                    else:
                        source = pl.multiple_of(first_sum + b * group.height + slot * levels, 8)
                        value = sums[u, pl.ds(source, size), :]
                    pieces.append(jnp.where(keep, value, 0.0))
                return jnp.concatenate(pieces, axis=1)

            def unpack(u, _, group=group, first_sum=first_sum):
                def packed(row, count):
                    at_row = first_sum + group.full + row * levels
                    return sums[u, at_row : at_row + count * levels, :]

                def to(slot, count, value):
                    at_row = pl.multiple_of(slot * levels, 8)
                    unpacked[u, pl.ds(at_row, count * levels), :] = value

                group.unpack(scal[3], packed, to)
                return 0

            if group.packed:
                lax.fori_loop(0, FIELDS, unpack, 0)
            if group.farthest:
                spec = jnp.concatenate([masked(u, 0, levels) for u in range(FIELDS)], axis=0)
                back = back_of(spec, FIELDS)

                @pl.when(scal[4] >= 0)
                def _(back=back):
                    for u in range(FIELDS):
                        held[u ^ scal[0], scal[4]] = back[u]
            else:
                start = group.start(scal[3], rows)

                def part(n, _, group=group, start=start, masked=masked, back_of=back_of):
                    u, slot = n // group.parts, group.chunk_at(lax.rem(n, group.parts))
                    back = back_of(masked(u, slot, group.chunk * levels), group.chunk)
                    held[u ^ scal[0], pl.ds(start + slot, group.chunk)] = back
                    return 0

                lax.fori_loop(0, FIELDS * group.parts, part, 0)

    @pl.when(step == 0)
    def _():
        for at, groups in enumerate(plan.roles):
            pl.when(scal[2] == at)(functools.partial(inverse, at, groups))
        for side, line in enumerate((top, bottom)):

            @pl.when(scal[5 + side] == 0)
            def _(side=side, line=line):
                for field in range(FIELDS):
                    held[field, side * (rows + 1), :, :width] = line[field]

    base = step * step_rows
    tail = width % LANES

    @pl.when(step < last_step)
    def _():
        lane = lax.broadcasted_iota(jnp.int32, (levels, LANES), 1)

        def load(n, _):
            at = n
            row = base + n
            is_raw = (row >= scal[7]) & (row < scal[8])
            for field in range(FIELDS):
                for half in range(halves):
                    piece = raw[field * halves + half]
                    some = slice(half * 8, half * 8 + 8)
                    value = piece[0, at] if field < 2 else piece[at]
                    held[field, row + 1, some, :width] = jnp.where(
                        is_raw, value, held[field, row + 1, some, :width]
                    )
                beyond = jnp.where(
                    lane == tail,
                    pltpu.roll(east[field], (tail + LANES - row) & (LANES - 1), 1),
                    pltpu.roll(west[field], (2 * LANES - 1 - row) & (LANES - 1), 1),
                )
                held[field, row + 1, :, width:] = jnp.where(
                    is_raw, beyond[:, tail:], held[field, row + 1, :, width:]
                )
            return 0

        @pl.when((base < scal[8]) & (base + step_rows > scal[7]))
        def _():
            lax.fori_loop(0, step_rows, load, 0, unroll=3 if step_rows % 3 == 0 else 1)

    slot = step % 2
    count = wide // LANES
    lane = lax.broadcasted_iota(jnp.int32, (8, LANES), 1)
    is_first, is_last = lane == 0, lane == LANES - 1

    def stencil(row, _):
        at = base - step_rows + row
        along, across, push, turn, cos_north, cos_south = [coef[k * rows + at] for k in range(6)]
        across_north, across_south = across * cos_north, across * cos_south
        for part in range(levels // 8):
            some = pl.ds(part * 8, 8)

            def load(field, shift, k):
                return held[field, at + shift, some, k * LANES : (k + 1) * LANES]

            here = [
                functools.lru_cache(maxsize=None)(lambda k, field=field: load(field, 1, k))
                for field in range(FIELDS)
            ]
            up = [functools.lru_cache(maxsize=None)(lambda k, f=f: pltpu.roll(f(k), LANES - 1, 1)) for f in here]
            down = [functools.lru_cache(maxsize=None)(lambda k, f=f: pltpu.roll(f(k), 1, 1)) for f in here]

            def shifted(which, k):
                return (
                    jnp.where(is_last, up[which]((k + 1) % count), up[which](k)),
                    jnp.where(is_first, down[which]((k - 1) % count), down[which](k)),
                )

            for k in range(count):
                stop = min(width, (k + 1) * LANES)

                def put(field, piece, k=k, stop=stop):
                    ready[slot, field, row, some, k * LANES : stop] = piece[:, : stop - k * LANES]

                u, v, t, h = [here[field](k) for field in range(FIELDS)]
                advect, carry = along * u, 0.1 * v
                (u_e, u_w), (v_e, v_w), (t_e, t_w), (h_e, h_w) = [shifted(field, k) for field in range(FIELDS)]
                v_n, v_s, h_n, h_s = load(1, 0, k), load(1, 2, k), load(3, 0, k), load(3, 2, k)
                put(
                    3,
                    h
                    - along * (u_e * h_e - u_w * h_w)
                    - (across_south * (v_s * h_s) - across_north * (v_n * h_n)),
                )
                put(
                    1,
                    v
                    - advect * (v_e - v_w)
                    - carry * (v_s - v_n)
                    - 0.15 * (h_s - h_n)
                    - turn * u,
                )
                put(
                    0,
                    u
                    - advect * (u_e - u_w)
                    - carry * (load(0, 2, k) - load(0, 0, k))
                    - push * (h_e - h_w)
                    + turn * v,
                )
                put(2, t - advect * (t_e - t_w) - carry * (load(2, 2, k) - load(2, 0, k)))
        return 0

    outs = (new_wind.at[0], new_wind.at[1], new_theta, new_thick)

    def leave(at_step, size, act):
        for field, out in enumerate(outs):
            for k in range(0, step_rows, size):
                act(
                    pltpu.make_async_copy(
                        ready.at[at_step % 2, field, pl.ds(k, size)],
                        out.at[pl.ds((at_step - 1) * step_rows + k, size)],
                        out_sems.at[at_step % 2, field],
                    )
                )

    @pl.when(step > 2)
    def _():
        leave(step - 2, step_rows, lambda copy: copy.wait())

    @pl.when(step > 0)
    def _():
        lax.fori_loop(0, step_rows, stencil, 0, unroll=5 if step_rows % 5 == 0 else 1)
        leave(step, PIECE if step_rows % PIECE == 0 else step_rows, lambda copy: copy.start())

    @pl.when(step == last_step)
    def _():
        if last_step > 1:
            leave(step - 1, step_rows, lambda copy: copy.wait())
        leave(step, step_rows, lambda copy: copy.wait())


def substep(plan, step_rows, scal, coef, winds, theta, thick, west, east, top, bottom, cuts, tabs, spectra):
    rows, width, levels = plan.rows, plan.width, plan.levels
    once = pl.Buffered(1)
    steps = rows // step_rows

    def block(i, s):
        return jnp.clip(i, s[9], s[10])

    def whole(shape):
        return pl.BlockSpec(shape, lambda i, s: (0,) * len(shape), pipeline_mode=once)

    anywhere = pl.BlockSpec(memory_space=pl.ANY)
    halves = range(levels // 8)
    raw_specs = [
        pl.BlockSpec((1, step_rows, 8, width), lambda i, s, w=wind, h=half: (w, block(i, s), h, 0))
        for wind in range(2)
        for half in halves
    ] + [
        pl.BlockSpec((step_rows, 8, width), lambda i, s, h=half: (block(i, s), h, 0))
        for _ in range(2)
        for half in halves
    ]
    raw = [array for array in (winds, winds, theta, thick) for _ in halves]
    edge, halo = (FIELDS, levels, LANES), (FIELDS, levels, width)
    in_specs = [
        pl.BlockSpec(memory_space=pltpu.SMEM),
        whole(edge),
        whole(edge),
        whole(halo),
        whole(halo),
        whole((plan.slots * levels, LANES)),
        anywhere,
        anywhere,
    ] + raw_specs + [anywhere] * len(spectra)
    shapes = [(2, rows, levels, width)] + [(rows, levels, width)] * 2
    most = max(sum(group.total for group in groups) for groups in plan.roles)
    return pl.pallas_call(
        functools.partial(step_kernel, plan, step_rows),
        grid_spec=pltpu.PrefetchScalarGridSpec(
            num_scalar_prefetch=1,
            grid=(steps + 1,),
            in_specs=in_specs,
            out_specs=[anywhere] * 3,
            scratch_shapes=[
                pltpu.VMEM((FIELDS, rows + 2, levels, plan.wide), jnp.float32),
                pltpu.VMEM((FIELDS, most, LANES), jnp.float32),
                pltpu.VMEM((FIELDS, max(group.height for groups in plan.roles for group in groups), LANES), jnp.float32),
                pltpu.VMEM((plan.table // LANES, 3, LANES, plan.wide), jnp.bfloat16),
                pltpu.VMEM((2, FIELDS, step_rows, levels, width), jnp.float32),
                pltpu.SemaphoreType.DMA((max(len(groups) for groups in plan.roles), FIELDS)),
                pltpu.SemaphoreType.DMA((plan.table // LANES, 3)),
                pltpu.SemaphoreType.DMA((2, FIELDS)),
            ],
        ),
        out_shape=[jax.ShapeDtypeStruct(shape, jnp.float32) for shape in shapes],
        compiler_params=pltpu.CompilerParams(vmem_limit_bytes=VMEM),
        cost_estimate=pl.CostEstimate(
            flops=6 * most * FIELDS * LANES * plan.wide, bytes_accessed=40_000_000, transcendentals=0
        ),
        name="inverse_and_substep",
    )(scal, coef, west, east, top, bottom, cuts, *tabs, *raw, *spectra)


def lon_swap(plan, value, moves):
    pairs = [
        (block * plan.lon + place, block * plan.lon + (place ^ (1 << bit)))
        for blocks, bit in moves
        for block in blocks
        for place in range(plan.lon)
    ]
    return lax.ppermute(value, ("lat", "lon"), pairs)


def lat_move(plan, value, sources, targets):
    pairs = [
        (source * plan.lon + place, target * plan.lon + place)
        for source, target in zip(sources, targets)
        for place in range(plan.lon)
    ]
    return lax.ppermute(value, ("lat", "lon"), pairs)


def gather_sums(plan, blocks, slots, order):
    slots = dict(slots)
    for bit in order:
        sent = [s for s in slots if s >> bit & 1]
        for s in sorted(sent, key=lambda s: -bin(s).count("1")):
            moved = lon_swap(plan, slots.pop(s), [(blocks, bit)])
            slots[s ^ (1 << bit)] = slots[s ^ (1 << bit)] + moved
    for bit in reversed(order):
        for s in sorted(slots):
            slots[s | (1 << bit)] = lon_swap(plan, slots[s], [(blocks, bit)])
    return slots


def field_sets(plan):
    sent, kept = [], []
    for at in range(len(plan.roles)):
        bit = at % 2
        sent.append([u for u in range(FIELDS) if u >> bit & 1])
        kept.append([u for u in range(FIELDS) if not u >> bit & 1])
    return sent, kept


def store_sums(plan, members, sent, kept, before=None):
    near = [(blocks, bit) for blocks, bit in members]
    far = [(blocks, 1 - bit) for blocks, bit in members]
    moved = lon_swap(plan, sent, near)
    own = (kept[0] + moved[0]) + lon_swap(plan, kept[1] + moved[1], far)
    across = lon_swap(plan, own, far)
    beside = lon_swap(plan, own, near)
    onward = across if before is None else lax.optimization_barrier((across, before))[0]
    return own, beside, across, lon_swap(plan, onward, near)


def split_sums(plan, place, at, sent, kept):
    first, second = field_sets(plan)
    parts, own = plan.parts, place % plan.parts
    bits = plan.lon.bit_length() - 1
    slots = {}
    for us, array in ((first[at], sent), (second[at], kept)):
        for i, u in enumerate(us):
            pieces = array[i].reshape(parts, -1, LANES)
            for k in range(parts):
                slots[u * parts + k] = pieces[k ^ own]
    order = list(range(bits)) if at % 2 == 0 else list(reversed(range(bits)))
    slots = gather_sums(plan, plan.blocks(at), slots, order)
    result = []
    for u in range(FIELDS):
        pieces = jnp.stack([slots[u * parts + k] for k in range(parts)])
        result.append(pieces[jnp.arange(parts) ^ own].reshape(-1, LANES))
    return result


def all_sums(plan, place, arrays):
    stores = plan.stores()
    if plan.parts > 1:
        return sum(
            [
                split_sums(plan, place, store[0][0], arrays[number, 0], arrays[number, 1])
                for number, store in enumerate(stores)
            ],
            [],
        )
    back, results = None, {}
    for number in reversed(range(len(stores))):
        store, first, second = stores[number], arrays[number, 0], arrays[number, 1]
        if store[0][1] == 0:
            members = [(plan.blocks(at), at % 2) for at, _ in store]
            results[number] = store_sums(plan, members, first, second, back)
        else:
            at = store[0][0]
            home, helpers = plan.blocks(at), plan.blocks(at + len(plan.roles))
            first, second = [lat_move(plan, array, home, helpers) for array in (first, second)]
            sums = store_sums(plan, [(helpers, at % 2)], first, second)
            results[number] = [lat_move(plan, array, helpers, home) for array in sums]
            back = (results[number][0], results[number][2])
    return [array for number in range(len(stores)) for array in results[number]]


def body(winds, theta, thick, polar_rows, cutoffs):
    lat, lon = lax.axis_size("lat"), lax.axis_size("lon")
    levels, rows, width = theta.shape
    sizes = (lat, lon, levels, rows, width, polar_rows.shape[0])
    plan = Plan(*sizes)
    t_tabs, i_tabs = [tuple(jnp.asarray(part) for part in pair) for pair in tables(sizes)]
    block, place = lax.axis_index("lat"), lax.axis_index("lon")
    winds = winds.transpose(0, 2, 1, 3)
    theta = theta.transpose(1, 0, 2)
    thick = thick.transpose(1, 0, 2)
    hemi = (block >= lat // 2).astype(jnp.int32)
    role = jnp.where(hemi == 1, lat - 1 - block, block)

    def line(row):
        return jnp.stack([winds[0, row], winds[1, row], theta[row], thick[row]])

    south_pairs = [(b * lon + p, (b + 1) * lon + p) for b in range(lat - 1) for p in range(lon)]
    north_pairs = [(to, at) for at, to in south_pairs]
    top = lax.ppermute(line(rows - 1), ("lat", "lon"), south_pairs)
    bottom = lax.ppermute(line(0), ("lat", "lon"), north_pairs)

    step_rows = max(k for k in range(1, 16) if rows % k == 0)
    listed = polar_rows.shape[0]
    north_run = jnp.sum((polar_rows < plan.total_rows // 2).astype(jnp.int32))
    south_first = plan.total_rows - listed + north_run
    far_row = jnp.where(hemi == 1, south_first, north_run - 1)
    far_at = far_row - block * rows + 1
    far_at = jnp.where((far_at >= 0) & (far_at <= rows + 1), far_at, -1)
    raw_from = jnp.clip(north_run - block * rows, 0, rows)
    raw_to = jnp.clip(south_first - block * rows, 0, rows)
    block_from = jnp.minimum(raw_from, rows - 1) // step_rows
    block_to = jnp.maximum(block_from, jnp.maximum(raw_to - 1, 0) // step_rows)
    above, below = block * rows - 1, (block + 1) * rows

    def is_listed(row):
        return (row >= 0) & (row < plan.total_rows) & ((row < north_run) | (row >= south_first))

    facts = [
        place // plan.parts, place, role, hemi, far_at, is_listed(above), is_listed(below),
        raw_from, raw_to, block_from, block_to,
    ]
    scal = jnp.stack([jnp.asarray(fact).astype(jnp.int32) for fact in facts])

    arrays = forward(plan, 0, scal, winds, theta, thick, top, bottom, t_tabs)

    first_edge, last_edge = edges(plan, arrays[plan.arrays()[0][0]], winds, theta, thick)
    some = [b for b in range(lat) if (min(b, lat - 1 - b) + 1) * rows > plan.low]
    east_pairs = [(b * lon + i, b * lon + (i + 1) % lon) for b in some for i in range(lon)]
    west = lax.ppermute(last_edge, ("lat", "lon"), east_pairs)
    east = lax.ppermute(first_edge, ("lat", "lon"), [(to, at) for at, to in east_pairs])

    scal, _ = lax.optimization_barrier((scal, first_edge))
    later = forward(plan, 1, scal, winds, theta, thick, top, bottom, t_tabs)
    added = {key: array for key, array in later.items() if plan.stores()[key[0]][0][1] == 0}
    added, west, east = lax.optimization_barrier((added, west, east))
    arrays = {**arrays, **later, **added}
    sums = all_sums(plan, place, arrays)

    slot_rows = jnp.asarray(plan.slot_rows())[jnp.minimum(role, len(plan.roles) - 1), hemi]
    slot_rows = jnp.where(slot_rows == -2, far_at, slot_rows)
    hits = (polar_rows[None, :] == (slot_rows - 1 + block * rows)[:, None]) & (slot_rows >= 0)[:, None]
    cut = jnp.sum(jnp.where(hits, cutoffs[None, :] + 1, 0), axis=1) - 1
    cuts = jnp.broadcast_to(cut.astype(jnp.int32)[:, None, None], (plan.slots, levels, LANES))
    cuts = cuts.reshape(plan.slots * levels, LANES)

    ring = block * rows - 1 + jnp.arange(rows + 2, dtype=jnp.int32)
    centre = (ring.astype(jnp.float32) + 0.5) * (jnp.pi / plan.total_rows)
    cos, sin = jnp.sin(centre), -jnp.cos(centre)
    mid = cos[1:-1]
    coef = jnp.concatenate([0.025 / mid, 0.1 / mid, 0.05 / mid, 0.3 * sin[1:-1], cos[:-2], cos[2:]])

    out = substep(
        plan, step_rows, scal, coef, winds, theta, thick, west, east, top, bottom, cuts, i_tabs, sums
    )
    return (out[0].transpose(0, 2, 1, 3), out[1].transpose(1, 0, 2), out[2].transpose(1, 0, 2))


def solution(mesh):
    in_specs = (P(None, None, "lat", "lon"), P(None, "lat", "lon"), P(None, "lat", "lon"), P(), P())
    out_specs = (P(None, None, "lat", "lon"), P(None, "lat", "lon"), P(None, "lat", "lon"))
    return jax.shard_map(body, mesh=mesh, in_specs=in_specs, out_specs=out_specs, check_vma=False)
```
